32 devices in a mesh: dp: 8 (over z, core), tensor: 4 (over y, x).
Axes of the slice: x: 2, y: 2, z: 4, core: 2. Of those that a mesh axis runs over, the one named last changes fastest.
Arguments:
- tokens_in: bfloat16 [4096, 2048], P(('dp', 'tensor')), may hold values from -24 to 24
- seq_lens: int32 [8, 4], P('dp'), may hold values from 0 to 512, as said below
- w_query: bfloat16 [2048, 2048], P('dp', 'tensor'), may hold values from -0.1875 to 0.1875
- w_key: bfloat16 [2048, 2048], P('dp', 'tensor'), may hold values from -0.1875 to 0.1875
- w_value: bfloat16 [2048, 2048], P('dp', 'tensor'), may hold values from -0.125 to 0.125
- w_out: bfloat16 [2048, 2048], P('tensor', 'dp'), may hold values from -1 to 1
- norm1_gain: bfloat16 [2048], P('dp'), may hold values from 0.099609375 to 1.8984375
- w_gate: bfloat16 [2048, 8192], P('dp', 'tensor'), may hold values from -0.125 to 0.125
- w_up: bfloat16 [2048, 8192], P('dp', 'tensor'), may hold values from -0.125 to 0.125
- w_down: bfloat16 [8192, 2048], P('tensor', 'dp'), may hold values from -0.0625 to 0.0625
- norm2_gain: bfloat16 [2048], P('dp'), may hold values from 0.099609375 to 1.8984375
- out_cotangent: bfloat16 [4096, 2048], P(('dp', 'tensor')), may hold values from -6 to 6
Outputs:
- block_out: bfloat16 [4096, 2048], P(('dp', 'tensor'))
- grad_tokens: float32 [4096, 2048], P(('dp', 'tensor'))
- grad_w_query: float32 [2048, 2048], P('dp', 'tensor')
- grad_w_key: float32 [2048, 2048], P('dp', 'tensor')
- grad_w_value: float32 [2048, 2048], P('dp', 'tensor')
- grad_w_out: float32 [2048, 2048], P('tensor', 'dp')
- grad_norm1_gain: float32 [2048], P('dp')
- grad_w_gate: float32 [2048, 8192], P('dp', 'tensor')
- grad_w_up: float32 [2048, 8192], P('dp', 'tensor')
- grad_w_down: float32 [8192, 2048], P('tensor', 'dp')
- grad_norm2_gain: float32 [2048], P('dp')
The draws below stay inside these ranges and needn't reach their ends.
Inputs may be any that keep to these rules, and one draw needn't show every extreme that they name: `seq_lens`: lengths of the 4 sequences of each group, 0 for an empty slot; each sequence begins at the first multiple of 128 slots after the one before it, and a group's sequences fit its 512 slots. In every draw one group's sequences fill all its padding blocks and some sequence has exactly 512 tokens.
All inputs are finite; a program needn't handle non-finite values.
Results may differ from the reference program's by a relative error of at most 0.025.
Values may be sent and summed in bfloat16 or wider, within the bound.
A program may use at most 192 MiB of HBM per device.

```python
import math
import jax
import jax.numpy as jnp
from jax import lax

D = 2048
HEADS = 32
HEAD_DIM = 64
FF = 8192
SEQS = 4
BLOCK = 128
ATT_ROWS = 512
GROUP_TOK = 512
MAXLEN = 512
TOKENS = 4096
N_DP = 8


def draw_tokens_in(key, part):
    key = jax.random.fold_in(key, 5)
    first, second, third = jax.random.split(key, 3)
    base = jax.random.truncated_normal(first, -4.0, 4.0, (TOKENS, D), jnp.float32)
    row_scale = jnp.exp(jax.random.uniform(second, (TOKENS, 1), jnp.float32, math.log(0.3), math.log(3.0)))
    col_scale = jnp.exp(jax.random.uniform(third, (1, D), jnp.float32, math.log(0.5), math.log(2.0)))
    return (base * row_scale * col_scale).astype(jnp.bfloat16)


def draw_seq_lens(key, part):
    key = jax.random.fold_in(key, 7)
    total_blocks = GROUP_TOK // BLOCK
    long_blocks = MAXLEN // BLOCK
    groups = jnp.arange(N_DP, dtype=jnp.int32)
    used = jax.random.randint(jax.random.fold_in(key, 100), (N_DP,), max(total_blocks // 4, 1), total_blocks + 1)
    full_group = jax.random.randint(jax.random.fold_in(key, 101), (), 0, N_DP)
    long_group = jax.random.randint(jax.random.fold_in(key, 102), (), 0, N_DP)
    used = jnp.where(groups == full_group, total_blocks, used)
    used = jnp.where(groups == long_group, jnp.maximum(used, long_blocks), used)
    remaining = used
    lengths = []
    for slot in range(SEQS):
        later = (SEQS - 1 - slot) * long_blocks
        lowest = jnp.maximum(jnp.minimum(remaining, 1), remaining - later)
        highest = jnp.minimum(remaining, long_blocks)
        picked = jax.random.randint(jax.random.fold_in(key, 2 * slot), (N_DP,), 0, 1 << 20)
        blocks = lowest + picked % (highest - lowest + 1)
        partial_value = 1 + jax.random.randint(jax.random.fold_in(key, 2 * slot + 1), (N_DP,), 0, BLOCK)
        length = jnp.where(blocks > 0, (blocks - 1) * BLOCK + partial_value, 0)
        if slot == 0:
            blocks = jnp.where(groups == long_group, long_blocks, blocks)
            length = jnp.where(groups == long_group, MAXLEN, length)
        lengths.append(length)
        remaining = remaining - blocks
    return jnp.stack(lengths, axis=1).astype(jnp.int32)


def spiked(entries, own_key, source, target, parts, factor):
    def block_of(dim):
        return (jnp.arange(entries.shape[dim]) // (entries.shape[dim] // parts)).reshape((-1,) + (1,) * (entries.ndim - 1 - dim))

    near = jax.random.permutation(own_key, parts)[block_of(target)]
    far = (block_of(target) + parts // 2) % parts
    return jnp.where((block_of(source) == near) | (block_of(source) == far), factor * entries, entries)


def steps_of(key, shape, cuts, smallest, largest):
    level, own = 1.0, jax.random.fold_in(key, 6)
    for dim, shards_of in cuts:
        heights = jnp.exp(jax.random.uniform(jax.random.fold_in(own, dim), (shards_of,), jnp.float32, smallest / len(cuts), largest / len(cuts)))
        level = level * jnp.repeat(heights, shape[dim] // shards_of).reshape([-1 if axis == dim else 1 for axis in range(len(shape))])
    return level


def noise(stream_key, extent, spread, limit, cuts=(), kind=jnp.bfloat16):
    loudness = steps_of(stream_key, extent, cuts, -0.22, 0.18) if cuts else 1.0
    array = jax.random.normal(stream_key, extent, jnp.float32) * spread * loudness
    return jnp.minimum(jnp.maximum(array, -limit), limit).astype(kind)


def noise_with(rng, shape, width, limit, cuts, heavy, kind=jnp.bfloat16):
    values = width * jax.random.normal(rng, shape, jnp.float32)
    if cuts:
        values = values * steps_of(rng, shape, cuts, -0.22, 0.18)
    return jnp.clip(spiked(values, jax.random.fold_in(rng, 3), *heavy), -limit, limit).astype(kind)


def setup_inputs(seed: int = 0) -> dict:
    key_list = jax.random.split(jax.random.key(seed), 13)
    return {
        "tokens_in": draw_tokens_in(jax.random.fold_in(key_list[12], 71), 0),
        "seq_lens": draw_seq_lens(jax.random.fold_in(key_list[12], 71), 0),
        "w_query": noise(key_list[2], (D, D), (D // 2) ** -0.5, 0.1875, ((0, 8), (1, 4))),
        "w_key": noise(key_list[3], (D, D), (D // 2) ** -0.5, 0.1875, ((0, 8), (1, 4))),
        "w_value": noise(key_list[4], (D, D), D ** -0.5, 0.125, ((0, 8), (1, 4))),
        "w_out": noise(key_list[5], (D, D), (D // 64) ** -0.5, 1.0, ((0, 4), (1, 8))),
        "norm1_gain": jnp.clip(1.0 + 0.18 * jax.random.normal(key_list[6], (D,), jnp.float32), 0.099609375, 1.8984375).astype(jnp.bfloat16),
        "w_gate": noise(key_list[7], (D, FF), D ** -0.5, 0.125, ((0, 8), (1, 4))),
        "w_up": noise(key_list[8], (D, FF), D ** -0.5, 0.125, ((0, 8), (1, 4))),
        "w_down": noise(key_list[9], (FF, D), FF ** -0.5, 0.0625, ((0, 4), (1, 8))),
        "norm2_gain": jnp.clip(1.0 + 0.18 * jax.random.normal(key_list[10], (D,), jnp.float32), 0.099609375, 1.8984375).astype(jnp.bfloat16),
        "out_cotangent": noise_with(key_list[11], (TOKENS, D), 1.0, 6.0, ((0, 32),), (0, 1, 32, 2.75)),
    }


EPSILON = 1e-05
ROPE_BASE = 130000.0
MASKED = -1e+30

@jax.custom_vjp
def low(v):
    return lax.optimization_barrier(v.astype(jnp.bfloat16)).astype(jnp.float32)

@jax.custom_vjp
def low_back(v):
    return v

def low_keep(v):
    return (low(v), None)

def low_pass(kept, grad):
    return (grad,)

def back_keep(v):
    return (v, None)

def back_low(kept, grad):
    return (low(grad),)
low.defvjp(low_keep, low_pass)
low_back.defvjp(back_keep, back_low)

def group_layout(lengths, total):
    blocks = (lengths + BLOCK - 1) // BLOCK
    starts = ((jnp.cumsum(blocks) - blocks) * BLOCK).astype(jnp.int32)
    rows = jnp.arange(total, dtype=jnp.int32)
    inside = (rows[:, None] >= starts[None, :]) & (rows[:, None] < (starts + lengths)[None, :])
    valid = jnp.any(inside, axis=1)
    slots = jnp.arange(lengths.shape[0], dtype=jnp.int32)
    segment = lax.optimization_barrier(jnp.sum(jnp.where(inside, slots[None, :], 0), axis=1)).astype(jnp.int32)
    segment = segment + jnp.where(valid, 0, lengths.shape[0] + rows).astype(jnp.int32)
    position = rows - lax.optimization_barrier(jnp.sum(jnp.where(inside, starts[None, :], 0), axis=1)).astype(jnp.int32)
    return (valid, segment.astype(jnp.int32), position.astype(jnp.int32))

def rope_tables(position):
    half = HEAD_DIM // 2
    freqs = jnp.exp(jnp.arange(half, dtype=jnp.float32) * (-2.0 * math.log(ROPE_BASE) / HEAD_DIM))
    angles = position.astype(jnp.float32)[:, None] * freqs[None, :]
    return (jnp.cos(angles)[:, None, :], jnp.sin(angles)[:, None, :])

def rotate(values, cosine, sine):
    half = values.shape[-1] // 2
    first, second = (values[..., :half], values[..., half:])
    return jnp.concatenate([first * cosine - second * sine, second * cosine + first * sine], axis=-1)

def rms_normalize(values):
    return values * lax.rsqrt(lax.optimization_barrier(jnp.mean(values * values, axis=-1, keepdims=True)) + EPSILON)

def matmul(left, right):
    return jnp.dot(left, right, precision=lax.Precision.HIGHEST)

def layer(tokens, w_query, w_key, w_value, w_out, gain_one, w_gate, w_up, w_down, gain_two, valid, segment, position):
    total = tokens.shape[0]
    cosine, sine = rope_tables(position)
    hidden_one = low(rms_normalize(tokens) * gain_one)

    def heads(values):
        return values.reshape(total, HEADS, HEAD_DIM)
    query = low(rotate(heads(low_back(matmul(hidden_one, w_query))), cosine, sine))
    keys = low(rotate(heads(low_back(matmul(hidden_one, w_key))), cosine, sine))
    values = low(heads(low_back(matmul(hidden_one, w_value))))
    block = min(ATT_ROWS, total)
    count = total // block
    rows = jnp.arange(total, dtype=jnp.int32)
    scale = HEAD_DIM ** (-0.5)

    def attend(item):
        query_block, segment_block, row_block = item
        raw = low_back(jnp.einsum('qhd,khd->hqk', query_block, keys, precision=lax.Precision.HIGHEST))
        allowed = (segment_block[:, None] == segment[None, :]) & (row_block[:, None] >= rows[None, :])
        scores = jnp.where(allowed[None], raw * scale, MASKED)
        weights = low(jax.nn.softmax(scores, axis=-1))
        return jnp.einsum('hqk,khd->qhd', weights, values, precision=lax.Precision.HIGHEST)
    mixed = lax.map(jax.checkpoint(attend), (query.reshape(count, block, HEADS, HEAD_DIM), segment.reshape(count, block), rows.reshape(count, block)))
    attended = low(low_back(mixed.reshape(total, D)))
    branch_one = low_back(matmul(attended, w_out))
    middle = tokens + valid[:, None] * branch_one
    hidden_two = low(rms_normalize(middle) * gain_two)
    gate = low_back(matmul(hidden_two, w_gate))
    up = low_back(matmul(hidden_two, w_up))
    inner = low(jax.nn.silu(gate) * up)
    branch_two = low_back(matmul(inner, w_down))
    return middle + valid[:, None] * branch_two

def reference(tokens_in, seq_lens, w_query, w_key, w_value, w_out, norm1_gain, w_gate, w_up, w_down, norm2_gain, out_cotangent):
    weights = tuple((weight.astype(jnp.float32) for weight in (w_query, w_key, w_value, w_out, norm1_gain, w_gate, w_up, w_down, norm2_gain)))
    inputs = tokens_in.astype(jnp.float32).reshape(N_DP, GROUP_TOK, D)
    cotangents = out_cotangent.astype(jnp.float32).reshape(N_DP, GROUP_TOK, D)

    def step(totals, item):
        group_in, group_cot, lengths = item
        valid, segment, position = group_layout(lengths, GROUP_TOK)

        def forward(group_tokens, *params):
            return layer(group_tokens, *params, valid.astype(jnp.float32), segment, position)
        result, pullback = jax.vjp(forward, group_in, *weights)
        grads = pullback(group_cot)
        totals = tuple((earlier + later for earlier, later in zip(totals, grads[1:])))
        return (totals, (result, grads[0]))
    zeros = tuple((jnp.zeros_like(weight) for weight in weights))
    totals, (results, input_grads) = lax.scan(step, zeros, (inputs, cotangents, seq_lens))
    return (results.reshape(TOKENS, D).astype(jnp.bfloat16), input_grads.reshape(TOKENS, D), totals[0], totals[1], totals[2], totals[3], totals[4], totals[5], totals[6], totals[7], totals[8])
```

```python
import functools
import math

import jax
import jax.numpy as jnp
from jax import lax
from jax.experimental import pallas as pl
from jax.experimental.pallas import tpu as pltpu
from jax.sharding import PartitionSpec as P

HEAD_DIM = 64
HALF = HEAD_DIM // 2
BLOCK = 128
LANES = 128
EPSILON = 1e-05
ROPE_BASE = 130000.0
MASKED = -1e30
SCALE = HEAD_DIM ** (-0.5)

LOW = jnp.bfloat16
WIDE = jnp.float32
VMEM_BYTES = 64 * 1024 * 1024
PARTS = 2
STRIP = 32


def dot_nn(left, right):
    return lax.dot_general(left, right, (((1,), (0,)), ((), ())), preferred_element_type=WIDE)


def dot_nt(left, right):
    return lax.dot_general(left, right, (((1,), (1,)), ((), ())), preferred_element_type=WIDE)


def identity(size):
    across = lax.broadcasted_iota(jnp.int32, (size, size), 0)
    down = lax.broadcasted_iota(jnp.int32, (size, size), 1)
    return jnp.where(across == down, 1.0, 0.0).astype(LOW)


def turn(values, eye):
    size = eye.shape[0]
    width = values.shape[1]
    if width <= size:
        return dot_nt(eye[:width, :width], values).astype(LOW)
    blocks = [dot_nt(eye, values[:, n : n + size]).astype(LOW) for n in range(0, width, size)]
    return jnp.concatenate(blocks, axis=0)


class Place:
    def __init__(self, chain, peers):
        self.chain, self.peers = chain, peers
        self.dp = lax.axis_index("dp")
        self.t = lax.axis_index("tensor")
        self.c = lax.rem(self.dp, 2)
        self.z = lax.div(self.dp, 2)

    def sibling(self):
        return {"dp": self.dp + 1 - 2 * self.c, "tensor": self.t}

    def along(self, step):
        return {"dp": self.dp + 2 * step, "tensor": self.t}

    def part(self, dp):
        return {"dp": dp, "tensor": self.t}

    def peer(self, t):
        return {"dp": self.dp, "tensor": t}

    def other_peers(self):
        return [lax.rem(self.t + n, self.peers) for n in range(1, self.peers)]

    def other_parts(self):
        parts = 2 * self.chain
        return [lax.rem(self.dp + n, parts) for n in range(1, parts)]


def remote(src, dst, send, recv, device):
    return pltpu.make_async_remote_copy(
        src_ref=src,
        dst_ref=dst,
        send_sem=send,
        recv_sem=recv,
        device_id=device,
        device_id_type=pl.DeviceIdType.MESH,
    )


def fetch(src, dst, sem):
    copy = pltpu.make_async_copy(src, dst, sem)
    copy.start()
    copy.wait()


def entry_barrier(at):
    barrier = pltpu.get_barrier_semaphore()
    devices = [at.peer(t) for t in at.other_peers()] + [at.part(dp) for dp in at.other_parts()]
    for device in devices:
        pl.semaphore_signal(barrier, inc=1, device_id=device, device_id_type=pl.DeviceIdType.MESH)
    pl.semaphore_wait(barrier, len(devices))


class PlaneGather:
    def __init__(self, at, full, rows, sems):
        self.at, self.full, self.rows = at, full, rows
        self.group = rows * at.peers
        self.send, self.recv, self.pass_send, self.pass_recv = sems

    def block(self, c, t):
        start = pl.multiple_of(c * self.group + t * self.rows, self.rows)
        return self.full.at[pl.ds(start, self.rows)]

    def to_peer(self, t):
        at = self.at
        own = self.block(at.c, at.t)
        return remote(own, own, self.send.at[t], self.recv.at[at.t], at.peer(t))

    def from_peer(self, t):
        block = self.block(self.at.c, t)
        return remote(block, block, self.send.at[t], self.recv.at[t], self.at.peer(t))

    def to_sibling(self, t):
        block = self.block(self.at.c, t)
        return remote(
            block, block, self.pass_send.at[t], self.pass_recv.at[t], self.at.sibling()
        )

    def from_sibling(self, t):
        block = self.block(1 - self.at.c, t)
        return remote(
            block, block, self.pass_send.at[t], self.pass_recv.at[t], self.at.sibling()
        )

    def start(self):
        for t in self.at.other_peers():
            self.to_peer(t).start()
        self.to_sibling(self.at.t).start()

    def forward(self):
        for t in self.at.other_peers():
            self.from_peer(t).wait_recv()
            self.to_sibling(t).start()

    def finish(self):
        for t in range(self.at.peers):
            self.from_sibling(t).wait_recv()
        for t in self.at.other_peers():
            self.to_peer(t).wait_send()
        for t in range(self.at.peers):
            self.to_sibling(t).wait_send()


class PlaneReduce:
    def __init__(self, at, rows, tile, buffer, first, second, stage, sems, local):
        self.at, self.rows, self.tile, self.buffer = at, rows, tile, buffer
        self.group = rows * at.peers
        self.first, self.second, self.stage, self.local = first, second, stage, local
        self.send1, self.recv1, self.send2, self.recv2 = sems

    def source(self, c, i):
        return pl.ds(pl.multiple_of(c * self.group + i * self.tile, self.tile), self.tile)

    def to_sibling(self, i):
        here = pl.ds(i * self.tile, self.tile)
        return remote(
            self.buffer.at[here],
            self.first.at[here],
            self.send1.at[i],
            self.recv1.at[i],
            self.at.sibling(),
        )

    def to_peer(self, t, source):
        return remote(
            self.buffer.at[pl.ds(pl.multiple_of(t * self.rows, self.rows), self.rows)],
            self.second.at[source],
            self.send2.at[t],
            self.recv2.at[source],
            self.at.peer(t),
        )

    def half(self, compute, begun=False):
        for i in range(self.group // self.tile):
            out = self.buffer.at[pl.ds(i * self.tile, self.tile)]
            compute(self.source(1 - self.at.c, i), out, [out] if begun else [])
            self.to_sibling(i).start()

    def rest(self, compute, begun=None):
        at = self.at
        for i in range(self.group // self.tile):
            here = pl.ds(i * self.tile, self.tile)
            self.to_sibling(i).wait_recv()
            fetch(self.first.at[here], self.stage, self.local)
            self.to_sibling(i).wait_send()
            extras = [self.stage] if begun is None else [self.stage, begun.at[here]]
            compute(self.source(at.c, i), self.buffer.at[here], extras)
            for j in range(i * self.tile // self.rows, (i + 1) * self.tile // self.rows):

                @pl.when(at.t != j)
                def _():
                    self.to_peer(j, at.t).start()

    def finish(self, out):
        at = self.at
        own = pl.ds(pl.multiple_of(at.t * self.rows, self.rows), self.rows)
        out[...] = self.buffer[own, :].astype(WIDE)
        for t in at.other_peers():
            self.to_peer(at.t, t).wait_recv()
            fetch(self.second.at[t], self.stage.at[pl.ds(0, self.rows)], self.local)
            out[...] += self.stage[0 : self.rows, :].astype(WIDE)

    def sent(self):
        for t in self.at.other_peers():
            self.to_peer(t, self.at.t).wait_send()


class ChainGather:
    def __init__(self, at, slabs, send, recv):
        self.at, self.slabs, self.sems = at, slabs, (send, recv)
        self.height = slabs.shape[1] // PARTS

    def copy(self, way, slab, step, part):
        send, recv = self.sems
        ref = self.slabs.at[slab, pl.ds(part * self.height, self.height)]
        return remote(
            ref,
            ref,
            send.at[way, step, part],
            recv.at[way, step, part],
            self.at.along(1 - 2 * way),
        )

    def each_send(self, step, part, act):
        z, last = self.at.z, self.at.chain - 1

        @pl.when((z < last) & (z >= max(step, 1)))
        def _():
            act(self.copy(0, z - step, step, part))

        @pl.when((z > 0) & (z + step <= last) & (z + 1 - min(step, 1) <= last))
        def _():
            act(self.copy(1, z + step, step, part))

    def each_end(self, part, act):
        z, last = self.at.z, self.at.chain - 1

        @pl.when(z == 0)
        def _():
            act(self.copy(0, 0, 0, part))

        @pl.when(z == last)
        def _():
            act(self.copy(1, last, 0, part))

    def start(self, step, part):
        self.each_send(step, part, lambda copy: copy.start())

    def start_end(self, part):
        self.each_end(part, lambda copy: copy.start())

    def sent(self):
        for part in range(PARTS):
            self.each_end(part, lambda copy: copy.wait_send())
            for step in range(self.at.chain - 1):
                self.each_send(step, part, lambda copy: copy.wait_send())

    def arrived(self, step, part):
        z, last = self.at.z, self.at.chain - 1

        @pl.when(z - 1 - step >= 0)
        def _():
            self.copy(0, z - 1 - step, step, part).wait_recv()

        @pl.when(z + 1 + step <= last)
        def _():
            self.copy(1, z + 1 + step, step, part).wait_recv()


class Stream:
    def __init__(self, chains, swapped):
        self.chains, self.swapped = chains, swapped
        self.steps = chains[0].at.chain - 1
        self.messages = [
            (n, step, part)
            for n in range(len(chains))
            for step in range(self.steps)
            for part in range(PARTS)
        ]
        self.ends = [(n, part) for n in range(len(chains)) for part in range(PARTS)]
        self.next = 0
        self.ready = 0

    def need(self, n):
        while self.ready <= n:
            self.swapped(self.ready)
            self.ready += 1

    def go(self, count=1):
        for _ in range(count):
            done = self.next - PARTS
            if 0 <= done < len(self.messages):
                n, step, part = self.messages[done]
                self.chains[n].arrived(step, part)
            if self.next < len(self.messages):
                n, step, part = self.messages[self.next]
                self.need(n)
                self.chains[n].start(step, part)
            if self.next < len(self.ends):
                n, part = self.ends[self.next]
                self.need(n)
                self.chains[n].start_end(part)
            self.next += 1

    def complete(self, n):
        while self.next < (n + 1) * self.steps * PARTS + PARTS:
            self.go()


class ChainReduce:
    def __init__(self, at, slabs, height, slots, send, recv, stage, local):
        self.at, self.slabs, self.slots, self.sems = at, slabs, slots, (send, recv)
        self.stage, self.local = stage, local
        self.height = height // PARTS

    def copy(self, way, slab, step, part):
        send, recv = self.sems
        rows = pl.ds(part * self.height, self.height)
        return remote(
            self.slabs.at[slab, rows],
            self.slots.at[way, step, rows],
            send.at[way, step, part],
            recv.at[way, step, part],
            self.at.along(1 - 2 * way),
        )

    def slab_of(self, way, step):
        last = self.at.chain - 1
        return self.at.z + last - step if way == 0 else self.at.z - last + step

    def sends(self, way, step):
        last = self.at.chain - 1
        return self.at.z <= step if way == 0 else self.at.z >= last - step

    def receives(self, way, step):
        last = self.at.chain - 1
        if way == 0:
            return (self.at.z >= 1) & (self.at.z <= step + 1)
        return (self.at.z < last) & (self.at.z >= last - step - 1)

    def ends(self, step, part):
        @pl.when(self.at.z == 0)
        def _():
            self.copy(0, self.slab_of(0, step), step, part).start()

        @pl.when(self.at.z == self.at.chain - 1)
        def _():
            self.copy(1, self.slab_of(1, step), step, part).start()

    def landed(self, way, step, part):
        return pltpu.make_async_copy(
            self.slots.at[way, step, pl.ds(part * self.height, self.height)],
            self.stage.at[way, pl.ds(0, self.height)],
            self.local.at[way],
        )

    def add(self, way, slab, step, part):
        self.landed(way, step, part).wait()
        tile = min(64, self.height)

        def body(i, carry):
            here = pl.ds(pl.multiple_of(i * tile, tile), tile)
            rows = pl.ds(pl.multiple_of(part * self.height + i * tile, tile), tile)
            total = self.slabs[slab, rows, :].astype(WIDE) + self.stage[way, here, :].astype(WIDE)
            self.slabs[slab, rows, :] = total.astype(LOW)
            return carry

        lax.fori_loop(0, self.height // tile, body, 0)

    def passes(self, way, step):
        inside = self.at.z > 0 if way == 0 else self.at.z < self.at.chain - 1
        return self.sends(way, step) & inside

    def step(self, step, part):
        for way in (0, 1):

            @pl.when(self.passes(way, step))
            def _():
                self.copy(way, 0, step - 1, part).wait_recv()
                self.landed(way, step - 1, part).start()

        for way in (0, 1):

            @pl.when(self.passes(way, step))
            def _():
                slab = self.slab_of(way, step)
                self.add(way, slab, step - 1, part)
                self.copy(way, slab, step, part).start()

    def finish(self):
        last = self.at.chain - 2
        for part in range(PARTS):
            for way in (0, 1):

                @pl.when(self.receives(way, last))
                def _():
                    self.copy(way, 0, last, part).wait_recv()
                    self.landed(way, last, part).start()

            for way in (0, 1):

                @pl.when(self.receives(way, last))
                def _():
                    self.add(way, self.at.z, last, part)

    def sent(self):
        for step in range(self.at.chain - 1):
            for part in range(PARTS):
                for way in (0, 1):

                    @pl.when(self.sends(way, step))
                    def _():
                        self.copy(way, 0, step, part).wait_send()


def layer_kernel(
    size,
    tokens,
    cot,
    gain_one,
    gain_two,
    lens_in,
    w_query,
    w_key,
    w_value,
    w_out,
    w_gate,
    w_up,
    w_down,
    block_out,
    grad_tokens,
    grad_gains,
    g_query,
    g_key,
    g_value,
    g_out,
    g_gate,
    g_up,
    g_down,
    kept,
    slots,
    first,
    second,
    weights,
    qkv_weights,
    out_weights,
    grads,
    hidden,
    rows_two,
    turned,
    inner,
    units,
    sums_low,
    begun,
    qkv,
    attended,
    logs,
    table,
    head_sums,
    chain_stage,
    plane_stage,
    middle,
    total,
    last_stage,
    gain_rows,
    gains_in,
    lens,
    gain_parts,
    gain_peers,
    swap_sems,
    gather_send,
    gather_recv,
    reduce_send,
    reduce_recv,
    last_sems,
    plane_sems,
    first_sems,
    second_sems,
    small_sems,
    gain_sems,
    local_sems,
):
    chain, peers, rows, width, stages, unit, wide, seqs, tile = size
    at = Place(chain, peers)
    c, t, z = at.c, at.t, at.z
    group = rows * peers
    plane = 2 * group
    steps = chain - 1
    heads = wide // HEAD_DIM
    own_start = pl.multiple_of(c * group + t * rows, rows)
    query_tile = min(256, group)
    hub = min(256, unit)
    splits = PARTS if wide % (PARTS * LANES) == 0 else 1

    def slab_cols(s):
        return pl.ds(pl.multiple_of(s * 2 * unit, 2 * unit), 2 * unit)

    entry_barrier(at)

    def gain_copy(dp, source):
        place = gain_rows.at[:, pl.ds(pl.multiple_of(source * unit, unit), unit)]
        return remote(gains_in, place, gain_sems.at[0, dp], gain_sems.at[1, source], at.part(dp))

    own_gain = pltpu.make_async_copy(
        gains_in, gain_rows.at[:, pl.ds(pl.multiple_of(at.dp * unit, unit), unit)], local_sems.at[2]
    )

    def lens_copy(core):
        return remote(
            lens.at[core], lens.at[core], small_sems.at[0], small_sems.at[1], at.sibling()
        )

    lane = lax.broadcasted_iota(jnp.int32, (1, LANES), 1)
    gains_in[...] = jnp.zeros_like(gains_in)
    gains_in[0:1, :] = gain_one[...].astype(WIDE).reshape(1, unit)
    gains_in[1:2, :] = gain_two[...].astype(WIDE).reshape(1, unit)
    lens_row = jnp.zeros((8, LANES), WIDE)
    for s in range(seqs):
        lens_row = jnp.where(lane == s, lens_in[0, s].astype(WIDE), lens_row)
    lens[c] = lens_row

    def swap_copies(n):
        if n == 0:
            arrays = [(w, True, k * wide, wide, 0) for k, w in enumerate((w_query, w_key, w_value))]
            slab, down = qkv_weights.at[z], 0
        elif n == 1:
            arrays = [(w_out, False, 0, wide, 0)]
            slab, down = out_weights.at[z], 0
        else:
            arrays = [(w_gate, True, 0, unit, n - 2), (w_up, True, unit, unit, n - 2)]
            arrays.append((w_down, False, 0, unit, n - 2))
            slab, down = weights.at[n - 2, z], 2 * unit
        copies = []
        mine = pl.multiple_of(c * unit, unit)
        for k, (array, tall, offset, extent, stage) in enumerate(arrays):

            def half(core):
                count = (array.shape[1] if tall else array.shape[0]) // 2
                piece = pl.ds(pl.multiple_of(core * count + stage * extent, extent), extent)
                return array.at[:, piece] if tall else array.at[piece, :]

            if tall:
                place = slab.at[pl.ds(mine, unit), pl.ds(offset, extent)]
            else:
                place = slab.at[pl.ds(down, extent), pl.ds(mine, unit)]
            keep = pltpu.make_async_copy(half(c), place, swap_sems.at[0, n, k])
            give = remote(
                half(1 - c), place, swap_sems.at[1, n, k], swap_sems.at[2, n, k], at.sibling()
            )
            copies.append((keep, give))
        return copies

    def swapped(n):
        for keep, give in swap_copies(n):
            keep.wait()
            give.wait()

    for keep, give in swap_copies(0):
        keep.start()
        give.start()
    for dp in at.other_parts():
        gain_copy(dp, at.dp).start()
    own_gain.start()
    lens_copy(c).start()
    for n in range(1, stages + 2):
        for keep, give in swap_copies(n):
            keep.start()
            give.start()

    slabs = [qkv_weights, out_weights] + [weights.at[q] for q in range(stages)]
    stream = Stream(
        [
            ChainGather(at, ref, gather_send.at[n], gather_recv.at[n])
            for n, ref in enumerate(slabs)
        ],
        swapped,
    )
    gathers = [
        PlaneGather(at, full, rows, [plane_sems.at[n, k] for k in range(4)])
        for n, full in enumerate((hidden, rows_two, hidden, rows_two))
    ]
    plane_sums = [
        PlaneReduce(
            at,
            rows,
            tile,
            buffer,
            first.at[n],
            second.at[n],
            plane_stage,
            [first_sems.at[n, 0], first_sems.at[n, 1], second_sems.at[n, 0], second_sems.at[n, 1]],
            local_sems.at[4],
        )
        for n, buffer in enumerate((sums_low, sums_low, begun, sums_low))
    ]
    chain_sums = [
        ChainReduce(
            at,
            ref,
            height,
            slots.at[n],
            reduce_send.at[n],
            reduce_recv.at[n],
            chain_stage,
            local_sems,
        )
        for n, (ref, height) in enumerate(
            [(grads.at[q], 3 * unit) for q in range(stages)]
            + [(weights.at[0], 3 * wide), (weights.at[1], wide)]
        )
    ]
    sum_qkv, sum_out = chain_sums[stages], chain_sums[stages + 1]

    stream.go(2)

    for dp in at.other_parts():
        gain_copy(at.dp, dp).wait_recv()
    own_gain.wait()

    def strips(body):
        def each(i, carry):
            here = pl.ds(pl.multiple_of(i * STRIP, STRIP), STRIP)
            there = pl.ds(pl.multiple_of(own_start + i * STRIP, STRIP), STRIP)
            body(here, there)
            return carry

        lax.fori_loop(0, rows // STRIP, each, 0)

    def factor_of(values):
        return lax.rsqrt(jnp.mean(values * values, axis=-1, keepdims=True) + EPSILON)

    def first_norm(here, there):
        values = tokens[here, :].astype(WIDE)
        hidden[there, :] = (values * factor_of(values) * gain_rows[0:1, :]).astype(LOW)

    strips(first_norm)
    gathers[0].start()

    lens_copy(c).wait_send()
    lens_copy(1 - c).wait_recv()
    frequency = jnp.exp(lax.rem(lane, HALF).astype(WIDE) * (-2.0 * math.log(ROPE_BASE) / HEAD_DIM))
    side = jnp.where(lax.rem(lane, HEAD_DIM) < HALF, -1.0, 1.0)

    def table_rows(core):
        def body(i, carry):
            shape = (rows, LANES)
            row = (lax.broadcasted_iota(jnp.int32, shape, 0) + i * rows).astype(WIDE)
            start = jnp.zeros((1, 1), WIDE)
            base = jnp.zeros(shape, WIDE)
            valid = jnp.zeros(shape, WIDE)
            for s in range(seqs):
                length = lens[core, 0:1, s : s + 1]
                inside = (row >= start) & (row < start + length)
                base = jnp.where(inside, start, base)
                valid = jnp.where(inside, 1.0, valid)
                start = start + jnp.floor((length + (BLOCK - 1.0)) * (1.0 / BLOCK)) * BLOCK
            angle = (row - base) * frequency
            lowest = jnp.where(valid > 0.5, base, row)
            here = pl.ds(pl.multiple_of(core * group + i * rows, rows), rows)
            table[0, here, :] = jnp.cos(angle)
            table[1, here, :] = jnp.sin(angle) * side
            table[2, here, :] = jnp.where(lane == 0, lowest, valid)
            return carry

        lax.fori_loop(0, peers, body, 0)

    table_rows(0)
    table_rows(1)
    stream.go(2)

    def own_cotangent(here, there):
        rows_two[there, :] = (cot[here, :].astype(WIDE) * table[2, there, 1:2]).astype(LOW)

    strips(own_cotangent)
    gathers[0].forward()
    gathers[1].start()
    stream.go(1)
    gathers[0].finish()
    stream.complete(0)

    first_half = lax.rem(lax.broadcasted_iota(jnp.int32, (1, LANES), 1), HEAD_DIM) < HALF

    def swap_halves(values):
        return jnp.where(
            first_half, pltpu.roll(values, LANES - HALF, 1), pltpu.roll(values, HALF, 1)
        )

    def rotated(values, there, sign):
        pieces = []
        for n in range(0, values.shape[1], LANES):
            piece = values[:, n : n + LANES]
            pieces.append(
                piece * table[0, there, :] + sign * (swap_halves(piece) * table[1, there, :])
            )
        return jnp.concatenate(pieces, axis=1) if len(pieces) > 1 else pieces[0]

    def project(i, carry):
        here = pl.ds(pl.multiple_of(i * tile, tile), tile)
        sums = jnp.zeros((tile, 3 * wide), WIDE)
        for s in range(chain):
            sums += dot_nn(hidden[here, s * 2 * unit : (s + 1) * 2 * unit], qkv_weights[s])
        qkv[0, here, :] = rotated(sums[:, :wide], here, 1.0).astype(LOW)
        qkv[1, here, :] = rotated(sums[:, wide : 2 * wide], here, 1.0).astype(LOW)
        qkv[2, here, :] = sums[:, 2 * wide :].astype(LOW)
        return carry

    lax.fori_loop(0, plane // tile, project, 0)
    keep_rows = pltpu.make_async_copy(hidden, kept, local_sems.at[5])
    keep_rows.start()
    stream.go(2)
    gathers[1].forward()

    head_lane = lax.div(lax.broadcasted_iota(jnp.int32, (1, wide), 1), HEAD_DIM)

    def masked(scores, here, offset):
        column = lax.broadcasted_iota(jnp.int32, scores.shape, 1)
        row = lax.broadcasted_iota(jnp.int32, scores.shape, 0) + offset
        lowest = table[2, here, 0:1].astype(jnp.int32)
        return jnp.where((column >= lowest) & (column <= row), scores, MASKED)

    def attend(core, low, high):
        base = pl.multiple_of(core * group, group)

        def body(h, carry):
            lanes = jnp.where(head_lane == h, 1.0, 0.0)
            for b in range(group // query_tile):
                here = pl.ds(pl.multiple_of(base + b * query_tile, query_tile), query_tile)
                keys = pl.ds(base, (b + 1) * query_tile)
                query = (qkv[0, here, :].astype(WIDE) * (lanes * SCALE)).astype(LOW)
                scores = masked(dot_nt(query, qkv[1, keys, :]), here, b * query_tile)
                peak = jnp.max(scores, axis=-1, keepdims=True)
                exponent = jnp.exp(scores - peak)
                sums = jnp.sum(exponent, axis=-1, keepdims=True)
                weight = (exponent / sums).astype(LOW)
                mixed = dot_nn(weight, qkv[2, keys, :]) * lanes
                place = slice(b * query_tile, (b + 1) * query_tile)
                earlier = jnp.where(h == 0, 0.0, head_sums[0, place, :])
                head_sums[0, place, :] = earlier + mixed
                logs[here, :] = jnp.where(lane == h, peak + jnp.log(sums), logs[here, :])
            return carry

        if low == 0:
            logs[pl.ds(base, group), :] = jnp.zeros((group, LANES), WIDE)
            head_sums[0] = jnp.zeros((group, wide), WIDE)
        lax.fori_loop(low, high, body, 0)
        if high == heads:
            attended[pl.ds(base, group), :] = head_sums[0].astype(LOW)

    middle_head = heads // 2
    attend(1 - c, 0, middle_head)
    stream.go(2)
    attend(1 - c, middle_head, heads)
    keep_rows.wait()
    stream.complete(1)

    def product_tile(terms):
        def compute(source, out, extras):
            def body(s, carry):
                cols = slab_cols(s)
                sums = terms(source, s)
                for extra in extras:
                    sums += extra[:, cols].astype(WIDE)
                out[:, cols] = sums.astype(LOW)
                return carry

            lax.fori_loop(0, chain, body, 0)

        return compute

    out_tile = product_tile(lambda source, s: dot_nn(attended[source, :], out_weights[s]))
    plane_sums[0].half(out_tile)
    attend(c, 0, heads)
    stream.go(1)
    plane_sums[0].rest(out_tile)
    gathers[1].finish()
    stream.go(3)
    plane_sums[0].finish(total)

    def second_norm(here, there):
        values = tokens[here, :].astype(WIDE) + total[here, :] * table[2, there, 1:2]
        middle[here, :] = values
        hidden[there, :] = (values * factor_of(values) * gain_rows[1:2, :]).astype(LOW)

    strips(second_norm)
    gathers[2].start()
    stream.go(2)
    gathers[2].forward()
    plane_sums[0].sent()
    stream.go(1)
    gathers[2].finish()

    def hidden_units(q):
        def body(i, carry):
            these = pl.ds(pl.multiple_of(i * tile, tile), tile)
            gate_up = jnp.zeros((tile, 2 * unit), WIDE)
            grad_inner = jnp.zeros((tile, unit), WIDE)
            for s in range(chain):
                cols = slice(s * 2 * unit, (s + 1) * 2 * unit)
                gate_up += dot_nn(hidden[these, cols], weights[q, s, 0 : 2 * unit, :])
                grad_inner += dot_nt(rows_two[these, cols], weights[q, s, 2 * unit :, :])
            gate, up = gate_up[:, :unit], gate_up[:, unit:]
            sigmoid_gate = jax.nn.sigmoid(gate)
            inner[q, these, :] = (gate * sigmoid_gate * up).astype(LOW)
            units[q, these, 0:unit] = (
                grad_inner * up * sigmoid_gate * (1.0 + gate * (1.0 - sigmoid_gate))
            ).astype(LOW)
            units[q, these, unit : 2 * unit] = (grad_inner * gate * sigmoid_gate).astype(LOW)
            return carry

        lax.fori_loop(0, plane // tile, body, 0)

    eye = identity(hub)

    def turn_into(start, source):
        extent = min(hub, source.shape[1])

        def body(i, carry):
            cols = pl.ds(pl.multiple_of(i * extent, extent), extent)
            place = pl.ds(pl.multiple_of(start + i * extent, extent), extent)
            turned[place, :] = dot_nt(eye[:extent, :extent], source[:, cols]).astype(LOW)
            return carry

        lax.fori_loop(0, source.shape[1] // extent, body, 0)

    def in_grads(q):
        turn_into(0, units.at[q])

        def body(s, carry):
            grads[q, s, 0 : 2 * unit, :] = dot_nn(
                turned[0 : 2 * unit, :], hidden[:, slab_cols(s)]
            ).astype(LOW)
            return carry

        lax.fori_loop(0, chain, body, 0)

    def down_grads(q):
        turn_into(2 * unit, inner.at[q])

        def body(s, carry):
            grads[q, s, 2 * unit :, :] = dot_nn(
                turned[2 * unit :, :], rows_two[:, slab_cols(s)]
            ).astype(LOW)
            return carry

        lax.fori_loop(0, chain, body, 0)

    def hidden_sums(stage_list):
        return product_tile(
            lambda source, s: sum(
                dot_nt(units[q, source, :], weights[q, s, 0 : 2 * unit, :]) for q in stage_list
            )
        )

    def begin_hidden():
        begin = hidden_sums(range(stages - 1))
        for i in range(group // tile):
            here = pl.ds(i * tile, tile)
            begin(plane_sums[1].source(1 - c, i), sums_low.at[here], [])
            begin(plane_sums[1].source(c, i), begun.at[here], [])

    for q in range(stages):
        stream.complete(q + 2)
        hidden_units(q)
        if q == stages - 1:
            break
        stream.go(1)
        in_grads(q)
        down_grads(q)
        for part in range(PARTS):
            chain_sums[q].ends(0, part)
        stream.go(1)
        for k in range(1, steps):
            for part in range(PARTS):
                stream.go(1)
                chain_sums[q].ends(k, part)
                if k > 1:
                    chain_sums[q].step(k - 1, part)
                if q == stages - 2 and (k, part) == (1, 0):
                    begin_hidden()
        if q == stages - 2 and steps == 1:
            begin_hidden()

    branch_tile = product_tile(
        lambda source, s: sum(
            dot_nn(inner[q, source, :], weights[q, s, 2 * unit :, :]) for q in range(stages)
        )
    )

    def chain_steps(n, low, high):
        for k in range(max(low, 1), high):
            for part in range(PARTS):
                chain_sums[n].step(k, part)

    def last_step(n):
        chain_steps(n, steps - 1, steps)

    def placed(n, core, source):
        own = chain_sums[n].slabs.at[z]
        cols = pl.ds(pl.multiple_of(core * unit, unit), unit)
        stage = last_stage.at[n % 2, core]
        if n < stages:
            place = pl.ds(pl.multiple_of((source * stages + n) * unit, unit), unit)
            return [
                (stage.at[0, :, pl.ds(0, unit)], g_gate.at[:, place]),
                (stage.at[1, :, pl.ds(0, unit)], g_up.at[:, place]),
                (own.at[pl.ds(2 * unit, unit), cols], g_down.at[place, :]),
            ]
        place = pl.ds(pl.multiple_of(source * wide, wide), wide)
        if n == stages:
            return [
                (stage.at[k, :, pl.ds(0, wide)], out.at[:, place])
                for k, out in enumerate((g_query, g_key, g_value))
            ]
        return [(own.at[pl.ds(0, wide), cols], g_out.at[place, :])]

    def last_copies(n):
        copies = []
        for k, ((mine, place), (theirs, _)) in enumerate(
            zip(placed(n, c, c), placed(n, 1 - c, c))
        ):
            keep = pltpu.make_async_copy(mine, place, last_sems.at[0, n, k])
            give = remote(theirs, place, last_sems.at[1, n, k], last_sems.at[2, n, k], at.sibling())
            copies.append((keep, give))
        return copies

    def finish_sum(n):
        chain_sums[n].finish()
        own = chain_sums[n].slabs
        pieces = []
        if n < stages:
            pieces = [(k, k * unit, 0, unit) for k in range(2)]
        elif n == stages:
            lanes = wide // splits
            pieces = [
                (k, (m * 3 + k) * lanes, m * lanes, lanes) for m in range(splits) for k in range(3)
            ]
        for core in (0, 1):
            for k, start, place, extent in pieces:
                piece = own[z, start : start + extent, core * unit : (core + 1) * unit]
                last_stage[n % 2, core, k, :, place : place + extent] = turn(piece, eye)
        for keep, give in last_copies(n):
            keep.start()
            give.start()

    def settle(n):
        for keep, give in last_copies(n):
            keep.wait()
            give.wait()
        chain_sums[n].sent()

    down_grads(stages - 1)
    last_tile = hidden_sums([stages - 1])
    plane_sums[1].half(last_tile, begun=True)
    plane_sums[1].rest(last_tile, begun=begun)
    in_grads(stages - 1)
    for k in range(steps):
        for part in range(PARTS):
            chain_sums[stages - 1].ends(k, part)
    for q in range(min(2, stages - 1)):
        last_step(q)
    plane_sums[2].half(branch_tile)
    bring_rows = pltpu.make_async_copy(kept, hidden, local_sems.at[5])
    bring_rows.start()
    plane_sums[1].finish(total)

    def second_back(here, there):
        values = middle[here, :]
        factor = factor_of(values)
        normed = values * factor
        grad = total[here, :]
        gain_parts[1:2, :] += jnp.sum(grad * normed, axis=0, keepdims=True)
        scaled = grad * gain_rows[1:2, :]
        mean = jnp.mean(scaled * normed, axis=-1, keepdims=True)
        result = cot[here, :].astype(WIDE) + factor * (scaled - normed * mean)
        grad_tokens[here, :] = result
        rows_two[there, :] = (result * table[2, there, 1:2]).astype(LOW)

    gain_parts[...] = jnp.zeros_like(gain_parts)
    strips(second_back)
    gathers[3].start()
    plane_sums[1].sent()
    for q in range(2, stages - 1):
        last_step(q)
    plane_sums[2].rest(branch_tile)
    chain_steps(stages - 1, 1, steps - 1)
    for chain_gather in stream.chains:
        chain_gather.sent()
    finish_sum(0)
    gathers[3].forward()
    gathers[3].finish()

    def finish_branch():
        plane_sums[2].finish(total)

        def last_rows(here, there):
            result = middle[here, :] + total[here, :] * table[2, there, 1:2]
            block_out[here, :] = result.astype(LOW)

        strips(last_rows)

    grad_attended = inner.at[0]

    def attended_grad(i, carry):
        here = pl.ds(pl.multiple_of(i * tile, tile), tile)
        sums = jnp.zeros((tile, wide), WIDE)
        for s in range(chain):
            sums += dot_nt(rows_two[here, s * 2 * unit : (s + 1) * 2 * unit], out_weights[s])
        grad_attended[here, :] = sums.astype(LOW)
        return carry

    turn_into(0, attended)

    def out_grads(s, carry):
        weights[1, s, 0:wide, :] = dot_nn(turned[0:wide, :], rows_two[:, slab_cols(s)]).astype(LOW)
        return carry

    lax.fori_loop(0, chain, out_grads, 0)
    for k in range(steps):
        for part in range(PARTS):
            sum_out.ends(k, part)
    lax.fori_loop(0, plane // tile, attended_grad, 0)

    def attend_back(core, low, high):
        base = core * group

        def body(h, carry):
            lanes = jnp.where(head_lane == h, 1.0, 0.0)
            lanes_low = lanes.astype(LOW)
            for b in range(group // query_tile):
                here = slice(base + b * query_tile, base + (b + 1) * query_tile)
                keys = slice(base, base + (b + 1) * query_tile)
                place = slice(b * query_tile, (b + 1) * query_tile)
                reach = slice(0, (b + 1) * query_tile)
                query = qkv[0, here, :] * lanes_low
                grad = grad_attended[here, :] * lanes_low
                scores = masked(dot_nt(query, qkv[1, keys, :]) * SCALE, here, b * query_tile)
                log_total = jnp.sum(
                    jnp.where(lane == h, logs[here, :], 0.0), axis=-1, keepdims=True
                )
                probs = jnp.exp(scores - log_total)
                grad_probs = dot_nt(grad, qkv[2, keys, :])
                shift = jnp.sum(probs * grad_probs, axis=-1, keepdims=True)
                grad_scores = (probs * (grad_probs - shift) * SCALE).astype(LOW)
                head_sums[0, place, :] += dot_nn(grad_scores, qkv[1, keys, :]) * lanes
                head_sums[1, reach, :] += dot_nn(turn(grad_scores, eye), query)
                head_sums[2, reach, :] += dot_nn(turn(probs.astype(LOW), eye), grad)
            return carry

        for k in range(3):
            head_sums[k] = jnp.zeros((group, wide), WIDE)
        lax.fori_loop(low, high, body, 0)
        lanes = slice(low * HEAD_DIM, high * HEAD_DIM)

        def back(i, carry):
            there = pl.ds(pl.multiple_of(base + i * query_tile, query_tile), query_tile)
            here = pl.ds(pl.multiple_of(i * query_tile, query_tile), query_tile)
            for k in range(2):
                values = rotated(head_sums[k, here, lanes], there, -1.0)
                units[0, there, k * wide + lanes.start : k * wide + lanes.stop] = values.astype(LOW)
            units[1, there, lanes] = head_sums[2, here, lanes].astype(LOW)
            return carry

        lax.fori_loop(0, group // query_tile, back, 0)

    def qkv_grads(n):
        lanes = wide // splits
        turn_into(0, units.at[0, :, pl.ds(n * lanes, lanes)])
        turn_into(lanes, units.at[0, :, pl.ds(wide + n * lanes, lanes)])
        turn_into(2 * lanes, units.at[1, :, pl.ds(n * lanes, lanes)])

        parts = range(n * PARTS // splits, (n + 1) * PARTS // splits)
        for k in range(chain):
            s = jnp.where(at.z < (chain + 1) // 2, chain - 1 - k, k)
            weights[0, s, n * 3 * lanes : (n + 1) * 3 * lanes, :] = dot_nn(
                turned[0 : 3 * lanes, :], hidden[:, slab_cols(s)]
            ).astype(LOW)
            if k < steps:
                for part in parts:
                    sum_qkv.ends(k, part)

    for n in range(splits):
        low, high = n * heads // splits, (n + 1) * heads // splits
        attend_back(0, low, high)
        if n == splits - 1:
            last_step(stages - 1)
        attend_back(1, low, high)
        if n == 0:
            bring_rows.wait()
        qkv_grads(n)

    first_tile = product_tile(
        lambda source, s: dot_nt(units[0, source, :], qkv_weights[s, :, 0 : 2 * wide])
        + dot_nt(units[1, source, 0:wide], qkv_weights[s, :, 2 * wide :])
    )
    chain_steps(stages + 1, 1, steps - 1)
    plane_sums[3].half(first_tile)
    plane_sums[3].rest(first_tile)

    def qkv_steps(part, low, high):
        for k in range(max(low, 1), high):
            sum_qkv.step(k, part)

    qkv_steps(0, 1, steps - 1)
    finish_sum(1)
    for part in range(1, PARTS):
        qkv_steps(part, 1, steps - 1)
    last_step(stages + 1)
    qkv_steps(0, steps - 1, steps)
    finish_branch()
    if stages > 2:
        settle(0)
        finish_sum(2)
    for part in range(1, PARTS):
        qkv_steps(part, steps - 1, steps)
    finish_sum(stages + 1)
    for q in range(3, stages):
        settle(q - 2)
        finish_sum(q)
    plane_sums[3].finish(total)

    def first_back(here, there):
        values = tokens[here, :].astype(WIDE)
        factor = factor_of(values)
        normed = values * factor
        grad = total[here, :]
        gain_parts[0:1, :] += jnp.sum(grad * normed, axis=0, keepdims=True)
        scaled = grad * gain_rows[0:1, :]
        mean = jnp.mean(scaled * normed, axis=-1, keepdims=True)
        grad_tokens[here, :] += factor * (scaled - normed * mean)

    strips(first_back)

    own_cols = pl.ds(pl.multiple_of(at.dp * unit, unit), unit)

    def gain_sum_copy(dp, source):
        cols = pl.ds(pl.multiple_of(dp * unit, unit), unit)
        return remote(
            gain_parts.at[:, cols],
            gain_peers.at[source],
            gain_sems.at[2, dp],
            gain_sems.at[3, source],
            at.part(dp),
        )

    def gain_peer_copy(peer, source):
        parts = 2 * chain
        return remote(
            gain_peers.at[parts + t],
            gain_peers.at[parts + source],
            gain_sems.at[4, peer],
            gain_sems.at[5, source],
            at.peer(peer),
        )

    for dp in at.other_parts():
        gain_sum_copy(dp, at.dp).start()
    settle(stages - 2)
    sums = gain_parts[:, own_cols]
    for dp in at.other_parts():
        gain_sum_copy(at.dp, dp).wait_recv()
        sums += gain_peers[dp]
    gain_peers[2 * chain + t] = sums
    for peer in at.other_peers():
        gain_peer_copy(peer, t).start()
    for peer in at.other_peers():
        gain_peer_copy(t, peer).wait_recv()
        sums += gain_peers[2 * chain + peer]
    grad_gains[...] = sums
    settle(stages - 1)
    finish_sum(stages)
    settle(stages)
    settle(stages + 1)
    plane_sums[2].sent()
    plane_sums[3].sent()
    for dp in at.other_parts():
        gain_copy(dp, at.dp).wait_send()
        gain_sum_copy(dp, at.dp).wait_send()
    for peer in at.other_peers():
        gain_peer_copy(peer, t).wait_send()


def finish_kernel(*refs):
    count = len(refs) // 2
    sources, outs = refs[:count], refs[count:]
    for source, out in zip(sources[:2] + sources[3:], outs[: count - 1]):
        out[...] = source[...].astype(out.dtype)
    outs[count - 1][...] = sources[2][0:1, :]
    outs[count][...] = sources[2][1:2, :]


def finish(arrays):
    steps = 4
    gains = arrays[2]

    def split(array):
        return pl.BlockSpec((array.shape[0] // steps, array.shape[1]), lambda i: (i, 0))

    whole = pl.BlockSpec(gains.shape, lambda i: (0, 0))
    row = pl.BlockSpec((1, gains.shape[1]), lambda i: (0, 0))
    kept = arrays[:2] + arrays[3:]
    dtypes = [array.dtype for array in arrays[:2]] + [WIDE] * len(arrays[3:])
    return pl.pallas_call(
        finish_kernel,
        grid=(steps,),
        out_shape=[jax.ShapeDtypeStruct(a.shape, d) for a, d in zip(kept, dtypes)]
        + [jax.ShapeDtypeStruct((1, gains.shape[1]), WIDE)] * 2,
        in_specs=[split(a) for a in arrays[:2]] + [whole] + [split(a) for a in arrays[3:]],
        out_specs=[split(a) for a in kept] + [row] * 2,
        compiler_params=pltpu.CompilerParams(vmem_limit_bytes=VMEM_BYTES),
        name="finish",
    )(*arrays)


def on_device(
    tokens_in,
    seq_lens,
    w_query,
    w_key,
    w_value,
    w_out,
    norm1_gain,
    w_gate,
    w_up,
    w_down,
    norm2_gain,
    out_cotangent,
):
    n_dp, peers = lax.axis_size("dp"), lax.axis_size("tensor")
    chain = n_dp // 2
    rows, width = tokens_in.shape
    unit = width // n_dp
    wide = w_query.shape[1] // 2
    stages = w_gate.shape[1] // 2 // unit
    seqs = seq_lens.shape[1]
    group = rows * peers
    plane = 2 * group
    tile = min(256, group)
    slab = (3 * unit, 2 * unit)
    size = (chain, peers, rows, width, stages, unit, wide, seqs, tile)
    hbm = pl.BlockSpec(memory_space=pl.ANY)
    vmem = pl.BlockSpec(memory_space=pltpu.VMEM)
    smem = pl.BlockSpec(memory_space=pltpu.SMEM)
    dma = pltpu.SemaphoreType.DMA

    def like(array):
        return jax.ShapeDtypeStruct(array.shape, LOW)

    outs = pl.pallas_call(
        functools.partial(layer_kernel, size),
        out_shape=(
            jax.ShapeDtypeStruct((rows, width), LOW),
            jax.ShapeDtypeStruct((rows, width), WIDE),
            jax.ShapeDtypeStruct((8, unit), WIDE),
            like(w_query),
            like(w_key),
            like(w_value),
            like(w_out),
            like(w_gate),
            like(w_up),
            like(w_down),
            jax.ShapeDtypeStruct((plane, width), LOW),
            jax.ShapeDtypeStruct((stages + 2, 2, chain - 1) + slab, LOW),
            jax.ShapeDtypeStruct((4, group, width), LOW),
            jax.ShapeDtypeStruct((4, peers, rows, width), LOW),
        ),
        in_specs=[vmem, vmem, vmem, vmem, smem] + [hbm] * 7,
        out_specs=(vmem, vmem, vmem) + (hbm,) * 11,
        scratch_shapes=[
            pltpu.VMEM((stages, chain) + slab, LOW),
            pltpu.VMEM((chain, 2 * unit, 3 * wide), LOW),
            pltpu.VMEM((chain, wide, 2 * unit), LOW),
            pltpu.VMEM((stages, chain) + slab, LOW),
            pltpu.VMEM((plane, width), LOW),
            pltpu.VMEM((plane, width), LOW),
            pltpu.VMEM((3 * unit, plane), LOW),
            pltpu.VMEM((stages, plane, unit), LOW),
            pltpu.VMEM((stages, plane, 2 * unit), LOW),
            pltpu.VMEM((group, width), LOW),
            pltpu.VMEM((group, width), LOW),
            pltpu.VMEM((3, plane, wide), LOW),
            pltpu.VMEM((plane, wide), LOW),
            pltpu.VMEM((plane, LANES), WIDE),
            pltpu.VMEM((3, plane, LANES), WIDE),
            pltpu.VMEM((3, group, wide), WIDE),
            pltpu.VMEM((2, slab[0] // PARTS, slab[1]), LOW),
            pltpu.VMEM((tile, width), LOW),
            pltpu.VMEM((rows, width), WIDE),
            pltpu.VMEM((rows, width), WIDE),
            pltpu.VMEM((2, 2, 3, unit, max(unit, wide)), LOW),
            pltpu.VMEM((8, width), WIDE),
            pltpu.VMEM((8, unit), WIDE),
            pltpu.VMEM((2, 8, LANES), WIDE),
            pltpu.VMEM((8, width), WIDE),
            pltpu.VMEM((n_dp + peers, 8, unit), WIDE),
            dma((3, stages + 2, 3)),
            dma((stages + 2, 2, chain - 1, PARTS)),
            dma((stages + 2, 2, chain - 1, PARTS)),
            dma((stages + 2, 2, chain - 1, PARTS)),
            dma((stages + 2, 2, chain - 1, PARTS)),
            dma((3, stages + 2, 3)),
            dma((4, 4, peers)),
            dma((4, 2, group // tile)),
            dma((4, 2, peers)),
            dma((2,)),
            dma((6, n_dp)),
            dma((6,)),
        ],
        compiler_params=pltpu.CompilerParams(
            collective_id=0, has_side_effects=True, vmem_limit_bytes=VMEM_BYTES
        ),
        cost_estimate=pl.CostEstimate(
            flops=6 * plane * width * (4 * wide + 3 * unit * stages),
            bytes_accessed=16 * width * (4 * wide + 3 * unit * stages),
            transcendentals=0,
        ),
        name="layer",
    )(
        tokens_in,
        out_cotangent,
        norm1_gain,
        norm2_gain,
        seq_lens,
        w_query,
        w_key,
        w_value,
        w_out,
        w_gate,
        w_up,
        w_down,
    )
    block_out, grad_tokens, *weight_grads, gain_one, gain_two = finish(outs[:10])
    return (
        block_out,
        grad_tokens,
        *weight_grads[:4],
        gain_one.reshape(unit),
        *weight_grads[4:],
        gain_two.reshape(unit),
    )


def solution(mesh):
    return jax.shard_map(
        on_device,
        mesh=mesh,
        in_specs=(
            P(("dp", "tensor"), None),
            P("dp", None),
            P("dp", "tensor"),
            P("dp", "tensor"),
            P("dp", "tensor"),
            P("tensor", "dp"),
            P("dp"),
            P("dp", "tensor"),
            P("dp", "tensor"),
            P("tensor", "dp"),
            P("dp"),
            P(("dp", "tensor"), None),
        ),
        out_specs=(
            P(("dp", "tensor"), None),
            P(("dp", "tensor"), None),
            P("dp", "tensor"),
            P("dp", "tensor"),
            P("dp", "tensor"),
            P("tensor", "dp"),
            P("dp"),
            P("dp", "tensor"),
            P("dp", "tensor"),
            P("tensor", "dp"),
            P("dp"),
        ),
        check_vma=False,
    )
```

```python
import functools
import math

import jax
import jax.numpy as jnp
from jax import lax
from jax.experimental import pallas as pl
from jax.experimental.pallas import tpu as pltpu
from jax.sharding import PartitionSpec as P

HEAD_DIM = 64
HALF = HEAD_DIM // 2
BLOCK = 128
LANES = 128
EPSILON = 1e-05
ROPE_BASE = 130000.0
MASKED = -1e30
SCALE = HEAD_DIM ** (-0.5)

LOW = jnp.bfloat16
WIDE = jnp.float32
VMEM_BYTES = 64 * 1024 * 1024
PARTS = 2
STRIP = 32


def dot_nn(left, right):
    return lax.dot_general(left, right, (((1,), (0,)), ((), ())), preferred_element_type=WIDE)


def dot_nt(left, right):
    return lax.dot_general(left, right, (((1,), (1,)), ((), ())), preferred_element_type=WIDE)


def identity(size):
    across = lax.broadcasted_iota(jnp.int32, (size, size), 0)
    down = lax.broadcasted_iota(jnp.int32, (size, size), 1)
    return jnp.where(across == down, 1.0, 0.0).astype(LOW)


def turn(values, eye):
    size = eye.shape[0]
    width = values.shape[1]
    if width <= size:
        return dot_nt(eye[:width, :width], values).astype(LOW)
    blocks = [dot_nt(eye, values[:, n : n + size]).astype(LOW) for n in range(0, width, size)]
    return jnp.concatenate(blocks, axis=0)


class Place:
    def __init__(self, chain, peers):
        self.chain, self.peers = chain, peers
        self.dp = lax.axis_index("dp")
        self.t = lax.axis_index("tensor")
        self.c = lax.rem(self.dp, 2)
        self.z = lax.div(self.dp, 2)

    def sibling(self):
        return {"dp": self.dp + 1 - 2 * self.c, "tensor": self.t}

    def along(self, step):
        return {"dp": self.dp + 2 * step, "tensor": self.t}

    def part(self, dp):
        return {"dp": dp, "tensor": self.t}

    def peer(self, t):
        return {"dp": self.dp, "tensor": t}

    def other_peers(self):
        return [lax.rem(self.t + n, self.peers) for n in range(1, self.peers)]

    def other_parts(self):
        parts = 2 * self.chain
        return [lax.rem(self.dp + n, parts) for n in range(1, parts)]


def remote(src, dst, send, recv, device):
    return pltpu.make_async_remote_copy(
        src_ref=src,
        dst_ref=dst,
        send_sem=send,
        recv_sem=recv,
        device_id=device,
        device_id_type=pl.DeviceIdType.MESH,
    )


def fetch(src, dst, sem):
    copy = pltpu.make_async_copy(src, dst, sem)
    copy.start()
    copy.wait()


def entry_barrier(at):
    barrier = pltpu.get_barrier_semaphore()
    devices = [at.peer(t) for t in at.other_peers()] + [at.part(dp) for dp in at.other_parts()]
    for device in devices:
        pl.semaphore_signal(barrier, inc=1, device_id=device, device_id_type=pl.DeviceIdType.MESH)
    pl.semaphore_wait(barrier, len(devices))


class PlaneGather:
    def __init__(self, at, full, rows, sems):
        self.at, self.full, self.rows = at, full, rows
        self.group = rows * at.peers
        self.send, self.recv, self.pass_send, self.pass_recv = sems

    def block(self, c, t):
        start = pl.multiple_of(c * self.group + t * self.rows, self.rows)
        return self.full.at[pl.ds(start, self.rows)]

    def to_peer(self, t):
        at = self.at
        own = self.block(at.c, at.t)
        return remote(own, own, self.send.at[t], self.recv.at[at.t], at.peer(t))

    def from_peer(self, t):
        block = self.block(self.at.c, t)
        return remote(block, block, self.send.at[t], self.recv.at[t], self.at.peer(t))

    def to_sibling(self, t):
        block = self.block(self.at.c, t)
        return remote(
            block, block, self.pass_send.at[t], self.pass_recv.at[t], self.at.sibling()
        )

    def from_sibling(self, t):
        block = self.block(1 - self.at.c, t)
        return remote(
            block, block, self.pass_send.at[t], self.pass_recv.at[t], self.at.sibling()
        )

    def start(self):
        for t in self.at.other_peers():
            self.to_peer(t).start()
        self.to_sibling(self.at.t).start()

    def forward(self):
        for t in self.at.other_peers():
            self.from_peer(t).wait_recv()
            self.to_sibling(t).start()

    def finish(self):
        for t in range(self.at.peers):
            self.from_sibling(t).wait_recv()
        for t in self.at.other_peers():
            self.to_peer(t).wait_send()
        for t in range(self.at.peers):
            self.to_sibling(t).wait_send()


class PlaneReduce:
    def __init__(self, at, rows, tile, buffer, first, second, stage, sems, local):
        self.at, self.rows, self.tile, self.buffer = at, rows, tile, buffer
        self.group = rows * at.peers
        self.first, self.second, self.stage, self.local = first, second, stage, local
        self.send1, self.recv1, self.send2, self.recv2 = sems

    def source(self, c, i):
        return pl.ds(pl.multiple_of(c * self.group + i * self.tile, self.tile), self.tile)

    def to_sibling(self, i):
        here = pl.ds(i * self.tile, self.tile)
        return remote(
            self.buffer.at[here],
            self.first.at[here],
            self.send1.at[i],
            self.recv1.at[i],
            self.at.sibling(),
        )

    def to_peer(self, t, source):
        return remote(
            self.buffer.at[pl.ds(pl.multiple_of(t * self.rows, self.rows), self.rows)],
            self.second.at[source],
            self.send2.at[t],
            self.recv2.at[source],
            self.at.peer(t),
        )

    def half(self, compute, begun=False):
        for i in range(self.group // self.tile):
            out = self.buffer.at[pl.ds(i * self.tile, self.tile)]
            compute(self.source(1 - self.at.c, i), out, [out] if begun else [])
            self.to_sibling(i).start()

    def rest(self, compute, begun=None):
        at = self.at
        for i in range(self.group // self.tile):
            here = pl.ds(i * self.tile, self.tile)
            self.to_sibling(i).wait_recv()
            fetch(self.first.at[here], self.stage, self.local)
            self.to_sibling(i).wait_send()
            extras = [self.stage] if begun is None else [self.stage, begun.at[here]]
            compute(self.source(at.c, i), self.buffer.at[here], extras)
            for j in range(i * self.tile // self.rows, (i + 1) * self.tile // self.rows):

                @pl.when(at.t != j)
                def _():
                    self.to_peer(j, at.t).start()

    def finish(self, out):
        at = self.at
        own = pl.ds(pl.multiple_of(at.t * self.rows, self.rows), self.rows)
        out[...] = self.buffer[own, :].astype(WIDE)
        for t in at.other_peers():
            self.to_peer(at.t, t).wait_recv()
            fetch(self.second.at[t], self.stage.at[pl.ds(0, self.rows)], self.local)
            out[...] += self.stage[0 : self.rows, :].astype(WIDE)

    def sent(self):
        for t in self.at.other_peers():
            self.to_peer(t, self.at.t).wait_send()


class ChainGather:
    def __init__(self, at, slabs, send, recv):
        self.at, self.slabs, self.sems = at, slabs, (send, recv)
        self.height = slabs.shape[1] // PARTS

    def copy(self, way, slab, step, part):
        send, recv = self.sems
        ref = self.slabs.at[slab, pl.ds(part * self.height, self.height)]
        return remote(
            ref,
            ref,
            send.at[way, step, part],
            recv.at[way, step, part],
            self.at.along(1 - 2 * way),
        )

    def each_send(self, step, part, act):
        z, last = self.at.z, self.at.chain - 1

        @pl.when((z < last) & (z >= max(step, 1)))
        def _():
            act(self.copy(0, z - step, step, part))

        @pl.when((z > 0) & (z + step <= last) & (z + 1 - min(step, 1) <= last))
        def _():
            act(self.copy(1, z + step, step, part))

    def each_end(self, part, act):
        z, last = self.at.z, self.at.chain - 1

        @pl.when(z == 0)
        def _():
            act(self.copy(0, 0, 0, part))

        @pl.when(z == last)
        def _():
            act(self.copy(1, last, 0, part))

    def start(self, step, part):
        self.each_send(step, part, lambda copy: copy.start())

    def start_end(self, part):
        self.each_end(part, lambda copy: copy.start())

    def sent(self):
        for part in range(PARTS):
            self.each_end(part, lambda copy: copy.wait_send())
            for step in range(self.at.chain - 1):
                self.each_send(step, part, lambda copy: copy.wait_send())

    def arrived(self, step, part):
        z, last = self.at.z, self.at.chain - 1

        @pl.when(z - 1 - step >= 0)
        def _():
            self.copy(0, z - 1 - step, step, part).wait_recv()

        @pl.when(z + 1 + step <= last)
        def _():
            self.copy(1, z + 1 + step, step, part).wait_recv()


class Stream:
    def __init__(self, chains, swapped):
        self.chains, self.swapped = chains, swapped
        self.steps = chains[0].at.chain - 1
        self.messages = [
            (n, step, part)
            for n in range(len(chains))
            for step in range(self.steps)
            for part in range(PARTS)
        ]
        self.ends = [(n, part) for n in range(len(chains)) for part in range(PARTS)]
        self.next = 0
        self.ready = 0

    def need(self, n):
        while self.ready <= n:
            self.swapped(self.ready)
            self.ready += 1

    def go(self, count=1):
        for _ in range(count):
            done = self.next - PARTS
            if 0 <= done < len(self.messages):
                n, step, part = self.messages[done]
                self.chains[n].arrived(step, part)
            if self.next < len(self.messages):
                n, step, part = self.messages[self.next]
                self.need(n)
                self.chains[n].start(step, part)
            if self.next < len(self.ends):
                n, part = self.ends[self.next]
                self.need(n)
                self.chains[n].start_end(part)
            self.next += 1

    def complete(self, n):
        while self.next < (n + 1) * self.steps * PARTS + PARTS:
            self.go()


class ChainReduce:
    def __init__(self, at, slabs, height, slots, send, recv, stage, local):
        self.at, self.slabs, self.slots, self.sems = at, slabs, slots, (send, recv)
        self.stage, self.local = stage, local
        self.height = height // PARTS

    def copy(self, way, slab, step, part):
        send, recv = self.sems
        rows = pl.ds(part * self.height, self.height)
        return remote(
            self.slabs.at[slab, rows],
            self.slots.at[way, step, rows],
            send.at[way, step, part],
            recv.at[way, step, part],
            self.at.along(1 - 2 * way),
        )

    def slab_of(self, way, step):
        last = self.at.chain - 1
        return self.at.z + last - step if way == 0 else self.at.z - last + step

    def sends(self, way, step):
        last = self.at.chain - 1
        return self.at.z <= step if way == 0 else self.at.z >= last - step

    def receives(self, way, step):
        last = self.at.chain - 1
        if way == 0:
            return (self.at.z >= 1) & (self.at.z <= step + 1)
        return (self.at.z < last) & (self.at.z >= last - step - 1)

    def ends(self, step, part):
        @pl.when(self.at.z == 0)
        def _():
            self.copy(0, self.slab_of(0, step), step, part).start()

        @pl.when(self.at.z == self.at.chain - 1)
        def _():
            self.copy(1, self.slab_of(1, step), step, part).start()

    def landed(self, way, step, part):
        return pltpu.make_async_copy(
            self.slots.at[way, step, pl.ds(part * self.height, self.height)],
            self.stage.at[way, pl.ds(0, self.height)],
            self.local.at[way],
        )

    def add(self, way, slab, step, part):
        self.landed(way, step, part).wait()
        tile = min(64, self.height)

        def body(i, carry):
            here = pl.ds(pl.multiple_of(i * tile, tile), tile)
            rows = pl.ds(pl.multiple_of(part * self.height + i * tile, tile), tile)
            total = self.slabs[slab, rows, :].astype(WIDE) + self.stage[way, here, :].astype(WIDE)
            self.slabs[slab, rows, :] = total.astype(LOW)
            return carry

        lax.fori_loop(0, self.height // tile, body, 0)

    def passes(self, way, step):
        inside = self.at.z > 0 if way == 0 else self.at.z < self.at.chain - 1
        return self.sends(way, step) & inside

    def step(self, step, part):
        for way in (0, 1):

            @pl.when(self.passes(way, step))
            def _():
                self.copy(way, 0, step - 1, part).wait_recv()
                self.landed(way, step - 1, part).start()

        for way in (0, 1):

            @pl.when(self.passes(way, step))
            def _():
                slab = self.slab_of(way, step)
                self.add(way, slab, step - 1, part)
                self.copy(way, slab, step, part).start()

    def finish(self):
        last = self.at.chain - 2
        for part in range(PARTS):
            for way in (0, 1):

                @pl.when(self.receives(way, last))
                def _():
                    self.copy(way, 0, last, part).wait_recv()
                    self.landed(way, last, part).start()

            for way in (0, 1):

                @pl.when(self.receives(way, last))
                def _():
                    self.add(way, self.at.z, last, part)

    def sent(self):
        for step in range(self.at.chain - 1):
            for part in range(PARTS):
                for way in (0, 1):

                    @pl.when(self.sends(way, step))
                    def _():
                        self.copy(way, 0, step, part).wait_send()


def layer_kernel(
    size,
    tokens,
    cot,
    gain_one,
    gain_two,
    lens_in,
    w_query,
    w_key,
    w_value,
    w_out,
    w_gate,
    w_up,
    w_down,
    block_out,
    grad_tokens,
    grad_gains,
    g_query,
    g_key,
    g_value,
    g_out,
    g_gate,
    g_up,
    g_down,
    kept,
    slots,
    first,
    second,
    weights,
    qkv_weights,
    out_weights,
    grads,
    hidden,
    rows_two,
    turned,
    inner,
    units,
    sums_low,
    begun,
    qkv,
    attended,
    logs,
    table,
    head_sums,
    chain_stage,
    plane_stage,
    middle,
    total,
    last_stage,
    gain_rows,
    gains_in,
    lens,
    gain_parts,
    gain_peers,
    swap_sems,
    gather_send,
    gather_recv,
    reduce_send,
    reduce_recv,
    last_sems,
    plane_sems,
    first_sems,
    second_sems,
    small_sems,
    gain_sems,
    local_sems,
):
    chain, peers, rows, width, stages, unit, wide, seqs, tile = size
    at = Place(chain, peers)
    c, t, z = at.c, at.t, at.z
    group = rows * peers
    plane = 2 * group
    steps = chain - 1
    heads = wide // HEAD_DIM
    own_start = pl.multiple_of(c * group + t * rows, rows)
    query_tile = min(256, group)
    hub = min(256, unit)
    splits = PARTS if wide % (PARTS * LANES) == 0 else 1

    def slab_cols(s):
        return pl.ds(pl.multiple_of(s * 2 * unit, 2 * unit), 2 * unit)

    entry_barrier(at)

    def gain_copy(dp, source):
        place = gain_rows.at[:, pl.ds(pl.multiple_of(source * unit, unit), unit)]
        return remote(gains_in, place, gain_sems.at[0, dp], gain_sems.at[1, source], at.part(dp))

    own_gain = pltpu.make_async_copy(
        gains_in, gain_rows.at[:, pl.ds(pl.multiple_of(at.dp * unit, unit), unit)], local_sems.at[2]
    )

    def lens_copy(core):
        return remote(
            lens.at[core], lens.at[core], small_sems.at[0], small_sems.at[1], at.sibling()
        )

    lane = lax.broadcasted_iota(jnp.int32, (1, LANES), 1)
    gains_in[...] = jnp.zeros_like(gains_in)
    gains_in[0:1, :] = gain_one[...].astype(WIDE).reshape(1, unit)
    gains_in[1:2, :] = gain_two[...].astype(WIDE).reshape(1, unit)
    lens_row = jnp.zeros((8, LANES), WIDE)
    for s in range(seqs):
        lens_row = jnp.where(lane == s, lens_in[0, s].astype(WIDE), lens_row)
    lens[c] = lens_row

    def swap_copies(n):
        if n == 0:
            arrays = [(w, True, k * wide, wide, 0) for k, w in enumerate((w_query, w_key, w_value))]
            slab, down = qkv_weights.at[z], 0
        elif n == 1:
            arrays = [(w_out, False, 0, wide, 0)]
            slab, down = out_weights.at[z], 0
        else:
            arrays = [(w_gate, True, 0, unit, n - 2), (w_up, True, unit, unit, n - 2)]
            arrays.append((w_down, False, 0, unit, n - 2))
            slab, down = weights.at[n - 2, z], 2 * unit
        copies = []
        mine = pl.multiple_of(c * unit, unit)
        for k, (array, tall, offset, extent, stage) in enumerate(arrays):

            def half(core):
                count = (array.shape[1] if tall else array.shape[0]) // 2
                piece = pl.ds(pl.multiple_of(core * count + stage * extent, extent), extent)
                return array.at[:, piece] if tall else array.at[piece, :]

            if tall:
                place = slab.at[pl.ds(mine, unit), pl.ds(offset, extent)]
            else:
                place = slab.at[pl.ds(down, extent), pl.ds(mine, unit)]
            keep = pltpu.make_async_copy(half(c), place, swap_sems.at[0, n, k])
            give = remote(
                half(1 - c), place, swap_sems.at[1, n, k], swap_sems.at[2, n, k], at.sibling()
            )
            copies.append((keep, give))
        return copies

    def swapped(n):
        for keep, give in swap_copies(n):
            keep.wait()
            give.wait()

    for keep, give in swap_copies(0):
        keep.start()
        give.start()
    for dp in at.other_parts():
        gain_copy(dp, at.dp).start()
    own_gain.start()
    lens_copy(c).start()
    for n in range(1, stages + 2):
        for keep, give in swap_copies(n):
            keep.start()
            give.start()

    slabs = [qkv_weights, out_weights] + [weights.at[q] for q in range(stages)]
    stream = Stream(
        [
            ChainGather(at, ref, gather_send.at[n], gather_recv.at[n])
            for n, ref in enumerate(slabs)
        ],
        swapped,
    )
    gathers = [
        PlaneGather(at, full, rows, [plane_sems.at[n, k] for k in range(4)])
        for n, full in enumerate((hidden, rows_two, hidden, rows_two))
    ]
    plane_sums = [
        PlaneReduce(
            at,
            rows,
            tile,
            buffer,
            first.at[n],
            second.at[n],
            plane_stage,
            [first_sems.at[n, 0], first_sems.at[n, 1], second_sems.at[n, 0], second_sems.at[n, 1]],
            local_sems.at[4],
        )
        for n, buffer in enumerate((sums_low, sums_low, begun, sums_low))
    ]
    chain_sums = [
        ChainReduce(
            at,
            ref,
            height,
            slots.at[n],
            reduce_send.at[n],
            reduce_recv.at[n],
            chain_stage,
            local_sems,
        )
        for n, (ref, height) in enumerate(
            [(grads.at[q], 3 * unit) for q in range(stages)]
            + [(weights.at[0], 3 * wide), (weights.at[1], wide)]
        )
    ]
    sum_qkv, sum_out = chain_sums[stages], chain_sums[stages + 1]

    stream.go(2)

    for dp in at.other_parts():
        gain_copy(at.dp, dp).wait_recv()
    own_gain.wait()

    def strips(body):
        def each(i, carry):
            here = pl.ds(pl.multiple_of(i * STRIP, STRIP), STRIP)
            there = pl.ds(pl.multiple_of(own_start + i * STRIP, STRIP), STRIP)
            body(here, there)
            return carry

        lax.fori_loop(0, rows // STRIP, each, 0)

    def factor_of(values):
        return lax.rsqrt(jnp.mean(values * values, axis=-1, keepdims=True) + EPSILON)

    def first_norm(here, there):
        values = tokens[here, :].astype(WIDE)
        hidden[there, :] = (values * factor_of(values) * gain_rows[0:1, :]).astype(LOW)

    strips(first_norm)
    gathers[0].start()

    lens_copy(c).wait_send()
    lens_copy(1 - c).wait_recv()
    frequency = jnp.exp(lax.rem(lane, HALF).astype(WIDE) * (-2.0 * math.log(ROPE_BASE) / HEAD_DIM))
    side = jnp.where(lax.rem(lane, HEAD_DIM) < HALF, -1.0, 1.0)

    def table_rows(core):
        def body(i, carry):
            shape = (rows, LANES)
            row = (lax.broadcasted_iota(jnp.int32, shape, 0) + i * rows).astype(WIDE)
            start = jnp.zeros((1, 1), WIDE)
            base = jnp.zeros(shape, WIDE)
            valid = jnp.zeros(shape, WIDE)
            for s in range(seqs):
                length = lens[core, 0:1, s : s + 1]
                inside = (row >= start) & (row < start + length)
                base = jnp.where(inside, start, base)
                valid = jnp.where(inside, 1.0, valid)
                start = start + jnp.floor((length + (BLOCK - 1.0)) * (1.0 / BLOCK)) * BLOCK
            angle = (row - base) * frequency
            lowest = jnp.where(valid > 0.5, base, row)
            here = pl.ds(pl.multiple_of(core * group + i * rows, rows), rows)
            table[0, here, :] = jnp.cos(angle)
            table[1, here, :] = jnp.sin(angle) * side
            table[2, here, :] = jnp.where(lane == 0, lowest, valid)
            return carry

        lax.fori_loop(0, peers, body, 0)

    table_rows(0)
    table_rows(1)
    stream.go(2)

    def own_cotangent(here, there):
        rows_two[there, :] = (cot[here, :].astype(WIDE) * table[2, there, 1:2]).astype(LOW)

    strips(own_cotangent)
    gathers[0].forward()
    gathers[1].start()
    stream.go(1)
    gathers[0].finish()
    stream.complete(0)

    first_half = lax.rem(lax.broadcasted_iota(jnp.int32, (1, LANES), 1), HEAD_DIM) < HALF

    def swap_halves(values):
        return jnp.where(
            first_half, pltpu.roll(values, LANES - HALF, 1), pltpu.roll(values, HALF, 1)
        )

    def rotated(values, there, sign):
        pieces = []
        for n in range(0, values.shape[1], LANES):
            piece = values[:, n : n + LANES]
            pieces.append(
                piece * table[0, there, :] + sign * (swap_halves(piece) * table[1, there, :])
            )
        return jnp.concatenate(pieces, axis=1) if len(pieces) > 1 else pieces[0]

    def project(i, carry):
        here = pl.ds(pl.multiple_of(i * tile, tile), tile)
        sums = jnp.zeros((tile, 3 * wide), WIDE)
        for s in range(chain):
            sums += dot_nn(hidden[here, s * 2 * unit : (s + 1) * 2 * unit], qkv_weights[s])
        qkv[0, here, :] = rotated(sums[:, :wide], here, 1.0).astype(LOW)
        qkv[1, here, :] = rotated(sums[:, wide : 2 * wide], here, 1.0).astype(LOW)
        qkv[2, here, :] = sums[:, 2 * wide :].astype(LOW)
        return carry

    lax.fori_loop(0, plane // tile, project, 0)
    keep_rows = pltpu.make_async_copy(hidden, kept, local_sems.at[5])
    keep_rows.start()
    stream.go(2)
    gathers[1].forward()

    head_lane = lax.div(lax.broadcasted_iota(jnp.int32, (1, wide), 1), HEAD_DIM)

    def masked(scores, here, offset):
        column = lax.broadcasted_iota(jnp.int32, scores.shape, 1)
        row = lax.broadcasted_iota(jnp.int32, scores.shape, 0) + offset
        lowest = table[2, here, 0:1].astype(jnp.int32)
        return jnp.where((column >= lowest) & (column <= row), scores, MASKED)

    def attend(core, low, high):
        base = pl.multiple_of(core * group, group)

        def body(h, carry):
            lanes = jnp.where(head_lane == h, 1.0, 0.0)
            for b in range(group // query_tile):
                here = pl.ds(pl.multiple_of(base + b * query_tile, query_tile), query_tile)
                keys = pl.ds(base, (b + 1) * query_tile)
                query = (qkv[0, here, :].astype(WIDE) * (lanes * SCALE)).astype(LOW)
                scores = masked(dot_nt(query, qkv[1, keys, :]), here, b * query_tile)
                peak = jnp.max(scores, axis=-1, keepdims=True)
                exponent = jnp.exp(scores - peak)
                sums = jnp.sum(exponent, axis=-1, keepdims=True)
                weight = (exponent / sums).astype(LOW)
                mixed = dot_nn(weight, qkv[2, keys, :]) * lanes
                place = slice(b * query_tile, (b + 1) * query_tile)
                earlier = jnp.where(h == 0, 0.0, head_sums[0, place, :])
                head_sums[0, place, :] = earlier + mixed
                logs[here, :] = jnp.where(lane == h, peak + jnp.log(sums), logs[here, :])
            return carry

        if low == 0:
            logs[pl.ds(base, group), :] = jnp.zeros((group, LANES), WIDE)
            head_sums[0] = jnp.zeros((group, wide), WIDE)
        lax.fori_loop(low, high, body, 0)
        if high == heads:
            attended[pl.ds(base, group), :] = head_sums[0].astype(LOW)

    middle_head = heads // 2
    attend(1 - c, 0, middle_head)
    stream.go(2)
    attend(1 - c, middle_head, heads)
    keep_rows.wait()
    stream.complete(1)

    def product_tile(terms):
        def compute(source, out, extras):
            def body(s, carry):
                cols = slab_cols(s)
                sums = terms(source, s)
                for extra in extras:
                    sums += extra[:, cols].astype(WIDE)
                out[:, cols] = sums.astype(LOW)
                return carry

            lax.fori_loop(0, chain, body, 0)

        return compute

    out_tile = product_tile(lambda source, s: dot_nn(attended[source, :], out_weights[s]))
    plane_sums[0].half(out_tile)
    attend(c, 0, heads)
    stream.go(1)
    plane_sums[0].rest(out_tile)
    gathers[1].finish()
    stream.go(3)
    plane_sums[0].finish(total)

    def second_norm(here, there):
        values = tokens[here, :].astype(WIDE) + total[here, :] * table[2, there, 1:2]
        middle[here, :] = values
        hidden[there, :] = (values * factor_of(values) * gain_rows[1:2, :]).astype(LOW)

    strips(second_norm)
    gathers[2].start()
    stream.go(2)
    gathers[2].forward()
    plane_sums[0].sent()
    stream.go(1)
    gathers[2].finish()

    def hidden_units(q):
        def body(i, carry):
            these = pl.ds(pl.multiple_of(i * tile, tile), tile)
            gate_up = jnp.zeros((tile, 2 * unit), WIDE)
            grad_inner = jnp.zeros((tile, unit), WIDE)
            for s in range(chain):
                cols = slice(s * 2 * unit, (s + 1) * 2 * unit)
                gate_up += dot_nn(hidden[these, cols], weights[q, s, 0 : 2 * unit, :])
                grad_inner += dot_nt(rows_two[these, cols], weights[q, s, 2 * unit :, :])
            gate, up = gate_up[:, :unit], gate_up[:, unit:]
            sigmoid_gate = jax.nn.sigmoid(gate)
            inner[q, these, :] = (gate * sigmoid_gate * up).astype(LOW)
            units[q, these, 0:unit] = (
                grad_inner * up * sigmoid_gate * (1.0 + gate * (1.0 - sigmoid_gate))
            ).astype(LOW)
            units[q, these, unit : 2 * unit] = (grad_inner * gate * sigmoid_gate).astype(LOW)
            return carry

        lax.fori_loop(0, plane // tile, body, 0)

    eye = identity(hub)

    def turn_into(start, source):
        extent = min(hub, source.shape[1])

        def body(i, carry):
            cols = pl.ds(pl.multiple_of(i * extent, extent), extent)
            place = pl.ds(pl.multiple_of(start + i * extent, extent), extent)
            turned[place, :] = dot_nt(eye[:extent, :extent], source[:, cols]).astype(LOW)
            return carry

        lax.fori_loop(0, source.shape[1] // extent, body, 0)

    def in_grads(q):
        turn_into(0, units.at[q])

        def body(s, carry):
            grads[q, s, 0 : 2 * unit, :] = dot_nn(
                turned[0 : 2 * unit, :], hidden[:, slab_cols(s)]
            ).astype(LOW)
            return carry

        lax.fori_loop(0, chain, body, 0)

    def down_grads(q):
        turn_into(2 * unit, inner.at[q])

        def body(s, carry):
            grads[q, s, 2 * unit :, :] = dot_nn(
                turned[2 * unit :, :], rows_two[:, slab_cols(s)]
            ).astype(LOW)
            return carry

        lax.fori_loop(0, chain, body, 0)

    def hidden_sums(stage_list):
        return product_tile(
            lambda source, s: sum(
                dot_nt(units[q, source, :], weights[q, s, 0 : 2 * unit, :]) for q in stage_list
            )
        )

    def begin_hidden():
        begin = hidden_sums(range(stages - 1))
        for i in range(group // tile):
            here = pl.ds(i * tile, tile)
            begin(plane_sums[1].source(1 - c, i), sums_low.at[here], [])
            begin(plane_sums[1].source(c, i), begun.at[here], [])

    for q in range(stages):
        stream.complete(q + 2)
        hidden_units(q)
        if q == stages - 1:
            break
        stream.go(1)
        in_grads(q)
        down_grads(q)
        for part in range(PARTS):
            chain_sums[q].ends(0, part)
        stream.go(1)
        for k in range(1, steps):
            for part in range(PARTS):
                stream.go(1)
                chain_sums[q].ends(k, part)
                if k > 1:
                    chain_sums[q].step(k - 1, part)
                if q == stages - 2 and (k, part) == (1, 0):
                    begin_hidden()
        if q == stages - 2 and steps == 1:
            begin_hidden()

    branch_tile = product_tile(
        lambda source, s: sum(
            dot_nn(inner[q, source, :], weights[q, s, 2 * unit :, :]) for q in range(stages)
        )
    )

    def chain_steps(n, low, high):
        for k in range(max(low, 1), high):
            for part in range(PARTS):
                chain_sums[n].step(k, part)

    def last_step(n):
        chain_steps(n, steps - 1, steps)

    def placed(n, core, source):
        own = chain_sums[n].slabs.at[z]
        cols = pl.ds(pl.multiple_of(core * unit, unit), unit)
        stage = last_stage.at[n % 2, core]
        if n < stages:
            place = pl.ds(pl.multiple_of((source * stages + n) * unit, unit), unit)
            return [
                (stage.at[0, :, pl.ds(0, unit)], g_gate.at[:, place]),
                (stage.at[1, :, pl.ds(0, unit)], g_up.at[:, place]),
                (own.at[pl.ds(2 * unit, unit), cols], g_down.at[place, :]),
            ]
        place = pl.ds(pl.multiple_of(source * wide, wide), wide)
        if n == stages:
            return [
                (stage.at[k, :, pl.ds(0, wide)], out.at[:, place])
                for k, out in enumerate((g_query, g_key, g_value))
            ]
        return [(own.at[pl.ds(0, wide), cols], g_out.at[place, :])]

    def last_copies(n):
        copies = []
        for k, ((mine, place), (theirs, _)) in enumerate(
            zip(placed(n, c, c), placed(n, 1 - c, c))
        ):
            keep = pltpu.make_async_copy(mine, place, last_sems.at[0, n, k])
            give = remote(theirs, place, last_sems.at[1, n, k], last_sems.at[2, n, k], at.sibling())
            copies.append((keep, give))
        return copies

    def finish_sum(n):
        chain_sums[n].finish()
        own = chain_sums[n].slabs
        pieces = []
        if n < stages:
            pieces = [(k, k * unit, 0, unit) for k in range(2)]
        elif n == stages:
            lanes = wide // splits
            pieces = [
                (k, (m * 3 + k) * lanes, m * lanes, lanes) for m in range(splits) for k in range(3)
            ]
        for core in (0, 1):
            for k, start, place, extent in pieces:
                piece = own[z, start : start + extent, core * unit : (core + 1) * unit]
                last_stage[n % 2, core, k, :, place : place + extent] = turn(piece, eye)
        for keep, give in last_copies(n):
            keep.start()
            give.start()

    def settle(n):
        for keep, give in last_copies(n):
            keep.wait()
            give.wait()
        chain_sums[n].sent()

    down_grads(stages - 1)
    last_tile = hidden_sums([stages - 1])
    plane_sums[1].half(last_tile, begun=True)
    plane_sums[1].rest(last_tile, begun=begun)
    early = list(range(stages - 1))
    for q in early[-1:] + early[:-1]:
        last_step(q)
    in_grads(stages - 1)
    for k in range(steps):
        for part in range(PARTS):
            chain_sums[stages - 1].ends(k, part)
    plane_sums[2].half(branch_tile)
    bring_rows = pltpu.make_async_copy(kept, hidden, local_sems.at[5])
    bring_rows.start()
    plane_sums[1].finish(total)

    def second_back(here, there):
        values = middle[here, :]
        factor = factor_of(values)
        normed = values * factor
        grad = total[here, :]
        gain_parts[1:2, :] += jnp.sum(grad * normed, axis=0, keepdims=True)
        scaled = grad * gain_rows[1:2, :]
        mean = jnp.mean(scaled * normed, axis=-1, keepdims=True)
        result = cot[here, :].astype(WIDE) + factor * (scaled - normed * mean)
        grad_tokens[here, :] = result
        rows_two[there, :] = (result * table[2, there, 1:2]).astype(LOW)

    gain_parts[...] = jnp.zeros_like(gain_parts)
    strips(second_back)
    gathers[3].start()
    plane_sums[1].sent()
    for chain_gather in stream.chains:
        chain_gather.sent()
    plane_sums[2].rest(branch_tile)
    finish_sum(0)
    chain_steps(stages - 1, 1, steps - 1)
    if stages > 3:
        settle(0)
        finish_sum(2)
    if stages > 2:
        finish_sum(1)
    gathers[3].forward()
    gathers[3].finish()

    def finish_branch():
        plane_sums[2].finish(total)

        def last_rows(here, there):
            result = middle[here, :] + total[here, :] * table[2, there, 1:2]
            block_out[here, :] = result.astype(LOW)

        strips(last_rows)

    grad_attended = inner.at[0]

    def attended_grad(i, carry):
        here = pl.ds(pl.multiple_of(i * tile, tile), tile)
        sums = jnp.zeros((tile, wide), WIDE)
        for s in range(chain):
            sums += dot_nt(rows_two[here, s * 2 * unit : (s + 1) * 2 * unit], out_weights[s])
        grad_attended[here, :] = sums.astype(LOW)
        return carry

    turn_into(0, attended)

    def out_grads(s, carry):
        weights[1, s, 0:wide, :] = dot_nn(turned[0:wide, :], rows_two[:, slab_cols(s)]).astype(LOW)
        return carry

    lax.fori_loop(0, chain, out_grads, 0)
    for k in range(steps):
        for part in range(PARTS):
            sum_out.ends(k, part)
    lax.fori_loop(0, plane // tile, attended_grad, 0)

    def attend_back(core, low, high):
        base = core * group

        def body(h, carry):
            lanes = jnp.where(head_lane == h, 1.0, 0.0)
            lanes_low = lanes.astype(LOW)
            for b in range(group // query_tile):
                here = slice(base + b * query_tile, base + (b + 1) * query_tile)
                keys = slice(base, base + (b + 1) * query_tile)
                place = slice(b * query_tile, (b + 1) * query_tile)
                reach = slice(0, (b + 1) * query_tile)
                query = qkv[0, here, :] * lanes_low
                grad = grad_attended[here, :] * lanes_low
                scores = masked(dot_nt(query, qkv[1, keys, :]) * SCALE, here, b * query_tile)
                log_total = jnp.sum(
                    jnp.where(lane == h, logs[here, :], 0.0), axis=-1, keepdims=True
                )
                probs = jnp.exp(scores - log_total)
                grad_probs = dot_nt(grad, qkv[2, keys, :])
                shift = jnp.sum(probs * grad_probs, axis=-1, keepdims=True)
                grad_scores = (probs * (grad_probs - shift) * SCALE).astype(LOW)
                head_sums[0, place, :] += dot_nn(grad_scores, qkv[1, keys, :]) * lanes
                head_sums[1, reach, :] += dot_nn(turn(grad_scores, eye), query)
                head_sums[2, reach, :] += dot_nn(turn(probs.astype(LOW), eye), grad)
            return carry

        for k in range(3):
            head_sums[k] = jnp.zeros((group, wide), WIDE)
        lax.fori_loop(low, high, body, 0)
        lanes = slice(low * HEAD_DIM, high * HEAD_DIM)

        def back(i, carry):
            there = pl.ds(pl.multiple_of(base + i * query_tile, query_tile), query_tile)
            here = pl.ds(pl.multiple_of(i * query_tile, query_tile), query_tile)
            for k in range(2):
                values = rotated(head_sums[k, here, lanes], there, -1.0)
                units[0, there, k * wide + lanes.start : k * wide + lanes.stop] = values.astype(LOW)
            units[1, there, lanes] = head_sums[2, here, lanes].astype(LOW)
            return carry

        lax.fori_loop(0, group // query_tile, back, 0)

    def qkv_grads(n):
        lanes = wide // splits
        turn_into(0, units.at[0, :, pl.ds(n * lanes, lanes)])
        turn_into(lanes, units.at[0, :, pl.ds(wide + n * lanes, lanes)])
        turn_into(2 * lanes, units.at[1, :, pl.ds(n * lanes, lanes)])

        parts = range(n * PARTS // splits, (n + 1) * PARTS // splits)
        for k in range(chain):
            s = jnp.where(at.z < (chain + 1) // 2, chain - 1 - k, k)
            weights[0, s, n * 3 * lanes : (n + 1) * 3 * lanes, :] = dot_nn(
                turned[0 : 3 * lanes, :], hidden[:, slab_cols(s)]
            ).astype(LOW)
            if k < steps:
                for part in parts:
                    sum_qkv.ends(k, part)

    for n in range(splits):
        low, high = n * heads // splits, (n + 1) * heads // splits
        attend_back(0, low, high)
        if n == 0:
            last_step(stages - 1)
        attend_back(1, low, high)
        if n == 0:
            bring_rows.wait()
        qkv_grads(n)

    first_tile = product_tile(
        lambda source, s: dot_nt(units[0, source, :], qkv_weights[s, :, 0 : 2 * wide])
        + dot_nt(units[1, source, 0:wide], qkv_weights[s, :, 2 * wide :])
    )
    chain_steps(stages + 1, 1, steps - 1)
    plane_sums[3].half(first_tile)
    plane_sums[3].rest(first_tile)

    def qkv_steps(part, low, high):
        for k in range(max(low, 1), high):
            sum_qkv.step(k, part)

    qkv_steps(0, 1, steps - 1)
    if stages > 2:
        settle(stages - 3)
    finish_sum(stages - 1)
    last_step(stages + 1)
    qkv_steps(0, steps - 1, steps)
    finish_branch()
    for part in range(1, PARTS):
        qkv_steps(part, 1, steps - 1)
    finish_sum(stages + 1)
    for part in range(1, PARTS):
        qkv_steps(part, steps - 1, steps)
    plane_sums[3].finish(total)

    def first_back(here, there):
        values = tokens[here, :].astype(WIDE)
        factor = factor_of(values)
        normed = values * factor
        grad = total[here, :]
        gain_parts[0:1, :] += jnp.sum(grad * normed, axis=0, keepdims=True)
        scaled = grad * gain_rows[0:1, :]
        mean = jnp.mean(scaled * normed, axis=-1, keepdims=True)
        grad_tokens[here, :] += factor * (scaled - normed * mean)

    strips(first_back)

    own_cols = pl.ds(pl.multiple_of(at.dp * unit, unit), unit)

    def gain_sum_copy(dp, source):
        cols = pl.ds(pl.multiple_of(dp * unit, unit), unit)
        return remote(
            gain_parts.at[:, cols],
            gain_peers.at[source],
            gain_sems.at[2, dp],
            gain_sems.at[3, source],
            at.part(dp),
        )

    def gain_peer_copy(peer, source):
        parts = 2 * chain
        return remote(
            gain_peers.at[parts + t],
            gain_peers.at[parts + source],
            gain_sems.at[4, peer],
            gain_sems.at[5, source],
            at.peer(peer),
        )

    for dp in at.other_parts():
        gain_sum_copy(dp, at.dp).start()
    settle(stages - 2)
    sums = gain_parts[:, own_cols]
    for dp in at.other_parts():
        gain_sum_copy(at.dp, dp).wait_recv()
        sums += gain_peers[dp]
    gain_peers[2 * chain + t] = sums
    for peer in at.other_peers():
        gain_peer_copy(peer, t).start()
    for peer in at.other_peers():
        gain_peer_copy(t, peer).wait_recv()
        sums += gain_peers[2 * chain + peer]
    grad_gains[...] = sums
    settle(stages - 1)
    finish_sum(stages)
    settle(stages)
    settle(stages + 1)
    plane_sums[2].sent()
    plane_sums[3].sent()
    for dp in at.other_parts():
        gain_copy(dp, at.dp).wait_send()
        gain_sum_copy(dp, at.dp).wait_send()
    for peer in at.other_peers():
        gain_peer_copy(peer, t).wait_send()


def finish_kernel(*refs):
    count = len(refs) // 2
    sources, outs = refs[:count], refs[count:]
    for source, out in zip(sources[:2] + sources[3:], outs[: count - 1]):
        out[...] = source[...].astype(out.dtype)
    outs[count - 1][...] = sources[2][0:1, :]
    outs[count][...] = sources[2][1:2, :]


def finish(arrays):
    steps = 4
    gains = arrays[2]

    def split(array):
        return pl.BlockSpec((array.shape[0] // steps, array.shape[1]), lambda i: (i, 0))

    whole = pl.BlockSpec(gains.shape, lambda i: (0, 0))
    row = pl.BlockSpec((1, gains.shape[1]), lambda i: (0, 0))
    kept = arrays[:2] + arrays[3:]
    dtypes = [array.dtype for array in arrays[:2]] + [WIDE] * len(arrays[3:])
    return pl.pallas_call(
        finish_kernel,
        grid=(steps,),
        out_shape=[jax.ShapeDtypeStruct(a.shape, d) for a, d in zip(kept, dtypes)]
        + [jax.ShapeDtypeStruct((1, gains.shape[1]), WIDE)] * 2,
        in_specs=[split(a) for a in arrays[:2]] + [whole] + [split(a) for a in arrays[3:]],
        out_specs=[split(a) for a in kept] + [row] * 2,
        compiler_params=pltpu.CompilerParams(vmem_limit_bytes=VMEM_BYTES),
        name="finish",
    )(*arrays)


def on_device(
    tokens_in,
    seq_lens,
    w_query,
    w_key,
    w_value,
    w_out,
    norm1_gain,
    w_gate,
    w_up,
    w_down,
    norm2_gain,
    out_cotangent,
):
    n_dp, peers = lax.axis_size("dp"), lax.axis_size("tensor")
    chain = n_dp // 2
    rows, width = tokens_in.shape
    unit = width // n_dp
    wide = w_query.shape[1] // 2
    stages = w_gate.shape[1] // 2 // unit
    seqs = seq_lens.shape[1]
    group = rows * peers
    plane = 2 * group
    tile = min(256, group)
    slab = (3 * unit, 2 * unit)
    size = (chain, peers, rows, width, stages, unit, wide, seqs, tile)
    hbm = pl.BlockSpec(memory_space=pl.ANY)
    vmem = pl.BlockSpec(memory_space=pltpu.VMEM)
    smem = pl.BlockSpec(memory_space=pltpu.SMEM)
    dma = pltpu.SemaphoreType.DMA

    def like(array):
        return jax.ShapeDtypeStruct(array.shape, LOW)

    outs = pl.pallas_call(
        functools.partial(layer_kernel, size),
        out_shape=(
            jax.ShapeDtypeStruct((rows, width), LOW),
            jax.ShapeDtypeStruct((rows, width), WIDE),
            jax.ShapeDtypeStruct((8, unit), WIDE),
            like(w_query),
            like(w_key),
            like(w_value),
            like(w_out),
            like(w_gate),
            like(w_up),
            like(w_down),
            jax.ShapeDtypeStruct((plane, width), LOW),
            jax.ShapeDtypeStruct((stages + 2, 2, chain - 1) + slab, LOW),
            jax.ShapeDtypeStruct((4, group, width), LOW),
            jax.ShapeDtypeStruct((4, peers, rows, width), LOW),
        ),
        in_specs=[vmem, vmem, vmem, vmem, smem] + [hbm] * 7,
        out_specs=(vmem, vmem, vmem) + (hbm,) * 11,
        scratch_shapes=[
            pltpu.VMEM((stages, chain) + slab, LOW),
            pltpu.VMEM((chain, 2 * unit, 3 * wide), LOW),
            pltpu.VMEM((chain, wide, 2 * unit), LOW),
            pltpu.VMEM((stages, chain) + slab, LOW),
            pltpu.VMEM((plane, width), LOW),
            pltpu.VMEM((plane, width), LOW),
            pltpu.VMEM((3 * unit, plane), LOW),
            pltpu.VMEM((stages, plane, unit), LOW),
            pltpu.VMEM((stages, plane, 2 * unit), LOW),
            pltpu.VMEM((group, width), LOW),
            pltpu.VMEM((group, width), LOW),
            pltpu.VMEM((3, plane, wide), LOW),
            pltpu.VMEM((plane, wide), LOW),
            pltpu.VMEM((plane, LANES), WIDE),
            pltpu.VMEM((3, plane, LANES), WIDE),
            pltpu.VMEM((3, group, wide), WIDE),
            pltpu.VMEM((2, slab[0] // PARTS, slab[1]), LOW),
            pltpu.VMEM((tile, width), LOW),
            pltpu.VMEM((rows, width), WIDE),
            pltpu.VMEM((rows, width), WIDE),
            pltpu.VMEM((2, 2, 3, unit, max(unit, wide)), LOW),
            pltpu.VMEM((8, width), WIDE),
            pltpu.VMEM((8, unit), WIDE),
            pltpu.VMEM((2, 8, LANES), WIDE),
            pltpu.VMEM((8, width), WIDE),
            pltpu.VMEM((n_dp + peers, 8, unit), WIDE),
            dma((3, stages + 2, 3)),
            dma((stages + 2, 2, chain - 1, PARTS)),
            dma((stages + 2, 2, chain - 1, PARTS)),
            dma((stages + 2, 2, chain - 1, PARTS)),
            dma((stages + 2, 2, chain - 1, PARTS)),
            dma((3, stages + 2, 3)),
            dma((4, 4, peers)),
            dma((4, 2, group // tile)),
            dma((4, 2, peers)),
            dma((2,)),
            dma((6, n_dp)),
            dma((6,)),
        ],
        compiler_params=pltpu.CompilerParams(
            collective_id=0, has_side_effects=True, vmem_limit_bytes=VMEM_BYTES
        ),
        cost_estimate=pl.CostEstimate(
            flops=6 * plane * width * (4 * wide + 3 * unit * stages),
            bytes_accessed=16 * width * (4 * wide + 3 * unit * stages),
            transcendentals=0,
        ),
        name="layer",
    )(
        tokens_in,
        out_cotangent,
        norm1_gain,
        norm2_gain,
        seq_lens,
        w_query,
        w_key,
        w_value,
        w_out,
        w_gate,
        w_up,
        w_down,
    )
    block_out, grad_tokens, *weight_grads, gain_one, gain_two = finish(outs[:10])
    return (
        block_out,
        grad_tokens,
        *weight_grads[:4],
        gain_one.reshape(unit),
        *weight_grads[4:],
        gain_two.reshape(unit),
    )


def solution(mesh):
    return jax.shard_map(
        on_device,
        mesh=mesh,
        in_specs=(
            P(("dp", "tensor"), None),
            P("dp", None),
            P("dp", "tensor"),
            P("dp", "tensor"),
            P("dp", "tensor"),
            P("tensor", "dp"),
            P("dp"),
            P("dp", "tensor"),
            P("dp", "tensor"),
            P("tensor", "dp"),
            P("dp"),
            P(("dp", "tensor"), None),
        ),
        out_specs=(
            P(("dp", "tensor"), None),
            P(("dp", "tensor"), None),
            P("dp", "tensor"),
            P("dp", "tensor"),
            P("dp", "tensor"),
            P("tensor", "dp"),
            P("dp"),
            P("dp", "tensor"),
            P("dp", "tensor"),
            P("tensor", "dp"),
            P("dp"),
        ),
        check_vma=False,
    )
```

```python
import functools
import math

import jax
import jax.numpy as jnp
from jax import lax
from jax.experimental import pallas as pl
from jax.experimental.pallas import tpu as pltpu
from jax.sharding import PartitionSpec as P

HEAD_DIM = 64
HALF = HEAD_DIM // 2
BLOCK = 128
LANES = 128
EPSILON = 1e-05
ROPE_BASE = 130000.0
MASKED = -1e30
SCALE = HEAD_DIM ** (-0.5)

LOW = jnp.bfloat16
WIDE = jnp.float32
VMEM_BYTES = 64 * 1024 * 1024
PARTS = 2
STRIP = 32


def dot_nn(left, right):
    return lax.dot_general(left, right, (((1,), (0,)), ((), ())), preferred_element_type=WIDE)


def dot_nt(left, right):
    return lax.dot_general(left, right, (((1,), (1,)), ((), ())), preferred_element_type=WIDE)


def identity(size):
    across = lax.broadcasted_iota(jnp.int32, (size, size), 0)
    down = lax.broadcasted_iota(jnp.int32, (size, size), 1)
    return jnp.where(across == down, 1.0, 0.0).astype(LOW)


def turn(values, eye):
    size = eye.shape[0]
    width = values.shape[1]
    if width <= size:
        return dot_nt(eye[:width, :width], values).astype(LOW)
    blocks = [dot_nt(eye, values[:, n : n + size]).astype(LOW) for n in range(0, width, size)]
    return jnp.concatenate(blocks, axis=0)


class Place:
    def __init__(self, chain, peers):
        self.chain, self.peers = chain, peers
        self.dp = lax.axis_index("dp")
        self.t = lax.axis_index("tensor")
        self.c = lax.rem(self.dp, 2)
        self.z = lax.div(self.dp, 2)

    def sibling(self):
        return {"dp": self.dp + 1 - 2 * self.c, "tensor": self.t}

    def along(self, step):
        return {"dp": self.dp + 2 * step, "tensor": self.t}

    def part(self, dp):
        return {"dp": dp, "tensor": self.t}

    def peer(self, t):
        return {"dp": self.dp, "tensor": t}

    def other_peers(self):
        return [lax.rem(self.t + n, self.peers) for n in range(1, self.peers)]

    def other_parts(self):
        parts = 2 * self.chain
        return [lax.rem(self.dp + n, parts) for n in range(1, parts)]


def remote(src, dst, send, recv, device):
    return pltpu.make_async_remote_copy(
        src_ref=src,
        dst_ref=dst,
        send_sem=send,
        recv_sem=recv,
        device_id=device,
        device_id_type=pl.DeviceIdType.MESH,
    )


def fetch(src, dst, sem):
    copy = pltpu.make_async_copy(src, dst, sem)
    copy.start()
    copy.wait()


def entry_barrier(at):
    barrier = pltpu.get_barrier_semaphore()
    devices = [at.peer(t) for t in at.other_peers()] + [at.part(dp) for dp in at.other_parts()]
    for device in devices:
        pl.semaphore_signal(barrier, inc=1, device_id=device, device_id_type=pl.DeviceIdType.MESH)
    pl.semaphore_wait(barrier, len(devices))


class PlaneGather:
    def __init__(self, at, full, rows, sems):
        self.at, self.full, self.rows = at, full, rows
        self.group = rows * at.peers
        self.send, self.recv, self.pass_send, self.pass_recv = sems

    def block(self, c, t):
        start = pl.multiple_of(c * self.group + t * self.rows, self.rows)
        return self.full.at[pl.ds(start, self.rows)]

    def to_peer(self, t):
        at = self.at
        own = self.block(at.c, at.t)
        return remote(own, own, self.send.at[t], self.recv.at[at.t], at.peer(t))

    def from_peer(self, t):
        block = self.block(self.at.c, t)
        return remote(block, block, self.send.at[t], self.recv.at[t], self.at.peer(t))

    def to_sibling(self, t):
        block = self.block(self.at.c, t)
        return remote(
            block, block, self.pass_send.at[t], self.pass_recv.at[t], self.at.sibling()
        )

    def from_sibling(self, t):
        block = self.block(1 - self.at.c, t)
        return remote(
            block, block, self.pass_send.at[t], self.pass_recv.at[t], self.at.sibling()
        )

    def start(self):
        for t in self.at.other_peers():
            self.to_peer(t).start()
        self.to_sibling(self.at.t).start()

    def forward(self):
        for t in self.at.other_peers():
            self.from_peer(t).wait_recv()
            self.to_sibling(t).start()

    def finish(self):
        for t in range(self.at.peers):
            self.from_sibling(t).wait_recv()
        for t in self.at.other_peers():
            self.to_peer(t).wait_send()
        for t in range(self.at.peers):
            self.to_sibling(t).wait_send()


class PlaneReduce:
    def __init__(self, at, rows, tile, buffer, first, second, stage, sems, local):
        self.at, self.rows, self.tile, self.buffer = at, rows, tile, buffer
        self.group = rows * at.peers
        self.first, self.second, self.stage, self.local = first, second, stage, local
        self.send1, self.recv1, self.send2, self.recv2 = sems

    def source(self, c, i):
        return pl.ds(pl.multiple_of(c * self.group + i * self.tile, self.tile), self.tile)

    def to_sibling(self, i):
        here = pl.ds(i * self.tile, self.tile)
        return remote(
            self.buffer.at[here],
            self.first.at[here],
            self.send1.at[i],
            self.recv1.at[i],
            self.at.sibling(),
        )

    def to_peer(self, t, source):
        return remote(
            self.buffer.at[pl.ds(pl.multiple_of(t * self.rows, self.rows), self.rows)],
            self.second.at[source],
            self.send2.at[t],
            self.recv2.at[source],
            self.at.peer(t),
        )

    def half(self, compute, begun=False):
        for i in range(self.group // self.tile):
            out = self.buffer.at[pl.ds(i * self.tile, self.tile)]
            compute(self.source(1 - self.at.c, i), out, [out] if begun else [])
            self.to_sibling(i).start()

    def rest(self, compute, begun=None):
        at = self.at
        for i in range(self.group // self.tile):
            here = pl.ds(i * self.tile, self.tile)
            self.to_sibling(i).wait_recv()
            fetch(self.first.at[here], self.stage, self.local)
            self.to_sibling(i).wait_send()
            extras = [self.stage] if begun is None else [self.stage, begun.at[here]]
            compute(self.source(at.c, i), self.buffer.at[here], extras)
            self.send_rows(i)

    def send_rows(self, i):
        at = self.at
        for j in range(i * self.tile // self.rows, (i + 1) * self.tile // self.rows):

            @pl.when(at.t != j)
            def _():
                self.to_peer(j, at.t).start()

    def merge(self):
        pass

    def finish(self, out):
        at = self.at
        own = pl.ds(pl.multiple_of(at.t * self.rows, self.rows), self.rows)
        out[...] = self.buffer[own, :].astype(WIDE)
        for t in at.other_peers():
            self.to_peer(at.t, t).wait_recv()
            fetch(self.second.at[t], self.stage.at[pl.ds(0, self.rows)], self.local)
            out[...] += self.stage[0 : self.rows, :].astype(WIDE)

    def sent(self):
        for t in self.at.other_peers():
            self.to_peer(t, self.at.t).wait_send()


class SquareGather(PlaneGather):
    def neighbour(self, n):
        t = self.at.t
        return t + 1 - 2 * lax.rem(t, 2) if n == 0 else t + 2 - 4 * lax.div(t, 2)

    def part(self, t, n):
        half = self.rows // 2
        start = self.at.c * self.group + t * self.rows + n * half
        return self.full.at[pl.ds(pl.multiple_of(start, half), half)]

    def near(self, n, t):
        block = self.block(self.at.c, t)
        device = self.at.peer(self.neighbour(n))
        return remote(block, block, self.send.at[n], self.recv.at[n], device)

    def passed(self, n, t):
        ref = self.part(t, n)
        device = self.at.peer(self.neighbour(1 - n))
        return remote(ref, ref, self.send.at[2 + n], self.recv.at[2 + n], device)

    def start(self):
        for n in (0, 1):
            self.near(n, self.at.t).start()
        self.to_sibling(self.at.t).start()

    def forward(self):
        for n in (0, 1):
            t = self.neighbour(n)
            self.near(n, t).wait_recv()
            self.passed(n, t).start()
            self.to_sibling(t).start()
        for n in (0, 1):
            self.passed(n, 3 - self.at.t).wait_recv()
        self.to_sibling(3 - self.at.t).start()

    def finish(self):
        for t in range(self.at.peers):
            self.from_sibling(t).wait_recv()
        for n in (0, 1):
            self.near(n, self.at.t).wait_send()
            self.passed(n, self.neighbour(n)).wait_send()
        for t in range(self.at.peers):
            self.to_sibling(t).wait_send()


class SquareReduce(PlaneReduce):
    def neighbour(self, n):
        t = self.at.t
        return t + 1 - 2 * lax.rem(t, 2) if n == 0 else t + 2 - 4 * lax.div(t, 2)

    def part(self, t, n):
        half = self.rows // 2
        return pl.ds(pl.multiple_of(t * self.rows + n * half, half), half)

    def message(self, kind, n):
        half = self.rows // 2
        t = 3 - self.at.t if kind == 0 else self.neighbour(n)
        m = 1 - n if kind == 2 else n
        place = self.second.at[0 if kind == 0 else 1 + n, pl.ds(m * half, half)]
        sems = (self.send2.at[2 * kind + n], self.recv2.at[2 * kind + n])
        return remote(self.buffer.at[self.part(t, m)], place, *sems, self.at.peer(self.neighbour(n)))

    def send_rows(self, i):
        if (i + 1) * self.tile == self.group:
            for kind in (0, 1):
                for n in (0, 1):
                    self.message(kind, n).start()

    def merge(self):
        half = self.rows // 2
        for n in (0, 1):
            self.message(0, n).wait_recv()
            here = pl.ds(n * half, half)
            fetch(self.second.at[0, here], self.stage.at[here], self.local)
            rows = self.part(self.neighbour(1 - n), n)
            sums = self.buffer[rows, :].astype(WIDE)
            sums += self.stage[n * half : (n + 1) * half, :].astype(WIDE)
            self.buffer[rows, :] = sums.astype(LOW)
            self.message(2, 1 - n).start()

    def finish(self, out):
        own = pl.ds(pl.multiple_of(self.at.t * self.rows, self.rows), self.rows)
        out[...] = self.buffer[own, :].astype(WIDE)
        for n in (0, 1):
            self.message(1, n).wait_recv()
            self.message(2, n).wait_recv()
            fetch(self.second.at[1 + n], self.stage.at[pl.ds(0, self.rows)], self.local)
            out[...] += self.stage[0 : self.rows, :].astype(WIDE)

    def sent(self):
        for kind in range(3):
            for n in (0, 1):
                self.message(kind, n).wait_send()


class ChainGather:
    def __init__(self, at, slabs, send, recv):
        self.at, self.slabs, self.sems = at, slabs, (send, recv)
        self.height = slabs.shape[1] // PARTS

    def copy(self, way, slab, step, part):
        send, recv = self.sems
        ref = self.slabs.at[slab, pl.ds(part * self.height, self.height)]
        return remote(
            ref,
            ref,
            send.at[way, step, part],
            recv.at[way, step, part],
            self.at.along(1 - 2 * way),
        )

    def each_send(self, step, part, act):
        z, last = self.at.z, self.at.chain - 1

        @pl.when((z < last) & (z >= max(step, 1)))
        def _():
            act(self.copy(0, z - step, step, part))

        @pl.when((z > 0) & (z + step <= last) & (z + 1 - min(step, 1) <= last))
        def _():
            act(self.copy(1, z + step, step, part))

    def each_end(self, part, act):
        z, last = self.at.z, self.at.chain - 1

        @pl.when(z == 0)
        def _():
            act(self.copy(0, 0, 0, part))

        @pl.when(z == last)
        def _():
            act(self.copy(1, last, 0, part))

    def start(self, step, part):
        self.each_send(step, part, lambda copy: copy.start())

    def start_end(self, part):
        self.each_end(part, lambda copy: copy.start())

    def sent(self):
        for part in range(PARTS):
            self.each_end(part, lambda copy: copy.wait_send())
            for step in range(self.at.chain - 1):
                self.each_send(step, part, lambda copy: copy.wait_send())

    def arrived(self, step, part):
        z, last = self.at.z, self.at.chain - 1

        @pl.when(z - 1 - step >= 0)
        def _():
            self.copy(0, z - 1 - step, step, part).wait_recv()

        @pl.when(z + 1 + step <= last)
        def _():
            self.copy(1, z + 1 + step, step, part).wait_recv()


class Stream:
    def __init__(self, chains, swapped):
        self.chains, self.swapped = chains, swapped
        self.steps = chains[0].at.chain - 1
        self.messages = [
            (n, step, part)
            for n in range(len(chains))
            for step in range(self.steps)
            for part in range(PARTS)
        ]
        self.ends = [(n, part) for n in range(len(chains)) for part in range(PARTS)]
        self.next = 0
        self.ready = 0

    def need(self, n):
        while self.ready <= n:
            self.swapped(self.ready)
            self.ready += 1

    def go(self, count=1):
        for _ in range(count):
            done = self.next - PARTS
            if 0 <= done < len(self.messages):
                n, step, part = self.messages[done]
                self.chains[n].arrived(step, part)
            if self.next < len(self.messages):
                n, step, part = self.messages[self.next]
                self.need(n)
                self.chains[n].start(step, part)
            if self.next < len(self.ends):
                n, part = self.ends[self.next]
                self.need(n)
                self.chains[n].start_end(part)
            self.next += 1

    def complete(self, n):
        while self.next < (n + 1) * self.steps * PARTS + PARTS:
            self.go()


class ChainReduce:
    def __init__(self, at, slabs, height, slots, send, recv, stage, local):
        self.at, self.slabs, self.slots, self.sems = at, slabs, slots, (send, recv)
        self.stage, self.local = stage, local
        self.height = height // PARTS

    def copy(self, way, slab, step, part):
        send, recv = self.sems
        rows = pl.ds(part * self.height, self.height)
        return remote(
            self.slabs.at[slab, rows],
            self.slots.at[way, step, rows],
            send.at[way, step, part],
            recv.at[way, step, part],
            self.at.along(1 - 2 * way),
        )

    def slab_of(self, way, step):
        last = self.at.chain - 1
        return self.at.z + last - step if way == 0 else self.at.z - last + step

    def sends(self, way, step):
        last = self.at.chain - 1
        return self.at.z <= step if way == 0 else self.at.z >= last - step

    def receives(self, way, step):
        last = self.at.chain - 1
        if way == 0:
            return (self.at.z >= 1) & (self.at.z <= step + 1)
        return (self.at.z < last) & (self.at.z >= last - step - 1)

    def ends(self, step, part):
        @pl.when(self.at.z == 0)
        def _():
            self.copy(0, self.slab_of(0, step), step, part).start()

        @pl.when(self.at.z == self.at.chain - 1)
        def _():
            self.copy(1, self.slab_of(1, step), step, part).start()

    def landed(self, way, step, part):
        return pltpu.make_async_copy(
            self.slots.at[way, step, pl.ds(part * self.height, self.height)],
            self.stage.at[way, pl.ds(0, self.height)],
            self.local.at[way],
        )

    def add(self, way, slab, step, part):
        self.landed(way, step, part).wait()
        tile = min(64, self.height)

        def body(i, carry):
            here = pl.ds(pl.multiple_of(i * tile, tile), tile)
            rows = pl.ds(pl.multiple_of(part * self.height + i * tile, tile), tile)
            total = self.slabs[slab, rows, :].astype(WIDE) + self.stage[way, here, :].astype(WIDE)
            self.slabs[slab, rows, :] = total.astype(LOW)
            return carry

        lax.fori_loop(0, self.height // tile, body, 0)

    def passes(self, way, step):
        inside = self.at.z > 0 if way == 0 else self.at.z < self.at.chain - 1
        return self.sends(way, step) & inside

    def step(self, step, part):
        for way in (0, 1):

            @pl.when(self.passes(way, step))
            def _():
                self.copy(way, 0, step - 1, part).wait_recv()
                self.landed(way, step - 1, part).start()

        for way in (0, 1):

            @pl.when(self.passes(way, step))
            def _():
                slab = self.slab_of(way, step)
                self.add(way, slab, step - 1, part)
                self.copy(way, slab, step, part).start()

    def finish(self):
        last = self.at.chain - 2
        for part in range(PARTS):
            for way in (0, 1):

                @pl.when(self.receives(way, last))
                def _():
                    self.copy(way, 0, last, part).wait_recv()
                    self.landed(way, last, part).start()

            for way in (0, 1):

                @pl.when(self.receives(way, last))
                def _():
                    self.add(way, self.at.z, last, part)

    def sent(self):
        for step in range(self.at.chain - 1):
            for part in range(PARTS):
                for way in (0, 1):

                    @pl.when(self.sends(way, step))
                    def _():
                        self.copy(way, 0, step, part).wait_send()


def layer_kernel(
    size,
    tokens,
    cot,
    gain_one,
    gain_two,
    lens_in,
    w_query,
    w_key,
    w_value,
    w_out,
    w_gate,
    w_up,
    w_down,
    block_out,
    grad_tokens,
    grad_gains,
    g_query,
    g_key,
    g_value,
    g_out,
    g_gate,
    g_up,
    g_down,
    kept,
    slots,
    first,
    second,
    weights,
    qkv_weights,
    out_weights,
    grads,
    hidden,
    rows_two,
    turned,
    inner,
    units,
    sums_low,
    begun,
    qkv,
    attended,
    logs,
    table,
    head_sums,
    chain_stage,
    plane_stage,
    middle,
    total,
    last_stage,
    gain_rows,
    gains_in,
    lens,
    gain_parts,
    gain_peers,
    swap_sems,
    gather_send,
    gather_recv,
    reduce_send,
    reduce_recv,
    last_sems,
    plane_sems,
    first_sems,
    second_sems,
    small_sems,
    gain_sems,
    local_sems,
):
    chain, peers, rows, width, stages, unit, wide, seqs, tile = size
    at = Place(chain, peers)
    c, t, z = at.c, at.t, at.z
    group = rows * peers
    plane = 2 * group
    steps = chain - 1
    heads = wide // HEAD_DIM
    own_start = pl.multiple_of(c * group + t * rows, rows)
    query_tile = min(256, group)
    hub = min(256, unit)
    splits = PARTS if wide % (PARTS * LANES) == 0 else 1

    def slab_cols(s):
        return pl.ds(pl.multiple_of(s * 2 * unit, 2 * unit), 2 * unit)

    entry_barrier(at)

    def gain_copy(dp, source):
        place = gain_rows.at[:, pl.ds(pl.multiple_of(source * unit, unit), unit)]
        return remote(gains_in, place, gain_sems.at[0, dp], gain_sems.at[1, source], at.part(dp))

    own_gain = pltpu.make_async_copy(
        gains_in, gain_rows.at[:, pl.ds(pl.multiple_of(at.dp * unit, unit), unit)], local_sems.at[2]
    )

    def lens_copy(core):
        return remote(
            lens.at[core], lens.at[core], small_sems.at[0], small_sems.at[1], at.sibling()
        )

    lane = lax.broadcasted_iota(jnp.int32, (1, LANES), 1)
    gains_in[...] = jnp.zeros_like(gains_in)
    gains_in[0:1, :] = gain_one[...].astype(WIDE).reshape(1, unit)
    gains_in[1:2, :] = gain_two[...].astype(WIDE).reshape(1, unit)
    lens_row = jnp.zeros((8, LANES), WIDE)
    for s in range(seqs):
        lens_row = jnp.where(lane == s, lens_in[0, s].astype(WIDE), lens_row)
    lens[c] = lens_row

    def swap_copies(n):
        if n == 0:
            arrays = [(w, True, k * wide, wide, 0) for k, w in enumerate((w_query, w_key, w_value))]
            slab, down = qkv_weights.at[z], 0
        elif n == 1:
            arrays = [(w_out, False, 0, wide, 0)]
            slab, down = out_weights.at[z], 0
        else:
            arrays = [(w_gate, True, 0, unit, n - 2), (w_up, True, unit, unit, n - 2)]
            arrays.append((w_down, False, 0, unit, n - 2))
            slab, down = weights.at[n - 2, z], 2 * unit
        copies = []
        mine = pl.multiple_of(c * unit, unit)
        for k, (array, tall, offset, extent, stage) in enumerate(arrays):

            def half(core):
                count = (array.shape[1] if tall else array.shape[0]) // 2
                piece = pl.ds(pl.multiple_of(core * count + stage * extent, extent), extent)
                return array.at[:, piece] if tall else array.at[piece, :]

            if tall:
                place = slab.at[pl.ds(mine, unit), pl.ds(offset, extent)]
            else:
                place = slab.at[pl.ds(down, extent), pl.ds(mine, unit)]
            keep = pltpu.make_async_copy(half(c), place, swap_sems.at[0, n, k])
            give = remote(
                half(1 - c), place, swap_sems.at[1, n, k], swap_sems.at[2, n, k], at.sibling()
            )
            copies.append((keep, give))
        return copies

    def swapped(n):
        for keep, give in swap_copies(n):
            keep.wait()
            give.wait()

    for keep, give in swap_copies(0):
        keep.start()
        give.start()
    for dp in at.other_parts():
        gain_copy(dp, at.dp).start()
    own_gain.start()
    lens_copy(c).start()
    for n in range(1, stages + 2):
        for keep, give in swap_copies(n):
            keep.start()
            give.start()

    slabs = [qkv_weights, out_weights] + [weights.at[q] for q in range(stages)]
    stream = Stream(
        [
            ChainGather(at, ref, gather_send.at[n], gather_recv.at[n])
            for n, ref in enumerate(slabs)
        ],
        swapped,
    )
    gathers = [
        (SquareGather if peers == 4 else PlaneGather)(at, full, rows, [plane_sems.at[n, k] for k in range(4)])
        for n, full in enumerate((hidden, rows_two, hidden, rows_two))
    ]
    plane_sums = [
        (SquareReduce if peers == 4 else PlaneReduce)(
            at,
            rows,
            tile,
            buffer,
            first.at[n],
            second.at[n],
            plane_stage,
            [first_sems.at[n, 0], first_sems.at[n, 1], second_sems.at[n, 0], second_sems.at[n, 1]],
            local_sems.at[4],
        )
        for n, buffer in enumerate((sums_low, sums_low, begun, sums_low))
    ]
    chain_sums = [
        ChainReduce(
            at,
            ref,
            height,
            slots.at[n],
            reduce_send.at[n],
            reduce_recv.at[n],
            chain_stage,
            local_sems,
        )
        for n, (ref, height) in enumerate(
            [(grads.at[q], 3 * unit) for q in range(stages)]
            + [(weights.at[0], 3 * wide), (weights.at[1], wide)]
        )
    ]
    sum_qkv, sum_out = chain_sums[stages], chain_sums[stages + 1]

    stream.go(2)

    for dp in at.other_parts():
        gain_copy(at.dp, dp).wait_recv()
    own_gain.wait()

    def strips(body):
        def each(i, carry):
            here = pl.ds(pl.multiple_of(i * STRIP, STRIP), STRIP)
            there = pl.ds(pl.multiple_of(own_start + i * STRIP, STRIP), STRIP)
            body(here, there)
            return carry

        lax.fori_loop(0, rows // STRIP, each, 0)

    def factor_of(values):
        return lax.rsqrt(jnp.mean(values * values, axis=-1, keepdims=True) + EPSILON)

    def first_norm(here, there):
        values = tokens[here, :].astype(WIDE)
        hidden[there, :] = (values * factor_of(values) * gain_rows[0:1, :]).astype(LOW)

    strips(first_norm)
    gathers[0].start()

    lens_copy(c).wait_send()
    lens_copy(1 - c).wait_recv()
    frequency = jnp.exp(lax.rem(lane, HALF).astype(WIDE) * (-2.0 * math.log(ROPE_BASE) / HEAD_DIM))
    side = jnp.where(lax.rem(lane, HEAD_DIM) < HALF, -1.0, 1.0)

    def table_rows(core):
        def body(i, carry):
            shape = (rows, LANES)
            row = (lax.broadcasted_iota(jnp.int32, shape, 0) + i * rows).astype(WIDE)
            start = jnp.zeros((1, 1), WIDE)
            base = jnp.zeros(shape, WIDE)
            valid = jnp.zeros(shape, WIDE)
            for s in range(seqs):
                length = lens[core, 0:1, s : s + 1]
                inside = (row >= start) & (row < start + length)
                base = jnp.where(inside, start, base)
                valid = jnp.where(inside, 1.0, valid)
                start = start + jnp.floor((length + (BLOCK - 1.0)) * (1.0 / BLOCK)) * BLOCK
            angle = (row - base) * frequency
            lowest = jnp.where(valid > 0.5, base, row)
            here = pl.ds(pl.multiple_of(core * group + i * rows, rows), rows)
            table[0, here, :] = jnp.cos(angle)
            table[1, here, :] = jnp.sin(angle) * side
            table[2, here, :] = jnp.where(lane == 0, lowest, valid)
            return carry

        lax.fori_loop(0, peers, body, 0)

    table_rows(0)
    table_rows(1)
    stream.go(2)

    def own_cotangent(here, there):
        rows_two[there, :] = (cot[here, :].astype(WIDE) * table[2, there, 1:2]).astype(LOW)

    strips(own_cotangent)
    gathers[0].forward()
    gathers[1].start()
    stream.go(1)
    gathers[0].finish()
    stream.complete(0)

    first_half = lax.rem(lax.broadcasted_iota(jnp.int32, (1, LANES), 1), HEAD_DIM) < HALF

    def swap_halves(values):
        return jnp.where(
            first_half, pltpu.roll(values, LANES - HALF, 1), pltpu.roll(values, HALF, 1)
        )

    def rotated(values, there, sign):
        pieces = []
        for n in range(0, values.shape[1], LANES):
            piece = values[:, n : n + LANES]
            pieces.append(
                piece * table[0, there, :] + sign * (swap_halves(piece) * table[1, there, :])
            )
        return jnp.concatenate(pieces, axis=1) if len(pieces) > 1 else pieces[0]

    def project(i, carry):
        here = pl.ds(pl.multiple_of(i * tile, tile), tile)
        sums = jnp.zeros((tile, 3 * wide), WIDE)
        for s in range(chain):
            sums += dot_nn(hidden[here, s * 2 * unit : (s + 1) * 2 * unit], qkv_weights[s])
        qkv[0, here, :] = rotated(sums[:, :wide], here, 1.0).astype(LOW)
        qkv[1, here, :] = rotated(sums[:, wide : 2 * wide], here, 1.0).astype(LOW)
        qkv[2, here, :] = sums[:, 2 * wide :].astype(LOW)
        return carry

    lax.fori_loop(0, plane // tile, project, 0)
    keep_rows = pltpu.make_async_copy(hidden, kept, local_sems.at[5])
    keep_rows.start()
    stream.go(2)
    gathers[1].forward()

    head_lane = lax.div(lax.broadcasted_iota(jnp.int32, (1, wide), 1), HEAD_DIM)

    def masked(scores, here, offset):
        column = lax.broadcasted_iota(jnp.int32, scores.shape, 1)
        row = lax.broadcasted_iota(jnp.int32, scores.shape, 0) + offset
        lowest = table[2, here, 0:1].astype(jnp.int32)
        return jnp.where((column >= lowest) & (column <= row), scores, MASKED)

    def attend(core, low, high):
        base = pl.multiple_of(core * group, group)

        def body(h, carry):
            lanes = jnp.where(head_lane == h, 1.0, 0.0)
            for b in range(group // query_tile):
                here = pl.ds(pl.multiple_of(base + b * query_tile, query_tile), query_tile)
                keys = pl.ds(base, (b + 1) * query_tile)
                query = (qkv[0, here, :].astype(WIDE) * (lanes * SCALE)).astype(LOW)
                scores = masked(dot_nt(query, qkv[1, keys, :]), here, b * query_tile)
                peak = jnp.max(scores, axis=-1, keepdims=True)
                exponent = jnp.exp(scores - peak)
                sums = jnp.sum(exponent, axis=-1, keepdims=True)
                weight = (exponent / sums).astype(LOW)
                mixed = dot_nn(weight, qkv[2, keys, :]) * lanes
                place = slice(b * query_tile, (b + 1) * query_tile)
                earlier = jnp.where(h == 0, 0.0, head_sums[0, place, :])
                head_sums[0, place, :] = earlier + mixed
                logs[here, :] = jnp.where(lane == h, peak + jnp.log(sums), logs[here, :])
            return carry

        if low == 0:
            logs[pl.ds(base, group), :] = jnp.zeros((group, LANES), WIDE)
            head_sums[0] = jnp.zeros((group, wide), WIDE)
        lax.fori_loop(low, high, body, 0)
        if high == heads:
            attended[pl.ds(base, group), :] = head_sums[0].astype(LOW)

    middle_head = heads // 2
    attend(1 - c, 0, middle_head)
    stream.go(2)
    attend(1 - c, middle_head, heads)
    keep_rows.wait()
    stream.complete(1)

    def product_tile(terms):
        def compute(source, out, extras):
            def body(s, carry):
                cols = slab_cols(s)
                sums = terms(source, s)
                for extra in extras:
                    sums += extra[:, cols].astype(WIDE)
                out[:, cols] = sums.astype(LOW)
                return carry

            lax.fori_loop(0, chain, body, 0)

        return compute

    out_tile = product_tile(lambda source, s: dot_nn(attended[source, :], out_weights[s]))
    plane_sums[0].half(out_tile)
    attend(c, 0, heads)
    stream.go(1)
    plane_sums[0].rest(out_tile)
    plane_sums[0].merge()
    gathers[1].finish()
    stream.go(3)
    plane_sums[0].finish(total)

    def second_norm(here, there):
        values = tokens[here, :].astype(WIDE) + total[here, :] * table[2, there, 1:2]
        middle[here, :] = values
        hidden[there, :] = (values * factor_of(values) * gain_rows[1:2, :]).astype(LOW)

    strips(second_norm)
    gathers[2].start()
    stream.go(2)
    gathers[2].forward()
    plane_sums[0].sent()
    stream.go(1)
    gathers[2].finish()

    def hidden_units(q):
        def body(i, carry):
            these = pl.ds(pl.multiple_of(i * tile, tile), tile)
            gate_up = jnp.zeros((tile, 2 * unit), WIDE)
            grad_inner = jnp.zeros((tile, unit), WIDE)
            for s in range(chain):
                cols = slice(s * 2 * unit, (s + 1) * 2 * unit)
                gate_up += dot_nn(hidden[these, cols], weights[q, s, 0 : 2 * unit, :])
                grad_inner += dot_nt(rows_two[these, cols], weights[q, s, 2 * unit :, :])
            gate, up = gate_up[:, :unit], gate_up[:, unit:]
            sigmoid_gate = jax.nn.sigmoid(gate)
            inner[q, these, :] = (gate * sigmoid_gate * up).astype(LOW)
            units[q, these, 0:unit] = (
                grad_inner * up * sigmoid_gate * (1.0 + gate * (1.0 - sigmoid_gate))
            ).astype(LOW)
            units[q, these, unit : 2 * unit] = (grad_inner * gate * sigmoid_gate).astype(LOW)
            return carry

        lax.fori_loop(0, plane // tile, body, 0)

    eye = identity(hub)

    def turn_into(start, source):
        extent = min(hub, source.shape[1])

        def body(i, carry):
            cols = pl.ds(pl.multiple_of(i * extent, extent), extent)
            place = pl.ds(pl.multiple_of(start + i * extent, extent), extent)
            turned[place, :] = dot_nt(eye[:extent, :extent], source[:, cols]).astype(LOW)
            return carry

        lax.fori_loop(0, source.shape[1] // extent, body, 0)

    def in_grads(q):
        turn_into(0, units.at[q])

        def body(s, carry):
            grads[q, s, 0 : 2 * unit, :] = dot_nn(
                turned[0 : 2 * unit, :], hidden[:, slab_cols(s)]
            ).astype(LOW)
            return carry

        lax.fori_loop(0, chain, body, 0)

    def down_grads(q):
        turn_into(2 * unit, inner.at[q])

        def body(s, carry):
            grads[q, s, 2 * unit :, :] = dot_nn(
                turned[2 * unit :, :], rows_two[:, slab_cols(s)]
            ).astype(LOW)
            return carry

        lax.fori_loop(0, chain, body, 0)

    def hidden_sums(stage_list):
        return product_tile(
            lambda source, s: sum(
                dot_nt(units[q, source, :], weights[q, s, 0 : 2 * unit, :]) for q in stage_list
            )
        )

    def begin_hidden():
        begin = hidden_sums(range(stages - 1))
        for i in range(group // tile):
            here = pl.ds(i * tile, tile)
            begin(plane_sums[1].source(1 - c, i), sums_low.at[here], [])
            begin(plane_sums[1].source(c, i), begun.at[here], [])

    for q in range(stages):
        stream.complete(q + 2)
        hidden_units(q)
        if q == stages - 1:
            break
        stream.go(1)
        in_grads(q)
        down_grads(q)
        for part in range(PARTS):
            chain_sums[q].ends(0, part)
        stream.go(1)
        for k in range(1, steps):
            for part in range(PARTS):
                stream.go(1)
                chain_sums[q].ends(k, part)
                if k > 1:
                    chain_sums[q].step(k - 1, part)
                if q == stages - 2 and (k, part) == (1, 0):
                    begin_hidden()
        if q == stages - 2 and steps == 1:
            begin_hidden()

    branch_tile = product_tile(
        lambda source, s: sum(
            dot_nn(inner[q, source, :], weights[q, s, 2 * unit :, :]) for q in range(stages)
        )
    )

    def chain_steps(n, low, high):
        for k in range(max(low, 1), high):
            for part in range(PARTS):
                chain_sums[n].step(k, part)

    def last_step(n):
        chain_steps(n, steps - 1, steps)

    def placed(n, core, source):
        own = chain_sums[n].slabs.at[z]
        cols = pl.ds(pl.multiple_of(core * unit, unit), unit)
        stage = last_stage.at[n % 2, core]
        if n < stages:
            place = pl.ds(pl.multiple_of((source * stages + n) * unit, unit), unit)
            return [
                (stage.at[0, :, pl.ds(0, unit)], g_gate.at[:, place]),
                (stage.at[1, :, pl.ds(0, unit)], g_up.at[:, place]),
                (own.at[pl.ds(2 * unit, unit), cols], g_down.at[place, :]),
            ]
        place = pl.ds(pl.multiple_of(source * wide, wide), wide)
        if n == stages:
            return [
                (stage.at[k, :, pl.ds(0, wide)], out.at[:, place])
                for k, out in enumerate((g_query, g_key, g_value))
            ]
        return [(own.at[pl.ds(0, wide), cols], g_out.at[place, :])]

    def last_copies(n):
        copies = []
        for k, ((mine, place), (theirs, _)) in enumerate(
            zip(placed(n, c, c), placed(n, 1 - c, c))
        ):
            keep = pltpu.make_async_copy(mine, place, last_sems.at[0, n, k])
            give = remote(theirs, place, last_sems.at[1, n, k], last_sems.at[2, n, k], at.sibling())
            copies.append((keep, give))
        return copies

    def finish_sum(n):
        chain_sums[n].finish()
        own = chain_sums[n].slabs
        pieces = []
        if n < stages:
            pieces = [(k, k * unit, 0, unit) for k in range(2)]
        elif n == stages:
            lanes = wide // splits
            pieces = [
                (k, (m * 3 + k) * lanes, m * lanes, lanes) for m in range(splits) for k in range(3)
            ]
        for core in (0, 1):
            for k, start, place, extent in pieces:
                piece = own[z, start : start + extent, core * unit : (core + 1) * unit]
                last_stage[n % 2, core, k, :, place : place + extent] = turn(piece, eye)
        for keep, give in last_copies(n):
            keep.start()
            give.start()

    def settle(n):
        for keep, give in last_copies(n):
            keep.wait()
            give.wait()
        chain_sums[n].sent()

    down_grads(stages - 1)
    last_tile = hidden_sums([stages - 1])
    plane_sums[1].half(last_tile, begun=True)
    plane_sums[1].rest(last_tile, begun=begun)
    early = list(range(stages - 1))
    for q in early[-1:] + early[:-1]:
        last_step(q)
        if q == early[-1]:
            plane_sums[1].merge()
    in_grads(stages - 1)
    for k in range(steps):
        for part in range(PARTS):
            chain_sums[stages - 1].ends(k, part)
    plane_sums[2].half(branch_tile)
    bring_rows = pltpu.make_async_copy(kept, hidden, local_sems.at[5])
    bring_rows.start()
    plane_sums[1].finish(total)

    def second_back(here, there):
        values = middle[here, :]
        factor = factor_of(values)
        normed = values * factor
        grad = total[here, :]
        gain_parts[1:2, :] += jnp.sum(grad * normed, axis=0, keepdims=True)
        scaled = grad * gain_rows[1:2, :]
        mean = jnp.mean(scaled * normed, axis=-1, keepdims=True)
        result = cot[here, :].astype(WIDE) + factor * (scaled - normed * mean)
        grad_tokens[here, :] = result
        rows_two[there, :] = (result * table[2, there, 1:2]).astype(LOW)

    gain_parts[...] = jnp.zeros_like(gain_parts)
    strips(second_back)
    gathers[3].start()
    plane_sums[1].sent()
    for chain_gather in stream.chains:
        chain_gather.sent()
    plane_sums[2].rest(branch_tile)
    finish_sum(0)
    plane_sums[2].merge()
    chain_steps(stages - 1, 1, steps - 1)
    if stages > 3:
        settle(0)
        finish_sum(2)
    if stages > 2:
        finish_sum(1)
    gathers[3].forward()
    gathers[3].finish()

    def finish_branch():
        plane_sums[2].finish(total)

        def last_rows(here, there):
            result = middle[here, :] + total[here, :] * table[2, there, 1:2]
            block_out[here, :] = result.astype(LOW)

        strips(last_rows)

    grad_attended = inner.at[0]

    def attended_grad(i, carry):
        here = pl.ds(pl.multiple_of(i * tile, tile), tile)
        sums = jnp.zeros((tile, wide), WIDE)
        for s in range(chain):
            sums += dot_nt(rows_two[here, s * 2 * unit : (s + 1) * 2 * unit], out_weights[s])
        grad_attended[here, :] = sums.astype(LOW)
        return carry

    turn_into(0, attended)

    def out_grads(s, carry):
        weights[1, s, 0:wide, :] = dot_nn(turned[0:wide, :], rows_two[:, slab_cols(s)]).astype(LOW)
        return carry

    lax.fori_loop(0, chain, out_grads, 0)
    for k in range(steps):
        for part in range(PARTS):
            sum_out.ends(k, part)
    lax.fori_loop(0, plane // tile, attended_grad, 0)

    def attend_back(core, low, high):
        base = core * group

        def body(h, carry):
            lanes = jnp.where(head_lane == h, 1.0, 0.0)
            lanes_low = lanes.astype(LOW)
            for b in range(group // query_tile):
                here = slice(base + b * query_tile, base + (b + 1) * query_tile)
                keys = slice(base, base + (b + 1) * query_tile)
                place = slice(b * query_tile, (b + 1) * query_tile)
                reach = slice(0, (b + 1) * query_tile)
                query = qkv[0, here, :] * lanes_low
                grad = grad_attended[here, :] * lanes_low
                scores = masked(dot_nt(query, qkv[1, keys, :]) * SCALE, here, b * query_tile)
                log_total = jnp.sum(
                    jnp.where(lane == h, logs[here, :], 0.0), axis=-1, keepdims=True
                )
                probs = jnp.exp(scores - log_total)
                grad_probs = dot_nt(grad, qkv[2, keys, :])
                shift = jnp.sum(probs * grad_probs, axis=-1, keepdims=True)
                grad_scores = (probs * (grad_probs - shift) * SCALE).astype(LOW)
                head_sums[0, place, :] += dot_nn(grad_scores, qkv[1, keys, :]) * lanes
                head_sums[1, reach, :] += dot_nn(turn(grad_scores, eye), query)
                head_sums[2, reach, :] += dot_nn(turn(probs.astype(LOW), eye), grad)
            return carry

        for k in range(3):
            head_sums[k] = jnp.zeros((group, wide), WIDE)
        lax.fori_loop(low, high, body, 0)
        lanes = slice(low * HEAD_DIM, high * HEAD_DIM)

        def back(i, carry):
            there = pl.ds(pl.multiple_of(base + i * query_tile, query_tile), query_tile)
            here = pl.ds(pl.multiple_of(i * query_tile, query_tile), query_tile)
            for k in range(2):
                values = rotated(head_sums[k, here, lanes], there, -1.0)
                units[0, there, k * wide + lanes.start : k * wide + lanes.stop] = values.astype(LOW)
            units[1, there, lanes] = head_sums[2, here, lanes].astype(LOW)
            return carry

        lax.fori_loop(0, group // query_tile, back, 0)

    def qkv_grads(n):
        lanes = wide // splits
        turn_into(0, units.at[0, :, pl.ds(n * lanes, lanes)])
        turn_into(lanes, units.at[0, :, pl.ds(wide + n * lanes, lanes)])
        turn_into(2 * lanes, units.at[1, :, pl.ds(n * lanes, lanes)])

        parts = range(n * PARTS // splits, (n + 1) * PARTS // splits)
        for k in range(chain):
            s = jnp.where(at.z < (chain + 1) // 2, chain - 1 - k, k)
            weights[0, s, n * 3 * lanes : (n + 1) * 3 * lanes, :] = dot_nn(
                turned[0 : 3 * lanes, :], hidden[:, slab_cols(s)]
            ).astype(LOW)
            if k < steps:
                for part in parts:
                    sum_qkv.ends(k, part)

    for n in range(splits):
        low, high = n * heads // splits, (n + 1) * heads // splits
        attend_back(0, low, high)
        if n == 0:
            last_step(stages - 1)
        attend_back(1, low, high)
        if n == 0:
            bring_rows.wait()
        qkv_grads(n)

    first_tile = product_tile(
        lambda source, s: dot_nt(units[0, source, :], qkv_weights[s, :, 0 : 2 * wide])
        + dot_nt(units[1, source, 0:wide], qkv_weights[s, :, 2 * wide :])
    )
    chain_steps(stages + 1, 1, steps - 1)
    plane_sums[3].half(first_tile)
    plane_sums[3].rest(first_tile)
    plane_sums[3].merge()

    def qkv_steps(part, low, high):
        for k in range(max(low, 1), high):
            sum_qkv.step(k, part)

    qkv_steps(0, 1, steps - 1)
    if stages > 2:
        settle(stages - 3)
    finish_sum(stages - 1)
    last_step(stages + 1)
    qkv_steps(0, steps - 1, steps)
    finish_branch()
    for part in range(1, PARTS):
        qkv_steps(part, 1, steps - 1)
    finish_sum(stages + 1)
    for part in range(1, PARTS):
        qkv_steps(part, steps - 1, steps)
    plane_sums[3].finish(total)

    def first_back(here, there):
        values = tokens[here, :].astype(WIDE)
        factor = factor_of(values)
        normed = values * factor
        grad = total[here, :]
        gain_parts[0:1, :] += jnp.sum(grad * normed, axis=0, keepdims=True)
        scaled = grad * gain_rows[0:1, :]
        mean = jnp.mean(scaled * normed, axis=-1, keepdims=True)
        grad_tokens[here, :] += factor * (scaled - normed * mean)

    strips(first_back)

    own_cols = pl.ds(pl.multiple_of(at.dp * unit, unit), unit)

    def gain_sum_copy(dp, source):
        cols = pl.ds(pl.multiple_of(dp * unit, unit), unit)
        return remote(
            gain_parts.at[:, cols],
            gain_peers.at[source],
            gain_sems.at[2, dp],
            gain_sems.at[3, source],
            at.part(dp),
        )

    def gain_peer_copy(peer, source):
        parts = 2 * chain
        return remote(
            gain_peers.at[parts + t],
            gain_peers.at[parts + source],
            gain_sems.at[4, peer],
            gain_sems.at[5, source],
            at.peer(peer),
        )

    for dp in at.other_parts():
        gain_sum_copy(dp, at.dp).start()
    settle(stages - 2)
    sums = gain_parts[:, own_cols]
    for dp in at.other_parts():
        gain_sum_copy(at.dp, dp).wait_recv()
        sums += gain_peers[dp]
    gain_peers[2 * chain + t] = sums
    for peer in at.other_peers():
        gain_peer_copy(peer, t).start()
    for peer in at.other_peers():
        gain_peer_copy(t, peer).wait_recv()
        sums += gain_peers[2 * chain + peer]
    grad_gains[...] = sums
    settle(stages - 1)
    finish_sum(stages)
    settle(stages)
    settle(stages + 1)
    plane_sums[2].sent()
    plane_sums[3].sent()
    for dp in at.other_parts():
        gain_copy(dp, at.dp).wait_send()
        gain_sum_copy(dp, at.dp).wait_send()
    for peer in at.other_peers():
        gain_peer_copy(peer, t).wait_send()


def finish_kernel(*refs):
    count = len(refs) // 2
    sources, outs = refs[:count], refs[count:]
    for source, out in zip(sources[:2] + sources[3:], outs[: count - 1]):
        out[...] = source[...].astype(out.dtype)
    outs[count - 1][...] = sources[2][0:1, :]
    outs[count][...] = sources[2][1:2, :]


def finish(arrays):
    steps = 4
    gains = arrays[2]

    def split(array):
        return pl.BlockSpec((array.shape[0] // steps, array.shape[1]), lambda i: (i, 0))

    whole = pl.BlockSpec(gains.shape, lambda i: (0, 0))
    row = pl.BlockSpec((1, gains.shape[1]), lambda i: (0, 0))
    kept = arrays[:2] + arrays[3:]
    dtypes = [array.dtype for array in arrays[:2]] + [WIDE] * len(arrays[3:])
    return pl.pallas_call(
        finish_kernel,
        grid=(steps,),
        out_shape=[jax.ShapeDtypeStruct(a.shape, d) for a, d in zip(kept, dtypes)]
        + [jax.ShapeDtypeStruct((1, gains.shape[1]), WIDE)] * 2,
        in_specs=[split(a) for a in arrays[:2]] + [whole] + [split(a) for a in arrays[3:]],
        out_specs=[split(a) for a in kept] + [row] * 2,
        compiler_params=pltpu.CompilerParams(vmem_limit_bytes=VMEM_BYTES),
        name="finish",
    )(*arrays)


def on_device(
    tokens_in,
    seq_lens,
    w_query,
    w_key,
    w_value,
    w_out,
    norm1_gain,
    w_gate,
    w_up,
    w_down,
    norm2_gain,
    out_cotangent,
):
    n_dp, peers = lax.axis_size("dp"), lax.axis_size("tensor")
    chain = n_dp // 2
    rows, width = tokens_in.shape
    unit = width // n_dp
    wide = w_query.shape[1] // 2
    stages = w_gate.shape[1] // 2 // unit
    seqs = seq_lens.shape[1]
    group = rows * peers
    plane = 2 * group
    tile = min(256, group)
    slab = (3 * unit, 2 * unit)
    size = (chain, peers, rows, width, stages, unit, wide, seqs, tile)
    hbm = pl.BlockSpec(memory_space=pl.ANY)
    vmem = pl.BlockSpec(memory_space=pltpu.VMEM)
    smem = pl.BlockSpec(memory_space=pltpu.SMEM)
    dma = pltpu.SemaphoreType.DMA

    def like(array):
        return jax.ShapeDtypeStruct(array.shape, LOW)

    outs = pl.pallas_call(
        functools.partial(layer_kernel, size),
        out_shape=(
            jax.ShapeDtypeStruct((rows, width), LOW),
            jax.ShapeDtypeStruct((rows, width), WIDE),
            jax.ShapeDtypeStruct((8, unit), WIDE),
            like(w_query),
            like(w_key),
            like(w_value),
            like(w_out),
            like(w_gate),
            like(w_up),
            like(w_down),
            jax.ShapeDtypeStruct((plane, width), LOW),
            jax.ShapeDtypeStruct((stages + 2, 2, chain - 1) + slab, LOW),
            jax.ShapeDtypeStruct((4, group, width), LOW),
            jax.ShapeDtypeStruct((4, peers, rows, width), LOW),
        ),
        in_specs=[vmem, vmem, vmem, vmem, smem] + [hbm] * 7,
        out_specs=(vmem, vmem, vmem) + (hbm,) * 11,
        scratch_shapes=[
            pltpu.VMEM((stages, chain) + slab, LOW),
            pltpu.VMEM((chain, 2 * unit, 3 * wide), LOW),
            pltpu.VMEM((chain, wide, 2 * unit), LOW),
            pltpu.VMEM((stages, chain) + slab, LOW),
            pltpu.VMEM((plane, width), LOW),
            pltpu.VMEM((plane, width), LOW),
            pltpu.VMEM((3 * unit, plane), LOW),
            pltpu.VMEM((stages, plane, unit), LOW),
            pltpu.VMEM((stages, plane, 2 * unit), LOW),
            pltpu.VMEM((group, width), LOW),
            pltpu.VMEM((group, width), LOW),
            pltpu.VMEM((3, plane, wide), LOW),
            pltpu.VMEM((plane, wide), LOW),
            pltpu.VMEM((plane, LANES), WIDE),
            pltpu.VMEM((3, plane, LANES), WIDE),
            pltpu.VMEM((3, group, wide), WIDE),
            pltpu.VMEM((2, slab[0] // PARTS, slab[1]), LOW),
            pltpu.VMEM((tile, width), LOW),
            pltpu.VMEM((rows, width), WIDE),
            pltpu.VMEM((rows, width), WIDE),
            pltpu.VMEM((2, 2, 3, unit, max(unit, wide)), LOW),
            pltpu.VMEM((8, width), WIDE),
            pltpu.VMEM((8, unit), WIDE),
            pltpu.VMEM((2, 8, LANES), WIDE),
            pltpu.VMEM((8, width), WIDE),
            pltpu.VMEM((n_dp + peers, 8, unit), WIDE),
            dma((3, stages + 2, 3)),
            dma((stages + 2, 2, chain - 1, PARTS)),
            dma((stages + 2, 2, chain - 1, PARTS)),
            dma((stages + 2, 2, chain - 1, PARTS)),
            dma((stages + 2, 2, chain - 1, PARTS)),
            dma((3, stages + 2, 3)),
            dma((4, 4, peers)),
            dma((4, 2, group // tile)),
            dma((4, 2, max(peers, 6))),
            dma((2,)),
            dma((6, n_dp)),
            dma((6,)),
        ],
        compiler_params=pltpu.CompilerParams(
            collective_id=0, has_side_effects=True, vmem_limit_bytes=VMEM_BYTES
        ),
        cost_estimate=pl.CostEstimate(
            flops=6 * plane * width * (4 * wide + 3 * unit * stages),
            bytes_accessed=16 * width * (4 * wide + 3 * unit * stages),
            transcendentals=0,
        ),
        name="layer",
    )(
        tokens_in,
        out_cotangent,
        norm1_gain,
        norm2_gain,
        seq_lens,
        w_query,
        w_key,
        w_value,
        w_out,
        w_gate,
        w_up,
        w_down,
    )
    block_out, grad_tokens, *weight_grads, gain_one, gain_two = finish(outs[:10])
    return (
        block_out,
        grad_tokens,
        *weight_grads[:4],
        gain_one.reshape(unit),
        *weight_grads[4:],
        gain_two.reshape(unit),
    )


def solution(mesh):
    return jax.shard_map(
        on_device,
        mesh=mesh,
        in_specs=(
            P(("dp", "tensor"), None),
            P("dp", None),
            P("dp", "tensor"),
            P("dp", "tensor"),
            P("dp", "tensor"),
            P("tensor", "dp"),
            P("dp"),
            P("dp", "tensor"),
            P("dp", "tensor"),
            P("tensor", "dp"),
            P("dp"),
            P(("dp", "tensor"), None),
        ),
        out_specs=(
            P(("dp", "tensor"), None),
            P(("dp", "tensor"), None),
            P("dp", "tensor"),
            P("dp", "tensor"),
            P("dp", "tensor"),
            P("tensor", "dp"),
            P("dp"),
            P("dp", "tensor"),
            P("dp", "tensor"),
            P("tensor", "dp"),
            P("dp"),
        ),
        check_vma=False,
    )
```

```python
import functools
import math

import jax
import jax.numpy as jnp
from jax import lax
from jax.experimental import pallas as pl
from jax.experimental.pallas import tpu as pltpu
from jax.sharding import PartitionSpec as P

HEAD_DIM = 64
HALF = HEAD_DIM // 2
BLOCK = 128
LANES = 128
EPSILON = 1e-05
ROPE_BASE = 130000.0
MASKED = -1e30
SCALE = HEAD_DIM ** (-0.5)

LOW = jnp.bfloat16
WIDE = jnp.float32
VMEM_BYTES = 64 * 1024 * 1024
PARTS = 2
STRIP = 32


def dot_nn(left, right):
    return lax.dot_general(left, right, (((1,), (0,)), ((), ())), preferred_element_type=WIDE)


def dot_nt(left, right):
    return lax.dot_general(left, right, (((1,), (1,)), ((), ())), preferred_element_type=WIDE)


def identity(size):
    across = lax.broadcasted_iota(jnp.int32, (size, size), 0)
    down = lax.broadcasted_iota(jnp.int32, (size, size), 1)
    return jnp.where(across == down, 1.0, 0.0).astype(LOW)


def turn(values, eye):
    size = eye.shape[0]
    width = values.shape[1]
    if width <= size:
        return dot_nt(eye[:width, :width], values).astype(LOW)
    blocks = [dot_nt(eye, values[:, n : n + size]).astype(LOW) for n in range(0, width, size)]
    return jnp.concatenate(blocks, axis=0)


class Place:
    def __init__(self, chain, peers):
        self.chain, self.peers = chain, peers
        self.dp = lax.axis_index("dp")
        self.t = lax.axis_index("tensor")
        self.c = lax.rem(self.dp, 2)
        self.z = lax.div(self.dp, 2)

    def sibling(self):
        return {"dp": self.dp + 1 - 2 * self.c, "tensor": self.t}

    def along(self, step):
        return {"dp": self.dp + 2 * step, "tensor": self.t}

    def part(self, dp):
        return {"dp": dp, "tensor": self.t}

    def peer(self, t):
        return {"dp": self.dp, "tensor": t}

    def other_peers(self):
        return [lax.rem(self.t + n, self.peers) for n in range(1, self.peers)]

    def other_parts(self):
        parts = 2 * self.chain
        return [lax.rem(self.dp + n, parts) for n in range(1, parts)]


def remote(src, dst, send, recv, device):
    return pltpu.make_async_remote_copy(
        src_ref=src,
        dst_ref=dst,
        send_sem=send,
        recv_sem=recv,
        device_id=device,
        device_id_type=pl.DeviceIdType.MESH,
    )


def fetch(src, dst, sem):
    copy = pltpu.make_async_copy(src, dst, sem)
    copy.start()
    copy.wait()


def entry_barrier(at):
    barrier = pltpu.get_barrier_semaphore()
    devices = [at.peer(t) for t in at.other_peers()] + [at.part(dp) for dp in at.other_parts()]
    for device in devices:
        pl.semaphore_signal(barrier, inc=1, device_id=device, device_id_type=pl.DeviceIdType.MESH)
    pl.semaphore_wait(barrier, len(devices))


class PlaneGather:
    def __init__(self, at, full, rows, sems):
        self.at, self.full, self.rows = at, full, rows
        self.group = rows * at.peers
        self.send, self.recv, self.pass_send, self.pass_recv = sems

    def block(self, c, t):
        start = pl.multiple_of(c * self.group + t * self.rows, self.rows)
        return self.full.at[pl.ds(start, self.rows)]

    def to_peer(self, t):
        at = self.at
        own = self.block(at.c, at.t)
        return remote(own, own, self.send.at[t], self.recv.at[at.t], at.peer(t))

    def from_peer(self, t):
        block = self.block(self.at.c, t)
        return remote(block, block, self.send.at[t], self.recv.at[t], self.at.peer(t))

    def to_sibling(self, t):
        block = self.block(self.at.c, t)
        return remote(
            block, block, self.pass_send.at[t], self.pass_recv.at[t], self.at.sibling()
        )

    def from_sibling(self, t):
        block = self.block(1 - self.at.c, t)
        return remote(
            block, block, self.pass_send.at[t], self.pass_recv.at[t], self.at.sibling()
        )

    def start(self):
        for t in self.at.other_peers():
            self.to_peer(t).start()
        self.to_sibling(self.at.t).start()

    def forward(self):
        for t in self.at.other_peers():
            self.from_peer(t).wait_recv()
            self.to_sibling(t).start()

    def finish(self):
        for t in range(self.at.peers):
            self.from_sibling(t).wait_recv()
        for t in self.at.other_peers():
            self.to_peer(t).wait_send()
        for t in range(self.at.peers):
            self.to_sibling(t).wait_send()


class PlaneReduce:
    def __init__(self, at, rows, tile, buffer, first, second, stage, sems, local):
        self.at, self.rows, self.tile, self.buffer = at, rows, tile, buffer
        self.group = rows * at.peers
        self.first, self.second, self.stage, self.local = first, second, stage, local
        self.send1, self.recv1, self.send2, self.recv2 = sems

    def source(self, c, i):
        return pl.ds(pl.multiple_of(c * self.group + i * self.tile, self.tile), self.tile)

    def to_sibling(self, i):
        here = pl.ds(i * self.tile, self.tile)
        return remote(
            self.buffer.at[here],
            self.first.at[here],
            self.send1.at[i],
            self.recv1.at[i],
            self.at.sibling(),
        )

    def to_peer(self, t, source):
        return remote(
            self.buffer.at[pl.ds(pl.multiple_of(t * self.rows, self.rows), self.rows)],
            self.second.at[source],
            self.send2.at[t],
            self.recv2.at[source],
            self.at.peer(t),
        )

    def half(self, compute, begun=False):
        for i in range(self.group // self.tile):
            out = self.buffer.at[pl.ds(i * self.tile, self.tile)]
            compute(self.source(1 - self.at.c, i), out, [out] if begun else [])
            self.to_sibling(i).start()

    def rest(self, compute, begun=None):
        at = self.at
        for i in range(self.group // self.tile):
            here = pl.ds(i * self.tile, self.tile)
            self.to_sibling(i).wait_recv()
            fetch(self.first.at[here], self.stage, self.local)
            self.to_sibling(i).wait_send()
            extras = [self.stage] if begun is None else [self.stage, begun.at[here]]
            compute(self.source(at.c, i), self.buffer.at[here], extras)
            for j in range(i * self.tile // self.rows, (i + 1) * self.tile // self.rows):

                @pl.when(at.t != j)
                def _():
                    self.to_peer(j, at.t).start()

    def finish(self, out):
        at = self.at
        own = pl.ds(pl.multiple_of(at.t * self.rows, self.rows), self.rows)
        out[...] = self.buffer[own, :].astype(WIDE)
        for t in at.other_peers():
            self.to_peer(at.t, t).wait_recv()
            fetch(self.second.at[t], self.stage.at[pl.ds(0, self.rows)], self.local)
            out[...] += self.stage[0 : self.rows, :].astype(WIDE)

    def sent(self):
        for t in self.at.other_peers():
            self.to_peer(t, self.at.t).wait_send()


class ChainGather:
    def __init__(self, at, slabs, send, recv):
        self.at, self.slabs, self.sems = at, slabs, (send, recv)
        self.height = slabs.shape[1] // PARTS

    def copy(self, way, slab, step, part):
        send, recv = self.sems
        ref = self.slabs.at[slab, pl.ds(part * self.height, self.height)]
        return remote(
            ref,
            ref,
            send.at[way, step, part],
            recv.at[way, step, part],
            self.at.along(1 - 2 * way),
        )

    def each_send(self, step, part, act):
        z, last = self.at.z, self.at.chain - 1

        @pl.when((z < last) & (z >= max(step, 1)))
        def _():
            act(self.copy(0, z - step, step, part))

        @pl.when((z > 0) & (z + step <= last) & (z + 1 - min(step, 1) <= last))
        def _():
            act(self.copy(1, z + step, step, part))

    def each_end(self, part, act):
        z, last = self.at.z, self.at.chain - 1

        @pl.when(z == 0)
        def _():
            act(self.copy(0, 0, 0, part))

        @pl.when(z == last)
        def _():
            act(self.copy(1, last, 0, part))

    def start(self, step, part):
        self.each_send(step, part, lambda copy: copy.start())

    def start_end(self, part):
        self.each_end(part, lambda copy: copy.start())

    def sent(self):
        for part in range(PARTS):
            self.each_end(part, lambda copy: copy.wait_send())
            for step in range(self.at.chain - 1):
                self.each_send(step, part, lambda copy: copy.wait_send())

    def arrived(self, step, part):
        z, last = self.at.z, self.at.chain - 1

        @pl.when(z - 1 - step >= 0)
        def _():
            self.copy(0, z - 1 - step, step, part).wait_recv()

        @pl.when(z + 1 + step <= last)
        def _():
            self.copy(1, z + 1 + step, step, part).wait_recv()


class Stream:
    def __init__(self, chains, swapped):
        self.chains, self.swapped = chains, swapped
        self.steps = chains[0].at.chain - 1
        self.messages = [
            (n, step, part)
            for n in range(len(chains))
            for step in range(self.steps)
            for part in range(PARTS)
        ]
        self.ends = [(n, part) for n in range(len(chains)) for part in range(PARTS)]
        self.next = 0
        self.ready = 0

    def need(self, n):
        while self.ready <= n:
            self.swapped(self.ready)
            self.ready += 1

    def go(self, count=1):
        for _ in range(count):
            done = self.next - PARTS
            if 0 <= done < len(self.messages):
                n, step, part = self.messages[done]
                self.chains[n].arrived(step, part)
            if self.next < len(self.messages):
                n, step, part = self.messages[self.next]
                self.need(n)
                self.chains[n].start(step, part)
            if self.next < len(self.ends):
                n, part = self.ends[self.next]
                self.need(n)
                self.chains[n].start_end(part)
            self.next += 1

    def complete(self, n):
        while self.next < (n + 1) * self.steps * PARTS + PARTS:
            self.go()


class ChainReduce:
    def __init__(self, at, slabs, height, slots, send, recv, stage, local):
        self.at, self.slabs, self.slots, self.sems = at, slabs, slots, (send, recv)
        self.stage, self.local = stage, local
        self.height = height // PARTS

    def copy(self, way, slab, step, part):
        send, recv = self.sems
        rows = pl.ds(part * self.height, self.height)
        return remote(
            self.slabs.at[slab, rows],
            self.slots.at[way, step, rows],
            send.at[way, step, part],
            recv.at[way, step, part],
            self.at.along(1 - 2 * way),
        )

    def slab_of(self, way, step):
        last = self.at.chain - 1
        return self.at.z + last - step if way == 0 else self.at.z - last + step

    def sends(self, way, step):
        last = self.at.chain - 1
        return self.at.z <= step if way == 0 else self.at.z >= last - step

    def receives(self, way, step):
        last = self.at.chain - 1
        if way == 0:
            return (self.at.z >= 1) & (self.at.z <= step + 1)
        return (self.at.z < last) & (self.at.z >= last - step - 1)

    def ends(self, step, part):
        @pl.when(self.at.z == 0)
        def _():
            self.copy(0, self.slab_of(0, step), step, part).start()

        @pl.when(self.at.z == self.at.chain - 1)
        def _():
            self.copy(1, self.slab_of(1, step), step, part).start()

    def landed(self, way, step, part):
        return pltpu.make_async_copy(
            self.slots.at[way, step, pl.ds(part * self.height, self.height)],
            self.stage.at[way, pl.ds(0, self.height)],
            self.local.at[way],
        )

    def add(self, way, slab, step, part):
        self.landed(way, step, part).wait()
        tile = min(64, self.height)

        def body(i, carry):
            here = pl.ds(pl.multiple_of(i * tile, tile), tile)
            rows = pl.ds(pl.multiple_of(part * self.height + i * tile, tile), tile)
            total = self.slabs[slab, rows, :].astype(WIDE) + self.stage[way, here, :].astype(WIDE)
            self.slabs[slab, rows, :] = total.astype(LOW)
            return carry

        lax.fori_loop(0, self.height // tile, body, 0)

    def passes(self, way, step):
        inside = self.at.z > 0 if way == 0 else self.at.z < self.at.chain - 1
        return self.sends(way, step) & inside

    def step(self, step, part):
        for way in (0, 1):

            @pl.when(self.passes(way, step))
            def _():
                self.copy(way, 0, step - 1, part).wait_recv()
                self.landed(way, step - 1, part).start()

        for way in (0, 1):

            @pl.when(self.passes(way, step))
            def _():
                slab = self.slab_of(way, step)
                self.add(way, slab, step - 1, part)
                self.copy(way, slab, step, part).start()

    def finish(self):
        last = self.at.chain - 2
        for part in range(PARTS):
            for way in (0, 1):

                @pl.when(self.receives(way, last))
                def _():
                    self.copy(way, 0, last, part).wait_recv()
                    self.landed(way, last, part).start()

            for way in (0, 1):

                @pl.when(self.receives(way, last))
                def _():
                    self.add(way, self.at.z, last, part)

    def sent(self):
        for step in range(self.at.chain - 1):
            for part in range(PARTS):
                for way in (0, 1):

                    @pl.when(self.sends(way, step))
                    def _():
                        self.copy(way, 0, step, part).wait_send()


def layer_kernel(
    size,
    tokens,
    cot,
    gain_one,
    gain_two,
    lens_in,
    w_query,
    w_key,
    w_value,
    w_out,
    w_gate,
    w_up,
    w_down,
    block_out,
    grad_tokens,
    grad_gains,
    g_query,
    g_key,
    g_value,
    g_out,
    g_gate,
    g_up,
    g_down,
    kept,
    slots,
    first,
    second,
    weights,
    qkv_weights,
    out_weights,
    grads,
    hidden,
    rows_two,
    turned,
    inner,
    units,
    sums_low,
    begun,
    qkv,
    attended,
    logs,
    table,
    head_sums,
    chain_stage,
    plane_stage,
    middle,
    total,
    last_stage,
    gain_rows,
    gains_in,
    lens,
    gain_parts,
    gain_peers,
    swap_sems,
    gather_send,
    gather_recv,
    reduce_send,
    reduce_recv,
    last_sems,
    plane_sems,
    first_sems,
    second_sems,
    small_sems,
    gain_sems,
    local_sems,
):
    chain, peers, rows, width, stages, unit, wide, seqs, tile = size
    at = Place(chain, peers)
    c, t, z = at.c, at.t, at.z
    group = rows * peers
    plane = 2 * group
    steps = chain - 1
    heads = wide // HEAD_DIM
    own_start = pl.multiple_of(c * group + t * rows, rows)
    query_tile = min(256, group)
    hub = min(256, unit)
    splits = PARTS if wide % (PARTS * LANES) == 0 else 1

    def slab_cols(s):
        return pl.ds(pl.multiple_of(s * 2 * unit, 2 * unit), 2 * unit)

    entry_barrier(at)

    def gain_copy(dp, source):
        place = gain_rows.at[:, pl.ds(pl.multiple_of(source * unit, unit), unit)]
        return remote(gains_in, place, gain_sems.at[0, dp], gain_sems.at[1, source], at.part(dp))

    own_gain = pltpu.make_async_copy(
        gains_in, gain_rows.at[:, pl.ds(pl.multiple_of(at.dp * unit, unit), unit)], local_sems.at[2]
    )

    def lens_copy(core):
        return remote(
            lens.at[core], lens.at[core], small_sems.at[0], small_sems.at[1], at.sibling()
        )

    lane = lax.broadcasted_iota(jnp.int32, (1, LANES), 1)
    gains_in[...] = jnp.zeros_like(gains_in)
    gains_in[0:1, :] = gain_one[...].astype(WIDE).reshape(1, unit)
    gains_in[1:2, :] = gain_two[...].astype(WIDE).reshape(1, unit)
    lens_row = jnp.zeros((8, LANES), WIDE)
    for s in range(seqs):
        lens_row = jnp.where(lane == s, lens_in[0, s].astype(WIDE), lens_row)
    lens[c] = lens_row

    def swap_copies(n):
        if n == 0:
            arrays = [(w, True, k * wide, wide, 0) for k, w in enumerate((w_query, w_key, w_value))]
            slab, down = qkv_weights.at[z], 0
        elif n == 1:
            arrays = [(w_out, False, 0, wide, 0)]
            slab, down = out_weights.at[z], 0
        else:
            arrays = [(w_gate, True, 0, unit, n - 2), (w_up, True, unit, unit, n - 2)]
            arrays.append((w_down, False, 0, unit, n - 2))
            slab, down = weights.at[n - 2, z], 2 * unit
        copies = []
        mine = pl.multiple_of(c * unit, unit)
        for k, (array, tall, offset, extent, stage) in enumerate(arrays):

            def half(core):
                count = (array.shape[1] if tall else array.shape[0]) // 2
                piece = pl.ds(pl.multiple_of(core * count + stage * extent, extent), extent)
                return array.at[:, piece] if tall else array.at[piece, :]

            if tall:
                place = slab.at[pl.ds(mine, unit), pl.ds(offset, extent)]
            else:
                place = slab.at[pl.ds(down, extent), pl.ds(mine, unit)]
            keep = pltpu.make_async_copy(half(c), place, swap_sems.at[0, n, k])
            give = remote(
                half(1 - c), place, swap_sems.at[1, n, k], swap_sems.at[2, n, k], at.sibling()
            )
            copies.append((keep, give))
        return copies

    def swapped(n):
        for keep, give in swap_copies(n):
            keep.wait()
            give.wait()

    for keep, give in swap_copies(0):
        keep.start()
        give.start()
    for dp in at.other_parts():
        gain_copy(dp, at.dp).start()
    own_gain.start()
    lens_copy(c).start()
    for n in range(1, stages + 2):
        for keep, give in swap_copies(n):
            keep.start()
            give.start()

    slabs = [qkv_weights, out_weights] + [weights.at[q] for q in range(stages)]
    stream = Stream(
        [
            ChainGather(at, ref, gather_send.at[n], gather_recv.at[n])
            for n, ref in enumerate(slabs)
        ],
        swapped,
    )
    gathers = [
        PlaneGather(at, full, rows, [plane_sems.at[n, k] for k in range(4)])
        for n, full in enumerate((hidden, rows_two, hidden, rows_two))
    ]
    plane_sums = [
        PlaneReduce(
            at,
            rows,
            tile,
            buffer,
            first.at[n],
            second.at[n],
            plane_stage,
            [first_sems.at[n, 0], first_sems.at[n, 1], second_sems.at[n, 0], second_sems.at[n, 1]],
            local_sems.at[4],
        )
        for n, buffer in enumerate((sums_low, sums_low, begun, sums_low))
    ]
    chain_sums = [
        ChainReduce(
            at,
            ref,
            height,
            slots.at[n],
            reduce_send.at[n],
            reduce_recv.at[n],
            chain_stage,
            local_sems,
        )
        for n, (ref, height) in enumerate(
            [(grads.at[q], 3 * unit) for q in range(stages)]
            + [(weights.at[0], 3 * wide), (weights.at[1], wide)]
        )
    ]
    sum_qkv, sum_out = chain_sums[stages], chain_sums[stages + 1]

    stream.go(2)

    for dp in at.other_parts():
        gain_copy(at.dp, dp).wait_recv()
    own_gain.wait()

    def strips(body):
        def each(i, carry):
            here = pl.ds(pl.multiple_of(i * STRIP, STRIP), STRIP)
            there = pl.ds(pl.multiple_of(own_start + i * STRIP, STRIP), STRIP)
            body(here, there)
            return carry

        lax.fori_loop(0, rows // STRIP, each, 0)

    def factor_of(values):
        return lax.rsqrt(jnp.mean(values * values, axis=-1, keepdims=True) + EPSILON)

    def first_norm(here, there):
        values = tokens[here, :].astype(WIDE)
        hidden[there, :] = (values * factor_of(values) * gain_rows[0:1, :]).astype(LOW)

    strips(first_norm)
    gathers[0].start()

    lens_copy(c).wait_send()
    lens_copy(1 - c).wait_recv()
    frequency = jnp.exp(lax.rem(lane, HALF).astype(WIDE) * (-2.0 * math.log(ROPE_BASE) / HEAD_DIM))
    side = jnp.where(lax.rem(lane, HEAD_DIM) < HALF, -1.0, 1.0)

    def table_rows(core):
        def body(i, carry):
            shape = (rows, LANES)
            row = (lax.broadcasted_iota(jnp.int32, shape, 0) + i * rows).astype(WIDE)
            start = jnp.zeros((1, 1), WIDE)
            base = jnp.zeros(shape, WIDE)
            valid = jnp.zeros(shape, WIDE)
            for s in range(seqs):
                length = lens[core, 0:1, s : s + 1]
                inside = (row >= start) & (row < start + length)
                base = jnp.where(inside, start, base)
                valid = jnp.where(inside, 1.0, valid)
                start = start + jnp.floor((length + (BLOCK - 1.0)) * (1.0 / BLOCK)) * BLOCK
            angle = (row - base) * frequency
            lowest = jnp.where(valid > 0.5, base, row)
            here = pl.ds(pl.multiple_of(core * group + i * rows, rows), rows)
            table[0, here, :] = jnp.cos(angle)
            table[1, here, :] = jnp.sin(angle) * side
            table[2, here, :] = jnp.where(lane == 0, lowest, valid)
            return carry

        lax.fori_loop(0, peers, body, 0)

    table_rows(0)
    table_rows(1)
    stream.go(2)

    def own_cotangent(here, there):
        rows_two[there, :] = (cot[here, :].astype(WIDE) * table[2, there, 1:2]).astype(LOW)

    strips(own_cotangent)
    gathers[0].forward()
    gathers[1].start()
    stream.go(1)
    gathers[0].finish()
    stream.complete(0)

    first_half = lax.rem(lax.broadcasted_iota(jnp.int32, (1, LANES), 1), HEAD_DIM) < HALF

    def swap_halves(values):
        return jnp.where(
            first_half, pltpu.roll(values, LANES - HALF, 1), pltpu.roll(values, HALF, 1)
        )

    def rotated(values, there, sign):
        pieces = []
        for n in range(0, values.shape[1], LANES):
            piece = values[:, n : n + LANES]
            pieces.append(
                piece * table[0, there, :] + sign * (swap_halves(piece) * table[1, there, :])
            )
        return jnp.concatenate(pieces, axis=1) if len(pieces) > 1 else pieces[0]

    def project(i, carry):
        here = pl.ds(pl.multiple_of(i * tile, tile), tile)
        sums = jnp.zeros((tile, 3 * wide), WIDE)
        for s in range(chain):
            sums += dot_nn(hidden[here, s * 2 * unit : (s + 1) * 2 * unit], qkv_weights[s])
        qkv[0, here, :] = rotated(sums[:, :wide], here, 1.0).astype(LOW)
        qkv[1, here, :] = rotated(sums[:, wide : 2 * wide], here, 1.0).astype(LOW)
        qkv[2, here, :] = sums[:, 2 * wide :].astype(LOW)
        return carry

    lax.fori_loop(0, plane // tile, project, 0)
    keep_rows = pltpu.make_async_copy(hidden, kept, local_sems.at[5])
    keep_rows.start()
    stream.go(2)
    gathers[1].forward()

    head_lane = lax.div(lax.broadcasted_iota(jnp.int32, (1, wide), 1), HEAD_DIM)

    def masked(scores, here, offset):
        column = lax.broadcasted_iota(jnp.int32, scores.shape, 1)
        row = lax.broadcasted_iota(jnp.int32, scores.shape, 0) + offset
        lowest = table[2, here, 0:1].astype(jnp.int32)
        return jnp.where((column >= lowest) & (column <= row), scores, MASKED)

    def attend(core, low, high):
        base = pl.multiple_of(core * group, group)

        def body(h, carry):
            lanes = jnp.where(head_lane == h, 1.0, 0.0)
            for b in range(group // query_tile):
                here = pl.ds(pl.multiple_of(base + b * query_tile, query_tile), query_tile)
                keys = pl.ds(base, (b + 1) * query_tile)
                query = (qkv[0, here, :].astype(WIDE) * (lanes * SCALE)).astype(LOW)
                scores = masked(dot_nt(query, qkv[1, keys, :]), here, b * query_tile)
                peak = jnp.max(scores, axis=-1, keepdims=True)
                exponent = jnp.exp(scores - peak)
                sums = jnp.sum(exponent, axis=-1, keepdims=True)
                weight = (exponent / sums).astype(LOW)
                mixed = dot_nn(weight, qkv[2, keys, :]) * lanes
                place = slice(b * query_tile, (b + 1) * query_tile)
                earlier = jnp.where(h == 0, 0.0, head_sums[0, place, :])
                head_sums[0, place, :] = earlier + mixed
                logs[here, :] = jnp.where(lane == h, peak + jnp.log(sums), logs[here, :])
            return carry

        if low == 0:
            logs[pl.ds(base, group), :] = jnp.zeros((group, LANES), WIDE)
            head_sums[0] = jnp.zeros((group, wide), WIDE)
        lax.fori_loop(low, high, body, 0)
        if high == heads:
            attended[pl.ds(base, group), :] = head_sums[0].astype(LOW)

    middle_head = heads // 2
    attend(1 - c, 0, middle_head)
    stream.go(2)
    attend(1 - c, middle_head, heads)
    keep_rows.wait()
    stream.complete(1)

    def product_tile(terms):
        def compute(source, out, extras):
            def body(s, carry):
                cols = slab_cols(s)
                sums = terms(source, s)
                for extra in extras:
                    sums += extra[:, cols].astype(WIDE)
                out[:, cols] = sums.astype(LOW)
                return carry

            lax.fori_loop(0, chain, body, 0)

        return compute

    out_tile = product_tile(lambda source, s: dot_nn(attended[source, :], out_weights[s]))
    plane_sums[0].half(out_tile)
    attend(c, 0, heads)
    stream.go(1)
    plane_sums[0].rest(out_tile)
    gathers[1].finish()
    stream.go(3)
    plane_sums[0].finish(total)

    def second_norm(here, there):
        values = tokens[here, :].astype(WIDE) + total[here, :] * table[2, there, 1:2]
        middle[here, :] = values
        hidden[there, :] = (values * factor_of(values) * gain_rows[1:2, :]).astype(LOW)

    strips(second_norm)
    gathers[2].start()
    stream.go(2)
    gathers[2].forward()
    plane_sums[0].sent()
    stream.go(1)
    gathers[2].finish()

    def hidden_units(q):
        def body(i, carry):
            these = pl.ds(pl.multiple_of(i * tile, tile), tile)
            gate_up = jnp.zeros((tile, 2 * unit), WIDE)
            grad_inner = jnp.zeros((tile, unit), WIDE)
            for s in range(chain):
                cols = slice(s * 2 * unit, (s + 1) * 2 * unit)
                gate_up += dot_nn(hidden[these, cols], weights[q, s, 0 : 2 * unit, :])
                grad_inner += dot_nt(rows_two[these, cols], weights[q, s, 2 * unit :, :])
            gate, up = gate_up[:, :unit], gate_up[:, unit:]
            sigmoid_gate = jax.nn.sigmoid(gate)
            inner[q, these, :] = (gate * sigmoid_gate * up).astype(LOW)
            units[q, these, 0:unit] = (
                grad_inner * up * sigmoid_gate * (1.0 + gate * (1.0 - sigmoid_gate))
            ).astype(LOW)
            units[q, these, unit : 2 * unit] = (grad_inner * gate * sigmoid_gate).astype(LOW)
            return carry

        lax.fori_loop(0, plane // tile, body, 0)

    eye = identity(hub)

    def turn_into(start, source):
        extent = min(hub, source.shape[1])

        def body(i, carry):
            cols = pl.ds(pl.multiple_of(i * extent, extent), extent)
            place = pl.ds(pl.multiple_of(start + i * extent, extent), extent)
            turned[place, :] = dot_nt(eye[:extent, :extent], source[:, cols]).astype(LOW)
            return carry

        lax.fori_loop(0, source.shape[1] // extent, body, 0)

    def in_grads(q):
        turn_into(0, units.at[q])

        def body(s, carry):
            grads[q, s, 0 : 2 * unit, :] = dot_nn(
                turned[0 : 2 * unit, :], hidden[:, slab_cols(s)]
            ).astype(LOW)
            return carry

        lax.fori_loop(0, chain, body, 0)

    def down_grads(q):
        turn_into(2 * unit, inner.at[q])

        def body(s, carry):
            grads[q, s, 2 * unit :, :] = dot_nn(
                turned[2 * unit :, :], rows_two[:, slab_cols(s)]
            ).astype(LOW)
            return carry

        lax.fori_loop(0, chain, body, 0)

    def hidden_sums(stage_list):
        return product_tile(
            lambda source, s: sum(
                dot_nt(units[q, source, :], weights[q, s, 0 : 2 * unit, :]) for q in stage_list
            )
        )

    def begin_hidden():
        begin = hidden_sums(range(stages - 1))
        for i in range(group // tile):
            here = pl.ds(i * tile, tile)
            begin(plane_sums[1].source(1 - c, i), sums_low.at[here], [])
            begin(plane_sums[1].source(c, i), begun.at[here], [])

    for q in range(stages):
        stream.complete(q + 2)
        hidden_units(q)
        if q == stages - 1:
            break
        stream.go(1)
        turn_into(0, units.at[q])
        turn_into(2 * unit, inner.at[q])
        for k in range(chain):
            s = jnp.where(z < (chain + 1) // 2, chain - 1 - k, k)
            cols = slab_cols(s)
            low = dot_nn(turned[0 : 2 * unit, :], hidden[:, cols])
            grads[q, s, 0 : 2 * unit, :] = low.astype(LOW)
            low = dot_nn(turned[2 * unit :, :], rows_two[:, cols])
            grads[q, s, 2 * unit :, :] = low.astype(LOW)
            if k == 0:
                for part in range(PARTS):
                    chain_sums[q].ends(0, part)
        stream.go(1)
        for k in range(1, steps):
            for part in range(PARTS):
                stream.go(1)
                chain_sums[q].ends(k, part)
                if k > 1:
                    chain_sums[q].step(k - 1, part)
                if q == stages - 2 and (k, part) == (1, 0):
                    begin_hidden()
        if q == stages - 2 and steps == 1:
            begin_hidden()

    branch_tile = product_tile(
        lambda source, s: sum(
            dot_nn(inner[q, source, :], weights[q, s, 2 * unit :, :]) for q in range(stages)
        )
    )

    def chain_steps(n, low, high):
        for k in range(max(low, 1), high):
            for part in range(PARTS):
                chain_sums[n].step(k, part)

    def last_step(n):
        chain_steps(n, steps - 1, steps)

    def placed(n, core, source):
        own = chain_sums[n].slabs.at[z]
        cols = pl.ds(pl.multiple_of(core * unit, unit), unit)
        stage = last_stage.at[n % 2, core]
        if n < stages:
            place = pl.ds(pl.multiple_of((source * stages + n) * unit, unit), unit)
            return [
                (stage.at[0, :, pl.ds(0, unit)], g_gate.at[:, place]),
                (stage.at[1, :, pl.ds(0, unit)], g_up.at[:, place]),
                (own.at[pl.ds(2 * unit, unit), cols], g_down.at[place, :]),
            ]
        place = pl.ds(pl.multiple_of(source * wide, wide), wide)
        if n == stages:
            return [
                (stage.at[k, :, pl.ds(0, wide)], out.at[:, place])
                for k, out in enumerate((g_query, g_key, g_value))
            ]
        return [(own.at[pl.ds(0, wide), cols], g_out.at[place, :])]

    def last_copies(n):
        copies = []
        for k, ((mine, place), (theirs, _)) in enumerate(
            zip(placed(n, c, c), placed(n, 1 - c, c))
        ):
            keep = pltpu.make_async_copy(mine, place, last_sems.at[0, n, k])
            give = remote(theirs, place, last_sems.at[1, n, k], last_sems.at[2, n, k], at.sibling())
            copies.append((keep, give))
        return copies

    def finish_sum(n):
        chain_sums[n].finish()
        own = chain_sums[n].slabs
        pieces = []
        if n < stages:
            pieces = [(k, k * unit, 0, unit) for k in range(2)]
        elif n == stages:
            lanes = wide // splits
            pieces = [
                (k, (m * 3 + k) * lanes, m * lanes, lanes) for m in range(splits) for k in range(3)
            ]
        for core in (0, 1):
            for k, start, place, extent in pieces:
                piece = own[z, start : start + extent, core * unit : (core + 1) * unit]
                last_stage[n % 2, core, k, :, place : place + extent] = turn(piece, eye)
        for keep, give in last_copies(n):
            keep.start()
            give.start()

    def settle(n):
        for keep, give in last_copies(n):
            keep.wait()
            give.wait()
        chain_sums[n].sent()

    down_grads(stages - 1)
    last_tile = hidden_sums([stages - 1])
    plane_sums[1].half(last_tile, begun=True)
    plane_sums[1].rest(last_tile, begun=begun)
    early = list(range(stages - 1))
    for q in early[-1:] + early[:-1]:
        last_step(q)
    in_grads(stages - 1)
    for k in range(steps):
        for part in range(PARTS):
            chain_sums[stages - 1].ends(k, part)
    plane_sums[2].half(branch_tile)
    bring_rows = pltpu.make_async_copy(kept, hidden, local_sems.at[5])
    bring_rows.start()
    plane_sums[1].finish(total)

    def second_back(here, there):
        values = middle[here, :]
        factor = factor_of(values)
        normed = values * factor
        grad = total[here, :]
        gain_parts[1:2, :] += jnp.sum(grad * normed, axis=0, keepdims=True)
        scaled = grad * gain_rows[1:2, :]
        mean = jnp.mean(scaled * normed, axis=-1, keepdims=True)
        result = cot[here, :].astype(WIDE) + factor * (scaled - normed * mean)
        grad_tokens[here, :] = result
        rows_two[there, :] = (result * table[2, there, 1:2]).astype(LOW)

    gain_parts[...] = jnp.zeros_like(gain_parts)
    strips(second_back)
    gathers[3].start()
    plane_sums[1].sent()
    for chain_gather in stream.chains:
        chain_gather.sent()
    plane_sums[2].rest(branch_tile)
    finish_sum(0)
    chain_steps(stages - 1, 1, steps - 1)
    if stages > 3:
        settle(0)
        finish_sum(2)
    if stages > 2:
        finish_sum(1)
    gathers[3].forward()
    gathers[3].finish()

    def finish_branch():
        plane_sums[2].finish(total)

        def last_rows(here, there):
            result = middle[here, :] + total[here, :] * table[2, there, 1:2]
            block_out[here, :] = result.astype(LOW)

        strips(last_rows)

    grad_attended = inner.at[0]

    def attended_grad(i, carry):
        here = pl.ds(pl.multiple_of(i * tile, tile), tile)
        sums = jnp.zeros((tile, wide), WIDE)
        for s in range(chain):
            sums += dot_nt(rows_two[here, s * 2 * unit : (s + 1) * 2 * unit], out_weights[s])
        grad_attended[here, :] = sums.astype(LOW)
        return carry

    turn_into(0, attended)

    def out_grads(s, carry):
        weights[1, s, 0:wide, :] = dot_nn(turned[0:wide, :], rows_two[:, slab_cols(s)]).astype(LOW)
        return carry

    lax.fori_loop(0, chain, out_grads, 0)
    for k in range(steps):
        for part in range(PARTS):
            sum_out.ends(k, part)
    lax.fori_loop(0, plane // tile, attended_grad, 0)

    def attend_back(core, low, high):
        base = core * group

        def body(h, carry):
            lanes = jnp.where(head_lane == h, 1.0, 0.0)
            lanes_low = lanes.astype(LOW)
            for b in range(group // query_tile):
                here = slice(base + b * query_tile, base + (b + 1) * query_tile)
                keys = slice(base, base + (b + 1) * query_tile)
                place = slice(b * query_tile, (b + 1) * query_tile)
                reach = slice(0, (b + 1) * query_tile)
                query = qkv[0, here, :] * lanes_low
                grad = grad_attended[here, :] * lanes_low
                scores = masked(dot_nt(query, qkv[1, keys, :]) * SCALE, here, b * query_tile)
                log_total = jnp.sum(
                    jnp.where(lane == h, logs[here, :], 0.0), axis=-1, keepdims=True
                )
                probs = jnp.exp(scores - log_total)
                grad_probs = dot_nt(grad, qkv[2, keys, :])
                shift = jnp.sum(probs * grad_probs, axis=-1, keepdims=True)
                grad_scores = (probs * (grad_probs - shift) * SCALE).astype(LOW)
                head_sums[0, place, :] += dot_nn(grad_scores, qkv[1, keys, :]) * lanes
                head_sums[1, reach, :] += dot_nn(turn(grad_scores, eye), query)
                head_sums[2, reach, :] += dot_nn(turn(probs.astype(LOW), eye), grad)
            return carry

        for k in range(3):
            head_sums[k] = jnp.zeros((group, wide), WIDE)
        lax.fori_loop(low, high, body, 0)
        lanes = slice(low * HEAD_DIM, high * HEAD_DIM)

        def back(i, carry):
            there = pl.ds(pl.multiple_of(base + i * query_tile, query_tile), query_tile)
            here = pl.ds(pl.multiple_of(i * query_tile, query_tile), query_tile)
            for k in range(2):
                values = rotated(head_sums[k, here, lanes], there, -1.0)
                units[0, there, k * wide + lanes.start : k * wide + lanes.stop] = values.astype(LOW)
            units[1, there, lanes] = head_sums[2, here, lanes].astype(LOW)
            return carry

        lax.fori_loop(0, group // query_tile, back, 0)

    def qkv_grads(n):
        lanes = wide // splits
        turn_into(0, units.at[0, :, pl.ds(n * lanes, lanes)])
        turn_into(lanes, units.at[0, :, pl.ds(wide + n * lanes, lanes)])
        turn_into(2 * lanes, units.at[1, :, pl.ds(n * lanes, lanes)])

        parts = range(n * PARTS // splits, (n + 1) * PARTS // splits)
        for k in range(chain):
            s = jnp.where(at.z < (chain + 1) // 2, chain - 1 - k, k)
            weights[0, s, n * 3 * lanes : (n + 1) * 3 * lanes, :] = dot_nn(
                turned[0 : 3 * lanes, :], hidden[:, slab_cols(s)]
            ).astype(LOW)
            if k < steps:
                for part in parts:
                    sum_qkv.ends(k, part)

    for n in range(splits):
        low, high = n * heads // splits, (n + 1) * heads // splits
        attend_back(0, low, high)
        if n == 0:
            last_step(stages - 1)
        attend_back(1, low, high)
        if n == 0:
            bring_rows.wait()
        qkv_grads(n)

    first_tile = product_tile(
        lambda source, s: dot_nt(units[0, source, :], qkv_weights[s, :, 0 : 2 * wide])
        + dot_nt(units[1, source, 0:wide], qkv_weights[s, :, 2 * wide :])
    )
    chain_steps(stages + 1, 1, steps - 1)
    plane_sums[3].half(first_tile)
    plane_sums[3].rest(first_tile)

    def qkv_steps(part, low, high):
        for k in range(max(low, 1), high):
            sum_qkv.step(k, part)

    qkv_steps(0, 1, steps - 1)
    if stages > 2:
        settle(stages - 3)
    finish_sum(stages - 1)
    last_step(stages + 1)
    qkv_steps(0, steps - 1, steps)
    finish_branch()
    for part in range(1, PARTS):
        qkv_steps(part, 1, steps - 1)
    finish_sum(stages + 1)
    for part in range(1, PARTS):
        qkv_steps(part, steps - 1, steps)
    plane_sums[3].finish(total)

    def first_back(here, there):
        values = tokens[here, :].astype(WIDE)
        factor = factor_of(values)
        normed = values * factor
        grad = total[here, :]
        gain_parts[0:1, :] += jnp.sum(grad * normed, axis=0, keepdims=True)
        scaled = grad * gain_rows[0:1, :]
        mean = jnp.mean(scaled * normed, axis=-1, keepdims=True)
        grad_tokens[here, :] += factor * (scaled - normed * mean)

    strips(first_back)

    own_cols = pl.ds(pl.multiple_of(at.dp * unit, unit), unit)

    def gain_sum_copy(dp, source):
        cols = pl.ds(pl.multiple_of(dp * unit, unit), unit)
        return remote(
            gain_parts.at[:, cols],
            gain_peers.at[source],
            gain_sems.at[2, dp],
            gain_sems.at[3, source],
            at.part(dp),
        )

    def gain_peer_copy(peer, source):
        parts = 2 * chain
        return remote(
            gain_peers.at[parts + t],
            gain_peers.at[parts + source],
            gain_sems.at[4, peer],
            gain_sems.at[5, source],
            at.peer(peer),
        )

    for dp in at.other_parts():
        gain_sum_copy(dp, at.dp).start()
    settle(stages - 2)
    sums = gain_parts[:, own_cols]
    for dp in at.other_parts():
        gain_sum_copy(at.dp, dp).wait_recv()
        sums += gain_peers[dp]
    gain_peers[2 * chain + t] = sums
    for peer in at.other_peers():
        gain_peer_copy(peer, t).start()
    for peer in at.other_peers():
        gain_peer_copy(t, peer).wait_recv()
        sums += gain_peers[2 * chain + peer]
    grad_gains[...] = sums
    settle(stages - 1)
    finish_sum(stages)
    settle(stages)
    settle(stages + 1)
    plane_sums[2].sent()
    plane_sums[3].sent()
    for dp in at.other_parts():
        gain_copy(dp, at.dp).wait_send()
        gain_sum_copy(dp, at.dp).wait_send()
    for peer in at.other_peers():
        gain_peer_copy(peer, t).wait_send()


def finish_kernel(*refs):
    count = len(refs) // 2
    sources, outs = refs[:count], refs[count:]
    for source, out in zip(sources[:2] + sources[3:], outs[: count - 1]):
        out[...] = source[...].astype(out.dtype)
    outs[count - 1][...] = sources[2][0:1, :]
    outs[count][...] = sources[2][1:2, :]


def finish(arrays):
    steps = 8
    gains = arrays[2]

    def split(array):
        return pl.BlockSpec((array.shape[0] // steps, array.shape[1]), lambda i: (i, 0))

    whole = pl.BlockSpec(gains.shape, lambda i: (0, 0))
    row = pl.BlockSpec((1, gains.shape[1]), lambda i: (0, 0))
    kept = arrays[:2] + arrays[3:]
    dtypes = [array.dtype for array in arrays[:2]] + [WIDE] * len(arrays[3:])
    return pl.pallas_call(
        finish_kernel,
        grid=(steps,),
        out_shape=[jax.ShapeDtypeStruct(a.shape, d) for a, d in zip(kept, dtypes)]
        + [jax.ShapeDtypeStruct((1, gains.shape[1]), WIDE)] * 2,
        in_specs=[split(a) for a in arrays[:2]] + [whole] + [split(a) for a in arrays[3:]],
        out_specs=[split(a) for a in kept] + [row] * 2,
        compiler_params=pltpu.CompilerParams(vmem_limit_bytes=VMEM_BYTES),
        name="finish",
    )(*arrays)


def on_device(
    tokens_in,
    seq_lens,
    w_query,
    w_key,
    w_value,
    w_out,
    norm1_gain,
    w_gate,
    w_up,
    w_down,
    norm2_gain,
    out_cotangent,
):
    n_dp, peers = lax.axis_size("dp"), lax.axis_size("tensor")
    chain = n_dp // 2
    rows, width = tokens_in.shape
    unit = width // n_dp
    wide = w_query.shape[1] // 2
    stages = w_gate.shape[1] // 2 // unit
    seqs = seq_lens.shape[1]
    group = rows * peers
    plane = 2 * group
    tile = min(256, group)
    slab = (3 * unit, 2 * unit)
    size = (chain, peers, rows, width, stages, unit, wide, seqs, tile)
    hbm = pl.BlockSpec(memory_space=pl.ANY)
    vmem = pl.BlockSpec(memory_space=pltpu.VMEM)
    smem = pl.BlockSpec(memory_space=pltpu.SMEM)
    dma = pltpu.SemaphoreType.DMA

    def like(array):
        return jax.ShapeDtypeStruct(array.shape, LOW)

    outs = pl.pallas_call(
        functools.partial(layer_kernel, size),
        out_shape=(
            jax.ShapeDtypeStruct((rows, width), LOW),
            jax.ShapeDtypeStruct((rows, width), WIDE),
            jax.ShapeDtypeStruct((8, unit), WIDE),
            like(w_query),
            like(w_key),
            like(w_value),
            like(w_out),
            like(w_gate),
            like(w_up),
            like(w_down),
            jax.ShapeDtypeStruct((plane, width), LOW),
            jax.ShapeDtypeStruct((stages + 2, 2, chain - 1) + slab, LOW),
            jax.ShapeDtypeStruct((4, group, width), LOW),
            jax.ShapeDtypeStruct((4, peers, rows, width), LOW),
        ),
        in_specs=[vmem, vmem, vmem, vmem, smem] + [hbm] * 7,
        out_specs=(vmem, vmem, vmem) + (hbm,) * 11,
        scratch_shapes=[
            pltpu.VMEM((stages, chain) + slab, LOW),
            pltpu.VMEM((chain, 2 * unit, 3 * wide), LOW),
            pltpu.VMEM((chain, wide, 2 * unit), LOW),
            pltpu.VMEM((stages, chain) + slab, LOW),
            pltpu.VMEM((plane, width), LOW),
            pltpu.VMEM((plane, width), LOW),
            pltpu.VMEM((3 * unit, plane), LOW),
            pltpu.VMEM((stages, plane, unit), LOW),
            pltpu.VMEM((stages, plane, 2 * unit), LOW),
            pltpu.VMEM((group, width), LOW),
            pltpu.VMEM((group, width), LOW),
            pltpu.VMEM((3, plane, wide), LOW),
            pltpu.VMEM((plane, wide), LOW),
            pltpu.VMEM((plane, LANES), WIDE),
            pltpu.VMEM((3, plane, LANES), WIDE),
            pltpu.VMEM((3, group, wide), WIDE),
            pltpu.VMEM((2, slab[0] // PARTS, slab[1]), LOW),
            pltpu.VMEM((tile, width), LOW),
            pltpu.VMEM((rows, width), WIDE),
            pltpu.VMEM((rows, width), WIDE),
            pltpu.VMEM((2, 2, 3, unit, max(unit, wide)), LOW),
            pltpu.VMEM((8, width), WIDE),
            pltpu.VMEM((8, unit), WIDE),
            pltpu.VMEM((2, 8, LANES), WIDE),
            pltpu.VMEM((8, width), WIDE),
            pltpu.VMEM((n_dp + peers, 8, unit), WIDE),
            dma((3, stages + 2, 3)),
            dma((stages + 2, 2, chain - 1, PARTS)),
            dma((stages + 2, 2, chain - 1, PARTS)),
            dma((stages + 2, 2, chain - 1, PARTS)),
            dma((stages + 2, 2, chain - 1, PARTS)),
            dma((3, stages + 2, 3)),
            dma((4, 4, peers)),
            dma((4, 2, group // tile)),
            dma((4, 2, peers)),
            dma((2,)),
            dma((6, n_dp)),
            dma((6,)),
        ],
        compiler_params=pltpu.CompilerParams(
            collective_id=0, has_side_effects=True, vmem_limit_bytes=VMEM_BYTES
        ),
        cost_estimate=pl.CostEstimate(
            flops=6 * plane * width * (4 * wide + 3 * unit * stages),
            bytes_accessed=16 * width * (4 * wide + 3 * unit * stages),
            transcendentals=0,
        ),
        name="layer",
    )(
        tokens_in,
        out_cotangent,
        norm1_gain,
        norm2_gain,
        seq_lens,
        w_query,
        w_key,
        w_value,
        w_out,
        w_gate,
        w_up,
        w_down,
    )
    block_out, grad_tokens, *weight_grads, gain_one, gain_two = finish(outs[:10])
    return (
        block_out,
        grad_tokens,
        *weight_grads[:4],
        gain_one.reshape(unit),
        *weight_grads[4:],
        gain_two.reshape(unit),
    )


def solution(mesh):
    return jax.shard_map(
        on_device,
        mesh=mesh,
        in_specs=(
            P(("dp", "tensor"), None),
            P("dp", None),
            P("dp", "tensor"),
            P("dp", "tensor"),
            P("dp", "tensor"),
            P("tensor", "dp"),
            P("dp"),
            P("dp", "tensor"),
            P("dp", "tensor"),
            P("tensor", "dp"),
            P("dp"),
            P(("dp", "tensor"), None),
        ),
        out_specs=(
            P(("dp", "tensor"), None),
            P(("dp", "tensor"), None),
            P("dp", "tensor"),
            P("dp", "tensor"),
            P("dp", "tensor"),
            P("tensor", "dp"),
            P("dp"),
            P("dp", "tensor"),
            P("dp", "tensor"),
            P("tensor", "dp"),
            P("dp"),
        ),
        check_vma=False,
    )
```
